32 devices in a mesh: ax: 8 (over z, x), az: 4 (over y, core).
Axes of the slice: x: 2, y: 2, z: 4, core: 2. Of those that a mesh axis runs over, the one named last changes fastest.
Arguments:
- conserved: float32 [5, 64, 1024, 128], P(None, 'ax', 'az'), may hold values from -0.6 to 3, as said below
- panel_cells: int32 [16384], P(('ax', 'az')), may hold values from 0 to 262143
- panel_counts: int32 [32], P(('ax', 'az')), may hold values from 1 to 512, 8192 in all
- time_bins: int32 [16384, 64], P(('ax', 'az')), may hold values from 0 to 1023
- amplitudes: float32 [16384, 64], P(('ax', 'az')), may hold values from 0.5 to 2
Outputs:
- section: float32 [5, 64, 1024, 128], P(None, 'ax', 'az')
- signal: float32 [64, 1024], P(None, ('ax', 'az'))
The draws below stay inside these ranges and needn't reach their ends.
Inputs may be any that keep to these rules, and one draw needn't show every extreme that they name: `conserved`: component 0 lies in 0.7 to 1.3, components 1 to 3 in -0.6 to 0.6, component 4 in 2.0 to 3.0. `panel_counts`: some device has exactly 512 live panel slots, each device at least one.
All inputs are finite; a program needn't handle non-finite values.
Results may differ from the reference program's by a relative error of at most 0.000076.
Values sent between devices are 32-bit elements; how exact they have to be, the bound alone decides.
No kernel may reach another device: no remote copies, remote signals or barrier semaphores. Data moves between devices by JAX's collectives and lax.ppermute only.
A program may use at most 128 MiB of HBM per device.

```python
import math
import jax
import jax.numpy as jnp
import numpy as np
from jax import lax

PLANES_DEV = 8
RADIAL = 128
AZIMUTH = 1024
CYCLES = 8
OBSERVERS = 64
BINS = 1024
PAN_DEV = 512
PLANES = 64
CELLS_DEV = 262144
PANELS = 16384
N_AZ = 4
DEVICES = 32


def draw_conserved(key, part):
    shape = (PLANES, AZIMUTH, RADIAL)
    key_density = jax.random.fold_in(key, 11)
    key_moment = jax.random.fold_in(key, 12)
    key_energy = jax.random.fold_in(key, 13)
    fluid_rho_value = jax.random.uniform(key_density, shape, jnp.float32, 0.8, 1.2)
    moment = jax.random.uniform(key_moment, (3,) + shape, jnp.float32, -0.6, 0.6)
    overall_heat_work = jax.random.uniform(key_energy, shape, jnp.float32, 2.2, 2.8)
    return jnp.concatenate([fluid_rho_value[None], moment, overall_heat_work[None]], axis=0)


def plant(array, key, low, largest):
    index_at = [jax.random.randint(jax.random.fold_in(key, axis), (), 0, length) for axis, length in enumerate(array.shape)]
    main_axis = array.shape.index(max(array.shape))
    beside = index_at[:main_axis] + [(index_at[main_axis] + 1) % array.shape[main_axis]] + index_at[main_axis + 1:]
    return array.at[tuple(index_at)].set(low).at[tuple(beside)].set(largest)


def shard_levels(rng, shape, pieces, smallest, high):
    def one(dim, blocks):
        heights = jax.random.uniform(jax.random.fold_in(jax.random.fold_in(rng, 6), dim), (blocks,), jnp.float32, smallest / len(pieces), high / len(pieces))
        return jnp.repeat(jnp.exp(heights), shape[dim] // blocks).reshape((-1,) + (1,) * (len(shape) - dim - 1))

    gain = one(*pieces[0])
    for cut in pieces[1:]:
        gain = gain * one(*cut)
    return gain


def profile(count, total, limit, skew):
    weights = [(1 << 20) // math.isqrt(standing ** skew) + 1 for standing in range(2, count + 1)]
    rest, holding = total - limit - (count - 1), [1] * (count - 1)
    while rest > 0:
        movable = [i for i in range(count - 1) if holding[i] < limit]
        whole, left = sum([weights[i] for i in movable]), rest
        for i in movable:
            addition = min(limit - holding[i], max(1, left * weights[i] // whole), rest)
            holding[i] = holding[i] + addition
            rest = rest - addition
    return np.array([limit] + holding)


def ragged(stream_key, count, total, limit, lean):
    if count == 2:
        one = jax.random.randint(stream_key, (), max(1, total - limit), min(limit, total - 1) + 1)
        return jnp.stack([one, total - one])
    lengths = jnp.asarray(profile(count, total, limit, lean), jnp.int32)
    pairs = (count - 1) // 2
    donor, sink = lengths[1:1 + 2 * pairs:2], lengths[2:2 + 2 * pairs:2]
    slack = jnp.minimum(donor - 1, limit - sink)
    moved = jax.random.randint(jax.random.fold_in(stream_key, 1), (pairs,), 0, 1 << 20) % (slack + 1)
    lengths = lengths.at[1:1 + 2 * pairs:2].set(donor - moved).at[2:2 + 2 * pairs:2].set(sink + moved)
    return lengths[jax.random.permutation(jax.random.fold_in(stream_key, 2), count)]


def setup_inputs(seed: int = 0) -> dict:
    splits = jax.random.split(jax.random.key(seed), 6)
    return {
        "conserved": draw_conserved(jax.random.fold_in(splits[5], 71), 0),
        "panel_cells": plant(jax.random.randint(splits[1], (PANELS,), 0, CELLS_DEV), jax.random.fold_in(splits[1], 1), 0, CELLS_DEV - 1).astype(jnp.int32),
        "panel_counts": ragged(splits[2], DEVICES, PANELS // 2, PAN_DEV, 2).astype(jnp.int32),
        "time_bins": plant(jax.random.randint(splits[3], (PANELS, OBSERVERS), 0, BINS), jax.random.fold_in(splits[3], 1), 0, BINS - 1).astype(jnp.int32),
        "amplitudes": jnp.clip(jnp.exp(math.log(2.0) - 1.3862944 * jax.random.uniform(splits[4], (PANELS, OBSERVERS), jnp.float32) ** shard_levels(splits[4], (PANELS, OBSERVERS), ((0, 32),), -0.2, 0.2)), 0.5, 2.0),
    }


gas_factor = 0.4
time_step = 0.02
ref_pressure = 0.95


def primitives(conserved):
    fluid_rho_value = conserved[0]
    axial_vel = conserved[1] / fluid_rho_value
    radial_vel = conserved[2] / fluid_rho_value
    swirl_vel = conserved[3] / fluid_rho_value
    kinetic = 0.5 * (conserved[1] * axial_vel + conserved[2] * radial_vel + conserved[3] * swirl_vel)
    thermo_stress_level = gas_factor * (conserved[4] - kinetic)
    return jnp.stack([fluid_rho_value, axial_vel, radial_vel, swirl_vel, thermo_stress_level])


def flux_along(primitive, stream_heading):
    fluid_rho_value = primitive[0]
    thermo_stress_level = primitive[4]
    stream_speed = [primitive[1], primitive[2], primitive[3]]
    overall_heat_work = thermo_stress_level / gas_factor + 0.5 * fluid_rho_value * (stream_speed[0] * stream_speed[0] + stream_speed[1] * stream_speed[1] + stream_speed[2] * stream_speed[2])
    holder_buffer = stream_speed[stream_heading]
    divided_pieces = [fluid_rho_value * holder_buffer]
    for entry_number in range(3):
        forcing_contribution = fluid_rho_value * stream_speed[entry_number] * holder_buffer
        if entry_number == stream_heading:
            forcing_contribution = forcing_contribution + thermo_stress_level
        divided_pieces.append(forcing_contribution)
    divided_pieces.append((overall_heat_work + thermo_stress_level) * holder_buffer)
    return jnp.stack(divided_pieces)


def fourth_diff(padded, along_axis, length):
    near_diff = lax.slice_in_dim(padded, 3, length + 3, axis=along_axis) - lax.slice_in_dim(padded, 1, length + 1, axis=along_axis)
    far_diff = lax.slice_in_dim(padded, 4, length + 4, axis=along_axis) - lax.slice_in_dim(padded, 0, length, axis=along_axis)
    return (8.0 * near_diff - far_diff) / 12.0


def cycle_weights(length):
    modes = jnp.arange(length // 2 + 1).astype(jnp.float32)
    cutoff = 4.0 * (jnp.arange(CYCLES).astype(jnp.float32) + 1.0)
    return jnp.exp(-((modes[None, :] / cutoff[:, None]) ** 8))


def reference(conserved, panel_cells, panel_counts, time_bins, amplitudes):
    primitive = primitives(conserved)
    planes_all = conserved.shape[1]
    radial_all = conserved.shape[3]
    radius = jnp.arange(radial_all).astype(jnp.float32) + 0.5
    dtheta = 2.0 * math.pi / AZIMUTH
    axial_flux = flux_along(primitive, 0)
    radial_flux = flux_along(primitive, 1)
    swirl_flux = flux_along(primitive, 2)
    padded_x = jnp.pad(axial_flux, ((0, 0), (2, 2), (0, 0), (0, 0)))
    padded_t = jnp.pad(swirl_flux, ((0, 0), (0, 0), (2, 2), (0, 0)), mode="wrap")
    padded_r = jnp.pad(radial_flux * radius, ((0, 0), (0, 0), (0, 0), (2, 2)))
    tendency = -fourth_diff(padded_x, 1, planes_all)
    tendency = tendency - fourth_diff(padded_r, 3, radial_all) / radius
    tendency = tendency - fourth_diff(padded_t, 2, AZIMUTH) / (radius * dtheta)
    fluid_rho_value = primitive[0]
    radial_vel = primitive[2]
    swirl_vel = primitive[3]
    thermo_stress_level = primitive[4]
    zeros_field = jnp.zeros_like(fluid_rho_value)
    source = jnp.stack([zeros_field, zeros_field, (thermo_stress_level + fluid_rho_value * swirl_vel * swirl_vel) / radius, -fluid_rho_value * radial_vel * swirl_vel / radius, zeros_field])
    raw_section = conserved + time_step * (tendency + source)
    inner = raw_section[..., :CYCLES]
    spectrum = jnp.fft.rfft(inner, axis=2) * jnp.transpose(cycle_weights(AZIMUTH))[None, None, :, :]
    smooth = jnp.fft.irfft(spectrum, n=AZIMUTH, axis=2).astype(raw_section.dtype)
    section = jnp.concatenate([smooth, raw_section[..., CYCLES:]], axis=3)
    sector = AZIMUTH // N_AZ
    slots = jnp.arange(PANELS).astype(jnp.int32)
    device = slots // PAN_DEV
    ax_index = device // N_AZ
    az_index = device % N_AZ
    plane_local = panel_cells // (sector * radial_all)
    theta_local = (panel_cells // radial_all) % sector
    radial_index = panel_cells % radial_all
    flat = ((ax_index * PLANES_DEV + plane_local) * AZIMUTH + az_index * sector + theta_local) * radial_all + radial_index
    flat = flat.astype(jnp.int32)
    live = (slots % PAN_DEV) < panel_counts[device]
    sampled = jnp.where(live, thermo_stress_level.reshape(-1)[flat] - ref_pressure, 0.0)
    contrib = sampled[:, None] * amplitudes
    segment = (jnp.arange(OBSERVERS).astype(jnp.int32)[None, :] * BINS + time_bins).astype(jnp.int32)
    signal = jax.ops.segment_sum(contrib.reshape(-1), segment.reshape(-1), num_segments=OBSERVERS * BINS)
    return section, signal.reshape(OBSERVERS, BINS)
```

```python
import functools
import math

import jax
import jax.numpy as jnp
import numpy as np
from jax import lax
from jax.experimental import pallas as pl
from jax.experimental.pallas import tpu as pltpu
from jax.sharding import PartitionSpec as P

CYCLES = 8
BINS = 1024
LOW_BINS = 32
FIELDS = 5
MODES = 8 * CYCLES
COEFS = 2 * MODES
ROWS = 8

gas_factor = 0.4
time_step = 0.02
ref_pressure = 0.95
VMEM_BYTES = 48 * 1024 * 1024

HIGHEST = lax.Precision.HIGHEST


def params(**more):
    return pltpu.CompilerParams(vmem_limit_bytes=VMEM_BYTES, **more)


def cost(flops, touched):
    return pl.CostEstimate(flops=flops, bytes_accessed=touched, transcendentals=0)


def basis_table(length):
    phase = (np.arange(length)[:, None] * np.arange(MODES)[None, :] % length) * (
        2.0 * math.pi / length
    )
    return np.concatenate([np.cos(phase), np.sin(phase)], axis=1).astype(np.float32)


def mode_weights(length):
    modes = np.arange(MODES).astype(np.float64)
    cutoff = 4.0 * (np.arange(CYCLES) + 1.0)
    weight = np.exp(-((modes[None, :] / cutoff[:, None]) ** 8))
    weight = weight * np.where(modes == 0, 1.0, 2.0)[None, :] / length
    return np.tile(np.concatenate([weight, weight], axis=1), (FIELDS, 1)).astype(np.float32)


def primitives(q):
    inverse = 1.0 / q[0]
    u, v, w = q[1] * inverse, q[2] * inverse, q[3] * inverse
    p = gas_factor * (q[4] - 0.5 * (q[1] * u + q[2] * v + q[3] * w))
    return u, v, w, p


def carried(q, p, speed, heading):
    flux = [q[0] * speed, q[1] * speed, q[2] * speed, q[3] * speed, (q[4] + p) * speed]
    flux[heading] = flux[heading] + p
    return flux


def inner_lanes(fields, lane):
    packed = jnp.where(lane < CYCLES, fields[0], 0.0)
    for f in range(1, FIELDS):
        here = (lane >= CYCLES * f) & (lane < CYCLES * (f + 1))
        packed = jnp.where(here, pltpu.roll(fields[f], CYCLES * f, 1), packed)
    return packed


def edge_kernel(up, q_ref, send_ref, inner_ref):
    sector, radial = q_ref.shape[2:]
    tail = sector * CYCLES // radial
    groups = radial // CYCLES - 1
    main = sector - tail
    scale = time_step / 12.0
    lane = lax.broadcasted_iota(jnp.int32, (1, radial), 1)

    def terms(start, size):
        rows = pl.ds(start, size)
        flux = []
        for plane in range(2):
            q = [q_ref[f, plane, rows, :] for f in range(FIELDS)]
            u, _, _, p = primitives(q)
            flux.append(carried(q, p, u, 1))
        near, far = (flux[1], flux[0]) if up else (flux[0], flux[1])
        whole, part = [], []
        for f in range(FIELDS):
            wide = scale * (8.0 * near[f] - far[f])
            narrow = scale * near[f]
            whole.append(wide if up else -wide)
            part.append(-narrow if up else narrow)
        slots = (whole, part) if up else (part, whole)
        for s in range(2):
            inner_ref[s, rows, :] = inner_lanes(slots[s], lane)
        return slots

    last = terms(main, tail)

    for g in range(groups):
        slots = terms(g * tail, tail)
        shift = radial - CYCLES * (g + 1)
        for s in range(2):
            for f in range(FIELDS):
                moved = pltpu.roll(last[s][f], shift, 1)
                send_ref[f, s, pl.ds(g * tail, tail), :] = jnp.where(
                    lane < CYCLES, moved, slots[s][f]
                )


def edge_terms(conserved, up):
    fields, planes, sector, radial = conserved.shape
    main = sector - sector * CYCLES // radial
    at = planes // 2 - 1 if up else 0
    return pl.pallas_call(
        functools.partial(edge_kernel, up),
        grid=(1,),
        in_specs=[pl.BlockSpec((fields, 2, sector, radial), lambda i: (0, at, 0, 0))],
        out_specs=[
            pl.BlockSpec((fields, 2, main, radial), lambda i: (0, 0, 0, 0)),
            pl.BlockSpec((2, sector, radial), lambda i: (0, 0, 0)),
        ],
        out_shape=[
            jax.ShapeDtypeStruct((fields, 2, main, radial), jnp.float32),
            jax.ShapeDtypeStruct((2, sector, radial), jnp.float32),
        ],
        compiler_params=params(),
        cost_estimate=cost(100 * 2 * sector * radial, 4 * 4 * fields * sector * radial),
        name="edge_up" if up else "edge_down",
    )(conserved)


def small_kernel(low_ref, high_ref, up_ref, down_ref, basis_ref, *outs):
    spec_up, spec_down, first_ref, last_ref = outs
    inner = FIELDS * CYCLES
    for y_ref, s_ref in ((up_ref, spec_up), (down_ref, spec_down)):
        for s in range(2):
            full = lax.dot_general(
                y_ref[s], basis_ref[...], (((0,), (0,)), ((), ())),
                precision=HIGHEST, preferred_element_type=jnp.float32,
            )
            s_ref[s] = full[:inner]
    planes = low_ref.shape[1]
    for ref, out, start in ((low_ref, first_ref, 0), (high_ref, last_ref, ROWS - 2)):
        for k in range(planes):
            q = [ref[f, k] for f in range(FIELDS)]
            _, _, w, p = primitives(q)
            flux = carried(q, p, w, 3)
            for f in range(FIELDS):
                out[f, 2 * k : 2 * k + 2, :] = flux[f][start : start + 2]


def small_terms(conserved, inner_up, inner_down, basis):
    fields, planes, sector, radial = conserved.shape
    end = sector // ROWS - 1
    edge = (fields, planes, ROWS, radial)
    spec = jax.ShapeDtypeStruct((2, FIELDS * CYCLES, COEFS), jnp.float32)
    ring = jax.ShapeDtypeStruct((fields, 2 * planes, radial), jnp.float32)
    zero3 = lambda i: (0, 0, 0)
    whole = pl.BlockSpec((2, sector, radial), zero3)
    return pl.pallas_call(
        small_kernel,
        grid=(1,),
        in_specs=[
            pl.BlockSpec(edge, lambda i: (0, 0, 0, 0)),
            pl.BlockSpec(edge, lambda i: (0, 0, end, 0)),
            whole,
            whole,
            pl.BlockSpec((sector, COEFS), lambda i: (0, 0)),
        ],
        out_specs=[
            pl.BlockSpec(spec.shape, zero3),
            pl.BlockSpec(spec.shape, zero3),
            pl.BlockSpec(ring.shape, zero3),
            pl.BlockSpec(ring.shape, zero3),
        ],
        out_shape=[spec, spec, ring, ring],
        compiler_params=params(),
        cost_estimate=cost(6 * 8 * sector * radial * COEFS, 10 * sector * radial * 4),
        name="small_terms",
    )(conserved, conserved, inner_up, inner_down, basis)


def panel_kernel(cells_ref, count_ref, row_ref, q_ref, bins_ref, amp_ref, out_ref, held):
    slots = row_ref.shape[1]
    radial = q_ref.shape[2]
    observers = bins_ref.shape[0]
    count = count_ref[0]
    width = 8

    def fetch(i, _):
        for k in range(width):
            s = i * width + k
            at = cells_ref[s] // radial
            held[:, pl.ds(s, 1), :] = q_ref[:, pl.ds(at, 1), :]
        return 0

    lax.fori_loop(0, (count + width - 1) // width, fetch, 0)
    q = [held[f] for f in range(FIELDS)]
    p = gas_factor * (q[4] - 0.5 * (q[1] * q[1] + q[2] * q[2] + q[3] * q[3]) / q[0])
    turned = jnp.transpose(p)
    which = lax.broadcasted_iota(jnp.int32, (radial, slots), 0)
    here = which == (row_ref[...] & (radial - 1))
    sampled = jnp.sum(jnp.where(here, turned, 0.0), axis=0, keepdims=True) - ref_pressure
    slot = lax.broadcasted_iota(jnp.int32, (1, slots), 1)
    sampled = jnp.where(slot < count, sampled, 0.0)

    contrib = sampled * amp_ref[...]
    first = contrib.astype(jnp.bfloat16).astype(jnp.float32)
    second = contrib - first
    bins = bins_ref[...]
    low = bins & (LOW_BINS - 1)
    high = bins // LOW_BINS
    each = 128 // LOW_BINS
    high_count = BINS // LOW_BINS
    low_iota = lax.broadcasted_iota(jnp.int32, (LOW_BINS, slots), 0)
    high_iota = lax.broadcasted_iota(jnp.int32, (high_count, slots), 0)
    lane = lax.broadcasted_iota(jnp.int32, (high_count, 128), 1)
    for g in range(observers // each):
        left, right = [], []
        for k in range(each):
            o = g * each + k
            hit = high_iota == high[o : o + 1]
            left.append(jnp.where(hit, first[o : o + 1], 0.0).astype(jnp.bfloat16))
            left.append(jnp.where(hit, second[o : o + 1], 0.0).astype(jnp.bfloat16))
            same = low_iota == low[o : o + 1]
            right.append(jnp.where(same, 1.0, 0.0).astype(jnp.bfloat16))
        sums = lax.dot_general(
            jnp.concatenate(left, axis=0),
            jnp.concatenate(right, axis=0),
            (((1,), (1,)), ((), ())),
            preferred_element_type=jnp.float32,
        )
        total = jnp.zeros((high_count, 128), jnp.float32)
        for k in range(each):
            at = 2 * k * high_count
            both = sums[at : at + high_count] + sums[at + high_count : at + 2 * high_count]
            total = jnp.where(lane // LOW_BINS == k, both, total)
        out_ref[:, g * 128 : (g + 1) * 128] = total


def panel_sums(conserved, cells, counts, bins, amplitudes):
    fields, planes, sector, radial = conserved.shape
    slots, observers = bins.shape
    flat = conserved.reshape(fields, planes * sector, radial)
    high_count = BINS // LOW_BINS
    full = lambda *shape: pl.BlockSpec(shape, lambda i, *_: (0,) * len(shape))
    return pl.pallas_call(
        panel_kernel,
        grid_spec=pltpu.PrefetchScalarGridSpec(
            num_scalar_prefetch=2,
            grid=(1,),
            in_specs=[
                full(1, slots),
                full(fields, planes * sector, radial),
                full(observers, slots),
                full(observers, slots),
            ],
            out_specs=full(high_count, observers * LOW_BINS),
            scratch_shapes=[pltpu.VMEM((fields, slots, radial), jnp.float32)],
        ),
        out_shape=jax.ShapeDtypeStruct((high_count, observers * LOW_BINS), jnp.float32),
        compiler_params=params(),
        cost_estimate=cost(8 * observers * slots * BINS, 4 * fields * planes * sector * radial),
        name="panel_sums",
    )(cells, counts, cells.reshape(1, slots), flat, bins.T, amplitudes.T)


def section_kernel(dtheta, q_ref, before_ref, after_ref, basis_ref, out_ref, spec_ref, axial, swirl, local, inner):
    fields, _, sector, radial = q_ref.shape
    step = pl.program_id(0)
    planes = pl.num_programs(0) - 2
    scale = time_step / 12.0
    chunk = 2 * ROWS
    lane = lax.broadcasted_iota(jnp.int32, (1, radial), 1)
    radius = lane.astype(jnp.float32) + 0.5
    inverse = 1.0 / radius
    near = 8.0 * scale * inverse
    far = scale * inverse
    near_up = jnp.where(lane < radial - 1, near, 0.0)
    near_down = jnp.where(lane >= 1, near, 0.0)
    far_up = jnp.where(lane < radial - 2, far, 0.0)
    far_down = jnp.where(lane >= 2, far, 0.0)
    source = time_step * inverse

    @pl.when(step == 0)
    def _():
        axial[0:2] = jnp.zeros((2,) + axial.shape[1:], jnp.float32)
        axial[planes + 2 : planes + 4] = jnp.zeros((2,) + axial.shape[1:], jnp.float32)

    @pl.when(step < planes)
    def _():
        slot = lax.rem(step, 3)
        for f in range(FIELDS):
            swirl[slot, f, ROWS - 2 : ROWS, :] = before_ref[f, pl.ds(2 * step, 2), :]
            swirl[slot, f, ROWS + sector : ROWS + sector + 2, :] = after_ref[f, pl.ds(2 * step, 2), :]

        def body(i, _):
            start = pl.multiple_of(i * chunk, chunk)
            rows = pl.ds(start, chunk)
            q = [q_ref[f, 0, rows, :] for f in range(FIELDS)]
            u, v, w, p = primitives(q)
            along = carried(q, p, u, 1)
            around = carried(q, p, w, 3)
            outward = carried(q, p, v, 2)
            for f in range(FIELDS):
                axial[step + 2, f, rows, :] = along[f]
                swirl[slot, f, pl.ds(start + ROWS, chunk), :] = around[f]
                g = outward[f] * radius
                value = q[f] - near_up * pltpu.roll(g, radial - 1, 1)
                value = value + near_down * pltpu.roll(g, 1, 1)
                value = value + far_up * pltpu.roll(g, radial - 2, 1)
                value = value - far_down * pltpu.roll(g, 2, 1)
                if f == 2:
                    value = value + source * (p + q[3] * w)
                if f == 3:
                    value = value - source * (q[2] * w)
                local[slot, f, rows, :] = value
            return 0

        lax.fori_loop(0, sector // chunk, body, 0)

    @pl.when(step >= 2)
    def _():
        plane = step - 2
        slot = lax.rem(plane, 3)
        turn = scale * inverse / dtheta

        def body(i, _):
            start = pl.multiple_of(i * chunk, chunk)
            rows = pl.ds(start, chunk)
            result = []
            for f in range(FIELDS):
                at = lambda k: swirl[slot, f, pl.ds(start + (ROWS + k), chunk), :]
                of = lambda k: axial[plane + 2 + k, f, rows, :]
                around = 8.0 * (at(1) - at(-1)) - (at(2) - at(-2))
                along = 8.0 * (of(1) - of(-1)) - (of(2) - of(-2))
                value = local[slot, f, rows, :] - turn * around - scale * along
                out_ref[f, 0, rows, :] = value
                result.append(value)
            inner[rows, :] = inner_lanes(result, lane)
            return 0

        lax.fori_loop(0, sector // chunk, body, 0)
        full = lax.dot_general(
            inner[...], basis_ref[...], (((0,), (0,)), ((), ())),
            precision=HIGHEST, preferred_element_type=jnp.float32,
        )
        spec_ref[0] = full[: FIELDS * CYCLES]


def local_section(conserved, before, after, basis, length):
    fields, planes, sector, radial = conserved.shape
    padded = sector + 2 * ROWS
    late = lambda i: jnp.maximum(i - 2, 0)
    ring = pl.BlockSpec(before.shape, lambda i: (0, 0, 0))
    coefs = FIELDS * CYCLES
    return pl.pallas_call(
        functools.partial(section_kernel, 2.0 * math.pi / length),
        grid=(planes + 2,),
        in_specs=[
            pl.BlockSpec(
                (fields, 1, sector, radial), lambda i: (0, jnp.minimum(i, planes - 1), 0, 0)
            ),
            ring,
            ring,
            pl.BlockSpec((sector, COEFS), lambda i: (0, 0)),
        ],
        out_specs=[
            pl.BlockSpec((fields, 1, sector, radial), lambda i: (0, late(i), 0, 0)),
            pl.BlockSpec((1, coefs, COEFS), lambda i: (late(i), 0, 0)),
        ],
        out_shape=[
            jax.ShapeDtypeStruct(conserved.shape, jnp.float32),
            jax.ShapeDtypeStruct((planes, coefs, COEFS), jnp.float32),
        ],
        scratch_shapes=[
            pltpu.VMEM((planes + 4, fields, sector, radial), jnp.float32),
            pltpu.VMEM((3, fields, padded, radial), jnp.float32),
            pltpu.VMEM((3, fields, sector, radial), jnp.float32),
            pltpu.VMEM((sector, radial), jnp.float32),
        ],
        compiler_params=params(),
        cost_estimate=cost(
            600 * planes * sector * radial, 10 * 4 * fields * planes * sector * radial
        ),
        name="local_section",
    )(conserved, before, after, basis)


def smooth_kernel(raw_ref, spec_ref, weight_ref, basis_ref, out_ref, padded):
    radial = raw_ref.shape[3]
    coefs = spec_ref.shape[1]
    lane = lax.broadcasted_iota(jnp.int32, (1, radial), 1)

    @pl.when(pl.program_id(0) == 0)
    def _():
        padded[...] = jnp.zeros_like(padded)

    padded[:coefs] = spec_ref[0] * weight_ref[...]
    smooth = lax.dot_general(
        basis_ref[...], padded[...], (((1,), (1,)), ((), ())),
        precision=HIGHEST, preferred_element_type=jnp.float32,
    )
    for f in range(FIELDS):
        moved = smooth if f == 0 else pltpu.roll(smooth, radial - CYCLES * f, 1)
        out_ref[f, 0] = jnp.where(lane < CYCLES, moved, raw_ref[f, 0])


def smooth_section(raw, spec, weights, basis):
    fields, planes, sector, radial = raw.shape
    plane = pl.BlockSpec((fields, 1, sector, radial), lambda i: (0, i, 0, 0))
    return pl.pallas_call(
        smooth_kernel,
        grid=(planes,),
        in_specs=[
            plane,
            pl.BlockSpec((1,) + spec.shape[1:], lambda i: (i, 0, 0)),
            pl.BlockSpec(weights.shape, lambda i: (0, 0)),
            pl.BlockSpec(basis.shape, lambda i: (0, 0)),
        ],
        out_specs=plane,
        out_shape=jax.ShapeDtypeStruct(raw.shape, jnp.float32),
        scratch_shapes=[pltpu.VMEM((radial, COEFS), jnp.float32)],
        input_output_aliases={0: 0},
        compiler_params=params(),
        cost_estimate=cost(
            12 * planes * sector * radial * COEFS, 2 * 4 * fields * planes * sector * radial
        ),
        name="smooth_section",
    )(raw, spec, weights, basis)


def add_kernel(part_ref, low_ref, high_ref, out_ref):
    fields, _, sector, radial = part_ref.shape
    tail = sector * CYCLES // radial
    groups = radial // CYCLES - 1
    main = sector - tail
    lane = lax.broadcasted_iota(jnp.int32, (1, radial), 1)
    chosen = lane >= CYCLES

    def go(ref):
        for f in range(fields):
            out_ref[f, 0, :main, :] = part_ref[f, 0, :main, :] + jnp.where(
                chosen, ref[f, 0], 0.0
            )
            rest = jnp.zeros((tail, radial), jnp.float32)
            for g in range(groups):
                start = CYCLES * (g + 1)
                here = (lane >= start) & (lane < start + CYCLES)
                moved = pltpu.roll(ref[f, 0, g * tail : (g + 1) * tail, :], start, 1)
                rest = jnp.where(here, moved, rest)
            out_ref[f, 0, main:, :] = part_ref[f, 0, main:, :] + rest

    pl.when(pl.program_id(0) < 2)(lambda: go(low_ref))
    pl.when(pl.program_id(0) >= 2)(lambda: go(high_ref))


def add_edges(part, low, high):
    fields, planes, sector, radial = part.shape
    main = low.shape[2]
    plane = pl.BlockSpec(
        (fields, 1, sector, radial), lambda i: (0, jnp.where(i < 2, i, planes - 4 + i), 0, 0)
    )
    return pl.pallas_call(
        add_kernel,
        grid=(4,),
        in_specs=[
            plane,
            pl.BlockSpec((fields, 1, main, radial), lambda i: (0, jnp.minimum(i, 1), 0, 0)),
            pl.BlockSpec((fields, 1, main, radial), lambda i: (0, jnp.maximum(i - 2, 0), 0, 0)),
        ],
        out_specs=plane,
        out_shape=jax.ShapeDtypeStruct(part.shape, jnp.float32),
        input_output_aliases={0: 0},
        compiler_params=params(),
        cost_estimate=cost(8 * fields * sector * radial, 4 * 12 * fields * sector * radial),
        name="add_edges",
    )(part, low, high)


def shared_sums(partial, observers):
    n_ax, n_az = lax.axis_size("ax"), lax.axis_size("az")
    mine = BINS // (n_ax * n_az)
    if mine != LOW_BINS:
        partial = partial.reshape(-1, observers, LOW_BINS).transpose(0, 2, 1)
        partial = partial.reshape(n_ax * n_az, mine, observers).transpose(0, 2, 1)
    blocks = partial.reshape(n_ax, n_az, observers * mine)
    blocks = lax.all_to_all(blocks, "az", split_axis=1, concat_axis=1, tiled=True).sum(axis=1)
    return lax.all_to_all(blocks, "ax", split_axis=0, concat_axis=0, tiled=True).sum(axis=0).reshape(
        observers, mine
    )


def on_device(conserved, panel_cells, panel_counts, time_bins, amplitudes):
    fields, planes, sector, radial = conserved.shape
    n_ax, n_az = lax.axis_size("ax"), lax.axis_size("az")
    length = sector * n_az
    up = [(i, i + 1) for i in range(n_ax - 1)]
    down = [(j, i) for i, j in up]
    ahead = [(i, (i + 1) % n_az) for i in range(n_az)]
    back = [(j, i) for i, j in ahead]

    send_up, inner_up = edge_terms(conserved, True)
    low = lax.ppermute(send_up, "ax", up)
    send_down, inner_down = edge_terms(conserved, False)
    high = lax.ppermute(send_down, "ax", down)

    basis = lax.dynamic_slice_in_dim(
        jnp.asarray(basis_table(length)), lax.axis_index("az") * sector, sector, axis=0
    )
    spec_up, spec_down, first, last = small_terms(conserved, inner_up, inner_down, basis)
    before = lax.ppermute(last, "az", ahead)
    after = lax.ppermute(first, "az", back)
    spec_low = lax.ppermute(spec_up, "ax", up)
    spec_high = lax.ppermute(spec_down, "ax", down)

    partial = panel_sums(conserved, panel_cells, panel_counts, time_bins, amplitudes)
    signal = shared_sums(partial, time_bins.shape[1])

    raw, spec = local_section(conserved, before, after, basis, length)
    spec = jnp.concatenate(
        [spec[:2] + spec_low, spec[2 : planes - 2], spec[planes - 2 :] + spec_high], axis=0
    )
    bit = 1
    while bit < n_az:
        spec = spec + lax.ppermute(spec, "az", [(i, i ^ bit) for i in range(n_az)])
        bit *= 2
    part = smooth_section(raw, spec, jnp.asarray(mode_weights(length)), basis)
    section = add_edges(part, low, high)
    return (section, signal)


def solution(mesh):
    placed = (
        P(None, "ax", "az", None),
        P(("ax", "az")),
        P(("ax", "az")),
        P(("ax", "az"), None),
        P(("ax", "az"), None),
    )
    return jax.shard_map(
        on_device,
        mesh=mesh,
        in_specs=placed,
        out_specs=(P(None, "ax", "az", None), P(None, ("ax", "az"))),
        check_vma=False,
    )
```

```python
import functools
import math

import jax
import jax.numpy as jnp
import numpy as np
from jax import lax
from jax.experimental import pallas as pl
from jax.experimental.pallas import tpu as pltpu
from jax.sharding import PartitionSpec as P

CYCLES = 8
BINS = 1024
LOW_BINS = 32
FIELDS = 5
MODES = 8 * CYCLES
COEFS = 2 * MODES
ROWS = 8

gas_factor = 0.4
time_step = 0.02
ref_pressure = 0.95
VMEM_BYTES = 48 * 1024 * 1024

HIGHEST = lax.Precision.HIGHEST


def params(**more):
    return pltpu.CompilerParams(vmem_limit_bytes=VMEM_BYTES, **more)


def cost(flops, touched):
    return pl.CostEstimate(flops=flops, bytes_accessed=touched, transcendentals=0)


def basis_table(length):
    phase = (np.arange(length)[:, None] * np.arange(MODES)[None, :] % length) * (
        2.0 * math.pi / length
    )
    return np.concatenate([np.cos(phase), np.sin(phase)], axis=1).astype(np.float32)


def mode_weights(length):
    modes = np.arange(MODES).astype(np.float64)
    cutoff = 4.0 * (np.arange(CYCLES) + 1.0)
    weight = np.exp(-((modes[None, :] / cutoff[:, None]) ** 8))
    weight = weight * np.where(modes == 0, 1.0, 2.0)[None, :] / length
    return np.concatenate([weight, weight], axis=1).astype(np.float32)


def primitives(q):
    inverse = 1.0 / q[0]
    u, v, w = q[1] * inverse, q[2] * inverse, q[3] * inverse
    p = gas_factor * (q[4] - 0.5 * (q[1] * u + q[2] * v + q[3] * w))
    return u, v, w, p


def carried(q, p, speed, heading):
    flux = [q[0] * speed, q[1] * speed, q[2] * speed, q[3] * speed, (q[4] + p) * speed]
    flux[heading] = flux[heading] + p
    return flux


def swirl_rows(ref, low):
    for k in range(ref.shape[1]):
        q = [ref[f, k] for f in range(FIELDS)]
        _, _, w, p = primitives(q)
        flux = carried(q, p, w, 3)
        yield k, [jnp.where(low, f[:2], f[ROWS - 2 :]) for f in flux]


def edge_kernel(az_ref, q_ref, rim_ref, up_ref, down_ref, early_ref):
    sector, radial = q_ref.shape[2:]
    groups = radial // CYCLES - 1
    tail = sector * CYCLES // radial
    scale = time_step / 12.0
    lane = lax.broadcasted_iota(jnp.int32, (1, radial), 1)

    def go(up, send):
        def terms(start):
            rows = pl.ds(start, tail)
            flux = []
            for plane in range(2):
                q = [q_ref[f, plane, rows, :] for f in range(FIELDS)]
                u, _, _, p = primitives(q)
                flux.append(carried(q, p, u, 1))
            near, far = (flux[1], flux[0]) if up else (flux[0], flux[1])
            whole, part = [], []
            for f in range(FIELDS):
                wide = scale * (8.0 * near[f] - far[f])
                narrow = scale * near[f]
                whole.append(wide if up else -wide)
                part.append(-narrow if up else narrow)
            return (whole, part) if up else (part, whole)

        last = terms(groups * tail)
        for g in range(groups):
            slots = terms(g * tail)
            shift = radial - CYCLES * (g + 1)
            for s in range(2):
                for f in range(FIELDS):
                    moved = pltpu.roll(last[s][f], shift, 1)
                    send[f, s, pl.ds(g * tail, tail), :] = jnp.where(
                        lane < CYCLES, moved, slots[s][f]
                    )

    @pl.when(pl.program_id(0) == 0)
    def _():
        go(True, up_ref)
        for k, flux in swirl_rows(rim_ref, lax.rem(az_ref[0], 2) == 1):
            for f in range(FIELDS):
                early_ref[f, 2 * k : 2 * k + 2, :] = flux[f]

    pl.when(pl.program_id(0) == 1)(lambda: go(False, down_ref))


def edge_terms(conserved, az):
    fields, planes, sector, radial = conserved.shape
    out = jax.ShapeDtypeStruct((fields, 2, sector - sector * CYCLES // radial, radial), jnp.float32)
    early = jax.ShapeDtypeStruct((fields, 2 * planes, radial), jnp.float32)
    last = sector // ROWS - 1
    wide = pl.BlockSpec(out.shape, lambda i, *_: (0, 0, 0, 0))
    return pl.pallas_call(
        edge_kernel,
        grid_spec=pltpu.PrefetchScalarGridSpec(
            num_scalar_prefetch=1,
            grid=(2,),
            in_specs=[
                pl.BlockSpec(
                    (fields, 2, sector, radial), lambda i, az: (0, (planes // 2 - 1) * (1 - i), 0, 0)
                ),
                pl.BlockSpec(
                    (fields, planes, ROWS, radial),
                    lambda i, az: (0, 0, last * (1 - lax.rem(az[0], 2)), 0),
                ),
            ],
            out_specs=[wide, wide, pl.BlockSpec(early.shape, lambda i, *_: (0, 0, 0))],
        ),
        out_shape=[out, out, early],
        compiler_params=params(),
        cost_estimate=cost(400 * sector * radial, 4 * 8 * fields * sector * radial),
        name="edge_terms",
    )(az, conserved, conserved)


def here_specs(table, sector):
    return pl.BlockSpec((sector, COEFS), lambda i, az, *_: (az[0], 0))


def inner_kernel(dtheta, *refs):
    az_ref, q_ref, rim_ref, before_ref, here_ref, after_ref, _ = refs[:7]
    message_ref, later_ref, local, swirl, outside = refs[7:]
    fields, planes, sector, radial = q_ref.shape
    group = 2 * CYCLES
    scale = time_step / 12.0
    chunk = min(sector, 8 * ROWS)
    lane = lax.broadcasted_iota(jnp.int32, (1, radial), 1)
    cycle = lane & (group - 1)
    plane = lane // group
    radius = cycle.astype(jnp.float32) + 0.5
    inverse = 1.0 / radius
    near = 8.0 * scale * inverse
    far = scale * inverse
    near_down = jnp.where(cycle >= 1, near, 0.0)
    far_down = jnp.where(cycle >= 2, far, 0.0)
    source = time_step * inverse
    turn = scale * inverse / dtheta

    def split(there, value):
        return jnp.where(there, value, 0.0), jnp.where(there, 0.0, value)

    behind, behind_out = split(plane >= 1, 8.0 * scale)
    behind2, behind2_out = split(plane >= 2, scale)
    ahead, ahead_out = split(plane < planes - 1, 8.0 * scale)
    ahead2, ahead2_out = split(plane < planes - 2, scale)

    zeros = jnp.zeros((FIELDS, 2 * ROWS, radial), jnp.float32)
    swirl[:, : 2 * ROWS, :] = zeros
    swirl[:, 2 * ROWS + sector :, :] = zeros
    local[:, :ROWS, :] = zeros[:, :ROWS]
    local[:, ROWS + sector :, :] = zeros[:, :ROWS]

    def body(i, _):
        start = pl.multiple_of(i * chunk, chunk)
        rows = pl.ds(start, chunk)
        q = []
        for f in range(FIELDS):
            packed = q_ref[f, 0, rows, :]
            for k in range(1, planes):
                moved = pltpu.roll(q_ref[f, k, rows, :], group * k, 1)
                packed = jnp.where(plane == k, moved, packed)
            q.append(packed)
        u, v, w, p = primitives(q)
        along = carried(q, p, u, 1)
        around = carried(q, p, w, 3)
        outward = carried(q, p, v, 2)
        for f in range(FIELDS):
            swirl[f, pl.ds(start + 2 * ROWS, chunk), :] = around[f]
            g = outward[f] * radius
            value = q[f] - near * pltpu.roll(g, radial - 1, 1)
            value = value + near_down * pltpu.roll(g, 1, 1)
            value = value + far * pltpu.roll(g, radial - 2, 1)
            value = value - far_down * pltpu.roll(g, 2, 1)
            if f == 2:
                value = value + source * (p + q[3] * w)
            if f == 3:
                value = value - source * (q[2] * w)
            up1 = pltpu.roll(along[f], group, 1)
            up2 = pltpu.roll(along[f], 2 * group, 1)
            down1 = pltpu.roll(along[f], radial - group, 1)
            down2 = pltpu.roll(along[f], radial - 2 * group, 1)
            value = value + behind * up1 - behind2 * up2 - ahead * down1 + ahead2 * down2
            local[f, pl.ds(start + ROWS, chunk), :] = value
            outside[f, rows, :] = (
                behind_out * up1 - behind2_out * up2 - ahead_out * down1 + ahead2_out * down2
            )
        return 0

    lax.fori_loop(0, sector // chunk, body, 0)

    def rest(start, size):
        for f in range(FIELDS):
            at = lambda k: swirl[f, pl.ds(start + (ROWS + k), size), :]
            around = 8.0 * (at(1) - at(-1)) - (at(2) - at(-2))
            rows = pl.ds(start, size)
            local[f, rows, :] = local[f, rows, :] - turn * around

    rest(0, ROWS)
    rest(ROWS + sector, ROWS)

    def body2(i, _):
        rest(pl.multiple_of(i * chunk, chunk) + ROWS, chunk)
        return 0

    lax.fori_loop(0, sector // chunk, body2, 0)

    basis = jnp.concatenate([before_ref[...], here_ref[...], after_ref[...]], axis=0)

    def transform(rows, table):
        return lax.dot_general(
            rows, table, (((0,), (0,)), ((), ())),
            precision=HIGHEST, preferred_element_type=jnp.float32,
        )

    for f in range(FIELDS):
        own = transform(local[f], basis)
        for k in range(planes):
            message_ref[f, k * CYCLES : (k + 1) * CYCLES, :] = own[k * group : k * group + CYCLES]
        other = transform(outside[f], here_ref[...])
        for s, k in enumerate((0, 1, planes - 2, planes - 1)):
            at = (planes + s) * CYCLES
            message_ref[f, at : at + CYCLES, :] = other[k * group : k * group + CYCLES]

    for k, flux in swirl_rows(rim_ref, lax.rem(az_ref[0], 2) == 0):
        for f in range(FIELDS):
            later_ref[f, 2 * k : 2 * k + 2, :] = flux[f]


def inner_terms(conserved, az, table, after):
    fields, planes, sector, radial = conserved.shape
    length = table.shape[0]
    message = (fields, (planes + 4) * CYCLES, COEFS)
    later = (fields, 2 * planes, radial)
    full = lambda *shape: pl.BlockSpec(shape, lambda i, *_: (0,) * len(shape))
    tiles = sector // ROWS
    wrap = lambda k: lax.rem(k + length // ROWS, length // ROWS)
    return pl.pallas_call(
        functools.partial(inner_kernel, 2.0 * math.pi / length),
        grid_spec=pltpu.PrefetchScalarGridSpec(
            num_scalar_prefetch=1,
            grid=(1,),
            in_specs=[
                full(*conserved.shape),
                pl.BlockSpec(
                    (fields, planes, ROWS, radial),
                    lambda i, az: (0, 0, (tiles - 1) * lax.rem(az[0], 2), 0),
                ),
                pl.BlockSpec((ROWS, COEFS), lambda i, az: (wrap(az[0] * tiles - 1), 0)),
                here_specs(table, sector),
                pl.BlockSpec((ROWS, COEFS), lambda i, az: (wrap((az[0] + 1) * tiles), 0)),
                pl.BlockSpec(memory_space=pl.ANY),
            ],
            out_specs=[full(*message), full(*later)],
            scratch_shapes=[
                pltpu.VMEM((fields, sector + 2 * ROWS, radial), jnp.float32),
                pltpu.VMEM((fields, sector + 4 * ROWS, radial), jnp.float32),
                pltpu.VMEM((fields, sector, radial), jnp.float32),
            ],
        ),
        out_shape=[
            jax.ShapeDtypeStruct(message, jnp.float32),
            jax.ShapeDtypeStruct(later, jnp.float32),
        ],
        compiler_params=params(),
        cost_estimate=cost(60 * sector * radial * COEFS, 4 * fields * planes * sector * radial),
        name="inner_terms",
    )(az, conserved, conserved, table, table, table, after)


def panel_kernel(cells_ref, count_ref, row_ref, q_ref, bins_ref, amp_ref, _, out_ref, held):
    slots = row_ref.shape[1]
    radial = q_ref.shape[2]
    observers = bins_ref.shape[0]
    count = count_ref[0]
    width = 8

    def fetch(i, _):
        for k in range(width):
            s = i * width + k
            at = cells_ref[s] // radial
            held[:, pl.ds(s, 1), :] = q_ref[:, pl.ds(at, 1), :]
        return 0

    lax.fori_loop(0, (count + width - 1) // width, fetch, 0)
    q = [held[f] for f in range(FIELDS)]
    p = gas_factor * (q[4] - 0.5 * (q[1] * q[1] + q[2] * q[2] + q[3] * q[3]) / q[0])
    turned = jnp.transpose(p)
    which = lax.broadcasted_iota(jnp.int32, (radial, slots), 0)
    here = which == (row_ref[...] & (radial - 1))
    sampled = jnp.sum(jnp.where(here, turned, 0.0), axis=0, keepdims=True) - ref_pressure
    slot = lax.broadcasted_iota(jnp.int32, (1, slots), 1)
    sampled = jnp.where(slot < count, sampled, 0.0)

    contrib = sampled * amp_ref[...]
    first = contrib.astype(jnp.bfloat16).astype(jnp.float32)
    second = contrib - first
    bins = bins_ref[...]
    low = bins & (LOW_BINS - 1)
    high = bins // LOW_BINS
    each = 128 // LOW_BINS
    high_count = BINS // LOW_BINS
    low_iota = lax.broadcasted_iota(jnp.int32, (LOW_BINS, slots), 0)
    high_iota = lax.broadcasted_iota(jnp.int32, (high_count, slots), 0)
    lane = lax.broadcasted_iota(jnp.int32, (high_count, 128), 1)
    for g in range(observers // each):
        left, right = [], []
        for k in range(each):
            o = g * each + k
            hit = high_iota == high[o : o + 1]
            left.append(jnp.where(hit, first[o : o + 1], 0.0).astype(jnp.bfloat16))
            left.append(jnp.where(hit, second[o : o + 1], 0.0).astype(jnp.bfloat16))
            same = low_iota == low[o : o + 1]
            right.append(jnp.where(same, 1.0, 0.0).astype(jnp.bfloat16))
        sums = lax.dot_general(
            jnp.concatenate(left, axis=0),
            jnp.concatenate(right, axis=0),
            (((1,), (1,)), ((), ())),
            preferred_element_type=jnp.float32,
        )
        total = jnp.zeros((high_count, 128), jnp.float32)
        for k in range(each):
            at = 2 * k * high_count
            both = sums[at : at + high_count] + sums[at + high_count : at + 2 * high_count]
            total = jnp.where(lane // LOW_BINS == k, both, total)
        out_ref[:, g, :] = total


def panel_sums(conserved, cells, counts, bins, amplitudes, after):
    fields, planes, sector, radial = conserved.shape
    slots, observers = bins.shape
    flat = conserved.reshape(fields, planes * sector, radial)
    high_count = BINS // LOW_BINS
    full = lambda *shape: pl.BlockSpec(shape, lambda i, *_: (0,) * len(shape))
    return pl.pallas_call(
        panel_kernel,
        grid_spec=pltpu.PrefetchScalarGridSpec(
            num_scalar_prefetch=2,
            grid=(1,),
            in_specs=[
                full(1, slots),
                full(fields, planes * sector, radial),
                full(observers, slots),
                full(observers, slots),
                pl.BlockSpec(memory_space=pl.ANY),
            ],
            out_specs=full(high_count, observers * LOW_BINS // 128, 128),
            scratch_shapes=[pltpu.VMEM((fields, slots, radial), jnp.float32)],
        ),
        out_shape=jax.ShapeDtypeStruct(
            (high_count, observers * LOW_BINS // 128, 128), jnp.float32
        ),
        compiler_params=params(),
        cost_estimate=cost(8 * observers * slots * BINS, 4 * fields * planes * sector * radial),
        name="panel_sums",
    )(cells, counts, cells.reshape(1, slots), flat, bins.T, amplitudes.T, after)


def section_kernel(dtheta, *refs):
    az_ref, q_ref, mine_ref, theirs_ref, early_ref, late_ref, weight_ref, basis_ref = refs[:8]
    out_ref, axial, swirl, local, spec, smooth = refs[8:]
    fields, _, sector, radial = q_ref.shape
    step = pl.program_id(0)
    planes = pl.num_programs(0) - 2
    scale = time_step / 12.0
    chunk = min(sector, 16 * ROWS)
    lane = lax.broadcasted_iota(jnp.int32, (1, radial), 1)
    radius = lane.astype(jnp.float32) + 0.5
    inverse = 1.0 / radius
    near = 8.0 * scale * inverse
    far = scale * inverse
    near_up = jnp.where(lane < radial - 1, near, 0.0)
    near_down = jnp.where(lane >= 1, near, 0.0)
    far_up = jnp.where(lane < radial - 2, far, 0.0)
    far_down = jnp.where(lane >= 2, far, 0.0)
    source = time_step * inverse
    odd = lax.rem(az_ref[0], 2) == 1
    static_planes = axial.shape[0] - 4

    @pl.when(step == 0)
    def _():
        axial[0:2] = jnp.zeros((2,) + axial.shape[1:], jnp.float32)
        axial[planes + 2 : planes + 4] = jnp.zeros((2,) + axial.shape[1:], jnp.float32)
        spec[...] = jnp.zeros_like(spec)
        for k in range(static_planes):
            for f in range(FIELDS):
                rows = slice(k * CYCLES, (k + 1) * CYCLES)
                value = mine_ref[f, rows, :] + theirs_ref[f, rows, :]
                spec[k, f * CYCLES : (f + 1) * CYCLES, :] = value * weight_ref[...]

    @pl.when(step < planes)
    def _():
        slot = lax.rem(step, 3)
        for f in range(FIELDS):
            early = early_ref[f, pl.ds(2 * step, 2), :]
            late = late_ref[f, pl.ds(2 * step, 2), :]
            swirl[slot, f, ROWS - 2 : ROWS, :] = jnp.where(odd, early, late)
            swirl[slot, f, ROWS + sector : ROWS + sector + 2, :] = jnp.where(odd, late, early)

        def body(i, _):
            start = pl.multiple_of(i * chunk, chunk)
            rows = pl.ds(start, chunk)
            q = [q_ref[f, 0, rows, :] for f in range(FIELDS)]
            u, v, w, p = primitives(q)
            along = carried(q, p, u, 1)
            around = carried(q, p, w, 3)
            outward = carried(q, p, v, 2)
            for f in range(FIELDS):
                axial[step + 2, f, rows, :] = along[f]
                swirl[slot, f, pl.ds(start + ROWS, chunk), :] = around[f]
                g = outward[f] * radius
                value = q[f] - near_up * pltpu.roll(g, radial - 1, 1)
                value = value + near_down * pltpu.roll(g, 1, 1)
                value = value + far_up * pltpu.roll(g, radial - 2, 1)
                value = value - far_down * pltpu.roll(g, 2, 1)
                if f == 2:
                    value = value + source * (p + q[3] * w)
                if f == 3:
                    value = value - source * (q[2] * w)
                local[slot, f, rows, :] = value
            return 0

        lax.fori_loop(0, sector // chunk, body, 0)

    @pl.when(step >= 2)
    def _():
        plane = step - 2
        slot = lax.rem(plane, 3)
        turn = scale * inverse / dtheta
        smooth[...] = lax.dot_general(
            basis_ref[...], spec[plane], (((1,), (1,)), ((), ())),
            precision=HIGHEST, preferred_element_type=jnp.float32,
        )

        def body(i, _):
            start = pl.multiple_of(i * chunk, chunk)
            rows = pl.ds(start, chunk)
            for f in range(FIELDS):
                at = lambda k: swirl[slot, f, pl.ds(start + (ROWS + k), chunk), :]
                of = lambda k: axial[plane + 2 + k, f, rows, :]
                around = 8.0 * (at(1) - at(-1)) - (at(2) - at(-2))
                along = 8.0 * (of(1) - of(-1)) - (of(2) - of(-2))
                value = local[slot, f, rows, :] - turn * around - scale * along
                moved = smooth[rows, :]
                if f > 0:
                    moved = pltpu.roll(moved, radial - CYCLES * f, 1)
                out_ref[f, 0, rows, :] = jnp.where(lane < CYCLES, moved, value)
            return 0

        lax.fori_loop(0, sector // chunk, body, 0)


def local_section(conserved, az, mine, theirs, early, late, weights, table):
    fields, planes, sector, radial = conserved.shape
    length = table.shape[0]
    two_back = lambda i: jnp.maximum(i - 2, 0)
    ring = (fields, 2 * planes, radial)
    last = late.shape[1] // ring[1] - 1
    full = lambda a: pl.BlockSpec(a.shape, lambda i, *_: (0,) * a.ndim)
    plane = (fields, 1, sector, radial)
    return pl.pallas_call(
        functools.partial(section_kernel, 2.0 * math.pi / length),
        grid_spec=pltpu.PrefetchScalarGridSpec(
            num_scalar_prefetch=1,
            grid=(planes + 2,),
            in_specs=[
                pl.BlockSpec(plane, lambda i, *_: (0, jnp.minimum(i, planes - 1), 0, 0)),
                full(mine),
                full(theirs),
                full(early),
                pl.BlockSpec(ring, lambda i, *_: (0, last, 0)),
                full(weights),
                here_specs(table, sector),
            ],
            out_specs=pl.BlockSpec(plane, lambda i, *_: (0, two_back(i), 0, 0)),
            scratch_shapes=[
                pltpu.VMEM((planes + 4, fields, sector, radial), jnp.float32),
                pltpu.VMEM((3, fields, sector + 2 * ROWS, radial), jnp.float32),
                pltpu.VMEM((3, fields, sector, radial), jnp.float32),
                pltpu.VMEM((planes, radial, COEFS), jnp.float32),
                pltpu.VMEM((sector, radial), jnp.float32),
            ],
        ),
        out_shape=jax.ShapeDtypeStruct(conserved.shape, jnp.float32),
        compiler_params=params(),
        cost_estimate=cost(
            600 * planes * sector * radial, 10 * 4 * fields * planes * sector * radial
        ),
        name="local_section",
    )(az, conserved, mine, theirs, early, late, weights, table)


def add_kernel(az_ref, part_ref, low_ref, high_ref, spec_low, spec_high, weight_ref, basis_ref, sums_ref, *outs):
    out_ref, signal_ref, padded, turned = outs
    step = pl.program_id(0)
    fields, _, sector, radial = part_ref.shape
    groups = radial // CYCLES - 1
    tail = sector // (groups + 1)
    main = groups * tail
    lane = lax.broadcasted_iota(jnp.int32, (1, radial), 1)
    wide = lane >= CYCLES

    @pl.when(step == 0)
    def _():
        padded[...] = jnp.zeros_like(padded)
        observers, _ = turned.shape
        bins = signal_ref.shape[0]
        total = jnp.sum(sums_ref[...], axis=0)
        for o in range(observers):
            row, at = o * bins // 128, o * bins % 128
            piece = total[row : row + 1]
            turned[o : o + 1, :] = pltpu.roll(piece, 128 - at, 1) if at else piece
        signal_ref[...] = jnp.transpose(turned[...])[:bins]

    def go(ref, spec_ref, slot):
        for f in range(fields):
            rows = slice(slot * CYCLES, (slot + 1) * CYCLES)
            padded[f * CYCLES : (f + 1) * CYCLES, :] = spec_ref[f, rows, :] * weight_ref[...]
        smooth = lax.dot_general(
            basis_ref[...], padded[...], (((1,), (1,)), ((), ())),
            precision=HIGHEST, preferred_element_type=jnp.float32,
        )
        for f in range(fields):
            inner = smooth if f == 0 else pltpu.roll(smooth, radial - CYCLES * f, 1)
            out_ref[f, 0, :main, :] = part_ref[f, 0, :main, :] + jnp.where(
                wide, ref[f, 0], inner[:main]
            )
            rest = inner[main:]
            for g in range(groups):
                moved = pltpu.roll(ref[f, 0, g * tail : (g + 1) * tail, :], CYCLES * (g + 1), 1)
                rest = jnp.where(lane // CYCLES == g + 1, moved, rest)
            out_ref[f, 0, main:, :] = part_ref[f, 0, main:, :] + rest

    for k in range(2):
        pl.when(step == k)(lambda k=k: go(low_ref, spec_low, k))
        pl.when(step == 2 + k)(lambda k=k: go(high_ref, spec_high, k))


def add_edges(section, az, low, high, spec_low, spec_high, weights, table, sums, observers):
    fields, planes, sector, radial = section.shape
    main = low.shape[2]
    bins = sums.shape[1] * sums.shape[2] // observers
    full = lambda a: pl.BlockSpec(a.shape, lambda i, *_: (0,) * a.ndim)
    plane = pl.BlockSpec(
        (fields, 1, sector, radial), lambda i, *_: (0, jnp.where(i < 2, i, planes - 4 + i), 0, 0)
    )
    return pl.pallas_call(
        add_kernel,
        grid_spec=pltpu.PrefetchScalarGridSpec(
            num_scalar_prefetch=1,
            grid=(4,),
            in_specs=[
                plane,
                pl.BlockSpec((fields, 1, main, radial), lambda i, *_: (0, jnp.minimum(i, 1), 0, 0)),
                pl.BlockSpec((fields, 1, main, radial), lambda i, *_: (0, jnp.maximum(i - 2, 0), 0, 0)),
                full(spec_low),
                full(spec_high),
                full(weights),
                here_specs(table, sector),
                full(sums),
            ],
            out_specs=[plane, pl.BlockSpec((bins, observers), lambda i, *_: (0, 0))],
            scratch_shapes=[
                pltpu.VMEM((radial, COEFS), jnp.float32),
                pltpu.VMEM((observers, 128), jnp.float32),
            ],
        ),
        out_shape=[
            jax.ShapeDtypeStruct(section.shape, jnp.float32),
            jax.ShapeDtypeStruct((bins, observers), jnp.float32),
        ],
        input_output_aliases={1: 0},
        compiler_params=params(),
        cost_estimate=cost(8 * fields * sector * radial, 4 * 12 * fields * sector * radial),
        name="add_edges",
    )(az, section, low, high, spec_low, spec_high, weights, table, sums)


def exchanged_sums(partial, observers):
    devices = lax.axis_size("ax") * lax.axis_size("az")
    mine = BINS // devices
    if mine != LOW_BINS:
        partial = partial.reshape(-1, observers, LOW_BINS).transpose(0, 2, 1)
        partial = partial.reshape(devices, mine, observers).transpose(0, 2, 1)
        partial = partial.reshape(devices, observers * mine // 128, 128)
    return lax.all_to_all(partial, ("ax", "az"), split_axis=0, concat_axis=0, tiled=True)


def on_device(conserved, panel_cells, panel_counts, time_bins, amplitudes):
    fields, planes, sector, radial = conserved.shape
    observers = time_bins.shape[1]
    n_ax, n_az = lax.axis_size("ax"), lax.axis_size("az")
    length = sector * n_az
    up = [(i, i + 1) for i in range(n_ax - 1)]
    down = [(j, i) for i, j in up]
    az = lax.axis_index("az").astype(jnp.int32).reshape(1)
    table = jnp.asarray(basis_table(length))
    weights = jnp.asarray(mode_weights(length))

    pair = [(i, i ^ 1) for i in range(n_az)]
    send_up, send_down, early = edge_terms(conserved, az)
    early = lax.ppermute(early, "az", pair)
    low = lax.ppermute(send_up, "ax", up)
    high = lax.ppermute(send_down, "ax", down)

    partial = panel_sums(conserved, panel_cells, panel_counts, time_bins, amplitudes, early)
    sums = exchanged_sums(partial, observers)

    message, later = inner_terms(conserved, az, table, partial)
    edge = (planes + 4) * CYCLES
    mine = jnp.concatenate([message + lax.ppermute(message, "az", pair), later], axis=1)
    pairs = [(i, (i + 1) % n_az) for i in range(1, n_az, 2)]
    theirs = lax.ppermute(mine, "az", pairs + [(j, i) for i, j in pairs])
    late = theirs
    shift = 4
    while shift < n_az:
        mine = mine + theirs
        theirs = lax.ppermute(mine, "az", [(i, (i + shift) % n_az) for i in range(n_az)])
        shift *= 2
    outside = mine[:, planes * CYCLES : edge] + theirs[:, planes * CYCLES : edge]
    spec_low = lax.ppermute(outside[:, : 2 * CYCLES], "ax", up)
    spec_high = lax.ppermute(outside[:, 2 * CYCLES :], "ax", down)

    section = local_section(conserved, az, mine, theirs, early, late, weights, table)
    section, signal = add_edges(
        section, az, low, high, spec_low, spec_high, weights, table, sums, observers
    )
    return (section, signal.T)


def solution(mesh):
    placed = (
        P(None, "ax", "az", None),
        P(("ax", "az")),
        P(("ax", "az")),
        P(("ax", "az"), None),
        P(("ax", "az"), None),
    )
    return jax.shard_map(
        on_device,
        mesh=mesh,
        in_specs=placed,
        out_specs=(P(None, "ax", "az", None), P(None, ("ax", "az"))),
        check_vma=False,
    )
```

```python
import functools
import math

import jax
import jax.numpy as jnp
import numpy as np
from jax import lax
from jax.experimental import pallas as pl
from jax.experimental.pallas import tpu as pltpu
from jax.sharding import PartitionSpec as P

CYCLES = 8
BINS = 1024
LOW_BINS = 32
FIELDS = 5
MODES = 8 * CYCLES
COEFS = 2 * MODES
ROWS = 8

gas_factor = 0.4
time_step = 0.02
ref_pressure = 0.95
VMEM_BYTES = 48 * 1024 * 1024

HIGHEST = lax.Precision.HIGHEST


def params(**more):
    return pltpu.CompilerParams(vmem_limit_bytes=VMEM_BYTES, **more)


def cost(flops, touched):
    return pl.CostEstimate(flops=flops, bytes_accessed=touched, transcendentals=0)


def basis_table(length):
    phase = (np.arange(length)[:, None] * np.arange(MODES)[None, :] % length) * (
        2.0 * math.pi / length
    )
    return np.concatenate([np.cos(phase), np.sin(phase)], axis=1).astype(np.float32)


def mode_weights(length):
    modes = np.arange(MODES).astype(np.float64)
    cutoff = 4.0 * (np.arange(CYCLES) + 1.0)
    weight = np.exp(-((modes[None, :] / cutoff[:, None]) ** 8))
    weight = weight * np.where(modes == 0, 1.0, 2.0)[None, :] / length
    return np.concatenate([weight, weight], axis=1).astype(np.float32)


def primitives(q):
    inverse = 1.0 / q[0]
    u, v, w = q[1] * inverse, q[2] * inverse, q[3] * inverse
    p = gas_factor * (q[4] - 0.5 * (q[1] * u + q[2] * v + q[3] * w))
    return u, v, w, p


def carried(q, p, speed, heading):
    flux = [q[0] * speed, q[1] * speed, q[2] * speed, q[3] * speed, (q[4] + p) * speed]
    flux[heading] = flux[heading] + p
    return flux


def swirl_rows(ref, low):
    for k in range(ref.shape[1]):
        q = [ref[f, k] for f in range(FIELDS)]
        _, _, w, p = primitives(q)
        flux = carried(q, p, w, 3)
        yield k, [jnp.where(low, f[:2], f[ROWS - 2 :]) for f in flux]


def edge_kernel(az_ref, q_ref, rim_ref, up_ref, down_ref, early_ref):
    sector, radial = q_ref.shape[2:]
    groups = radial // CYCLES - 1
    tail = sector * CYCLES // radial
    scale = time_step / 12.0
    lane = lax.broadcasted_iota(jnp.int32, (1, radial), 1)

    def go(up, send):
        def terms(start):
            rows = pl.ds(start, tail)
            flux = []
            for plane in range(2):
                q = [q_ref[f, plane, rows, :] for f in range(FIELDS)]
                u, _, _, p = primitives(q)
                flux.append(carried(q, p, u, 1))
            near, far = (flux[1], flux[0]) if up else (flux[0], flux[1])
            whole, part = [], []
            for f in range(FIELDS):
                wide = scale * (8.0 * near[f] - far[f])
                narrow = scale * near[f]
                whole.append(wide if up else -wide)
                part.append(-narrow if up else narrow)
            return (whole, part) if up else (part, whole)

        last = terms(groups * tail)
        for g in range(groups):
            slots = terms(g * tail)
            shift = radial - CYCLES * (g + 1)
            for s in range(2):
                for f in range(FIELDS):
                    moved = pltpu.roll(last[s][f], shift, 1)
                    send[f, s, pl.ds(g * tail, tail), :] = jnp.where(
                        lane < CYCLES, moved, slots[s][f]
                    )

    @pl.when(pl.program_id(0) == 0)
    def _():
        go(True, up_ref)
        for k, flux in swirl_rows(rim_ref, lax.rem(az_ref[0], 2) == 1):
            for f in range(FIELDS):
                early_ref[f, 2 * k : 2 * k + 2, :] = flux[f]

    pl.when(pl.program_id(0) == 1)(lambda: go(False, down_ref))


def edge_terms(conserved, az):
    fields, planes, sector, radial = conserved.shape
    out = jax.ShapeDtypeStruct((fields, 2, sector - sector * CYCLES // radial, radial), jnp.float32)
    early = jax.ShapeDtypeStruct((fields, 2 * planes, radial), jnp.float32)
    last = sector // ROWS - 1
    wide = pl.BlockSpec(out.shape, lambda i, *_: (0, 0, 0, 0))
    return pl.pallas_call(
        edge_kernel,
        grid_spec=pltpu.PrefetchScalarGridSpec(
            num_scalar_prefetch=1,
            grid=(2,),
            in_specs=[
                pl.BlockSpec(
                    (fields, 2, sector, radial), lambda i, az: (0, (planes // 2 - 1) * (1 - i), 0, 0)
                ),
                pl.BlockSpec(
                    (fields, planes, ROWS, radial),
                    lambda i, az: (0, 0, last * (1 - lax.rem(az[0], 2)), 0),
                ),
            ],
            out_specs=[wide, wide, pl.BlockSpec(early.shape, lambda i, *_: (0, 0, 0))],
        ),
        out_shape=[out, out, early],
        compiler_params=params(),
        cost_estimate=cost(400 * sector * radial, 4 * 8 * fields * sector * radial),
        name="edge_terms",
    )(az, conserved, conserved)


def inner_kernel(dtheta, *refs):
    az_ref, q_ref, rim_ref, basis_ref, _ = refs[:5]
    message_ref, later_ref, local, swirl, outside = refs[5:]
    fields, planes, sector, radial = q_ref.shape
    group = 2 * CYCLES
    scale = time_step / 12.0
    chunk = min(sector, 32 * ROWS)
    lane = lax.broadcasted_iota(jnp.int32, (1, radial), 1)
    cycle = lane & (group - 1)
    plane = lane // group
    radius = cycle.astype(jnp.float32) + 0.5
    inverse = 1.0 / radius
    near = 8.0 * scale * inverse
    far = scale * inverse
    near_down = jnp.where(cycle >= 1, near, 0.0)
    far_down = jnp.where(cycle >= 2, far, 0.0)
    source = time_step * inverse
    turn = scale * inverse / dtheta

    def split(there, value):
        return jnp.where(there, value, 0.0), jnp.where(there, 0.0, value)

    behind, behind_out = split(plane >= 1, 8.0 * scale)
    behind2, behind2_out = split(plane >= 2, scale)
    ahead, ahead_out = split(plane < planes - 1, 8.0 * scale)
    ahead2, ahead2_out = split(plane < planes - 2, scale)

    zeros = jnp.zeros((FIELDS, 2 * ROWS, radial), jnp.float32)
    swirl[:, : 2 * ROWS, :] = zeros
    swirl[:, 2 * ROWS + sector :, :] = zeros
    local[:, :ROWS, :] = zeros[:, :ROWS]
    local[:, ROWS + sector :, :] = zeros[:, :ROWS]

    def body(i, _):
        start = pl.multiple_of(i * chunk, chunk)
        rows = pl.ds(start, chunk)
        q = []
        for f in range(FIELDS):
            packed = q_ref[f, 0, rows, :]
            for k in range(1, planes):
                moved = pltpu.roll(q_ref[f, k, rows, :], group * k, 1)
                packed = jnp.where(plane == k, moved, packed)
            q.append(packed)
        u, v, w, p = primitives(q)
        along = carried(q, p, u, 1)
        around = carried(q, p, w, 3)
        outward = carried(q, p, v, 2)
        for f in range(FIELDS):
            swirl[f, pl.ds(start + 2 * ROWS, chunk), :] = around[f]
            g = outward[f] * radius
            value = q[f] - near * pltpu.roll(g, radial - 1, 1)
            value = value + near_down * pltpu.roll(g, 1, 1)
            value = value + far * pltpu.roll(g, radial - 2, 1)
            value = value - far_down * pltpu.roll(g, 2, 1)
            if f == 2:
                value = value + source * (p + q[3] * w)
            if f == 3:
                value = value - source * (q[2] * w)
            up1 = pltpu.roll(along[f], group, 1)
            up2 = pltpu.roll(along[f], 2 * group, 1)
            down1 = pltpu.roll(along[f], radial - group, 1)
            down2 = pltpu.roll(along[f], radial - 2 * group, 1)
            value = value + behind * up1 - behind2 * up2 - ahead * down1 + ahead2 * down2
            local[f, pl.ds(start + ROWS, chunk), :] = value
            outside[f, rows, :] = (
                behind_out * up1 - behind2_out * up2 - ahead_out * down1 + ahead2_out * down2
            )
        return 0

    lax.fori_loop(0, sector // chunk, body, 0)

    def rest(start, size):
        for f in range(FIELDS):
            at = lambda k: swirl[f, pl.ds(start + (ROWS + k), size), :]
            around = 8.0 * (at(1) - at(-1)) - (at(2) - at(-2))
            rows = pl.ds(start, size)
            local[f, rows, :] = local[f, rows, :] - turn * around

    rest(0, ROWS)
    rest(ROWS + sector, ROWS)

    def body2(i, _):
        rest(pl.multiple_of(i * chunk, chunk) + ROWS, chunk)
        return 0

    lax.fori_loop(0, sector // chunk, body2, 0)

    def transform(rows, table):
        return lax.dot_general(
            rows, table, (((0,), (0,)), ((), ())),
            precision=HIGHEST, preferred_element_type=jnp.float32,
        )

    for f in range(FIELDS):
        own = transform(local[f], basis_ref[: sector + 2 * ROWS, :])
        for k in range(planes):
            message_ref[f, k * CYCLES : (k + 1) * CYCLES, :] = own[k * group : k * group + CYCLES]
        other = transform(outside[f], basis_ref[ROWS : ROWS + sector, :])
        for s, k in enumerate((0, 1, planes - 2, planes - 1)):
            at = (planes + s) * CYCLES
            message_ref[f, at : at + CYCLES, :] = other[k * group : k * group + CYCLES]

    for k, flux in swirl_rows(rim_ref, lax.rem(az_ref[0], 2) == 0):
        for f in range(FIELDS):
            later_ref[f, 2 * k : 2 * k + 2, :] = flux[f]


def inner_terms(conserved, az, basis, length, after):
    fields, planes, sector, radial = conserved.shape
    message = (fields, (planes + 4) * CYCLES, COEFS)
    later = (fields, 2 * planes, radial)
    full = lambda *shape: pl.BlockSpec(shape, lambda i, *_: (0,) * len(shape))
    tiles = sector // ROWS
    return pl.pallas_call(
        functools.partial(inner_kernel, 2.0 * math.pi / length),
        grid_spec=pltpu.PrefetchScalarGridSpec(
            num_scalar_prefetch=1,
            grid=(1,),
            in_specs=[
                full(*conserved.shape),
                pl.BlockSpec(
                    (fields, planes, ROWS, radial),
                    lambda i, az: (0, 0, (tiles - 1) * lax.rem(az[0], 2), 0),
                ),
                full(*basis.shape),
                pl.BlockSpec(memory_space=pl.ANY),
            ],
            out_specs=[full(*message), full(*later)],
            scratch_shapes=[
                pltpu.VMEM((fields, sector + 2 * ROWS, radial), jnp.float32),
                pltpu.VMEM((fields, sector + 4 * ROWS, radial), jnp.float32),
                pltpu.VMEM((fields, sector, radial), jnp.float32),
            ],
        ),
        out_shape=[
            jax.ShapeDtypeStruct(message, jnp.float32),
            jax.ShapeDtypeStruct(later, jnp.float32),
        ],
        compiler_params=params(),
        cost_estimate=cost(60 * sector * radial * COEFS, 4 * fields * planes * sector * radial),
        name="inner_terms",
    )(az, conserved, conserved, basis, after)


def panel_kernel(n_ax, n_az, cells_ref, count_ref, row_ref, q_ref, bins_ref, amp_ref, _, out_ref, held):
    slots = row_ref.shape[1]
    radial = q_ref.shape[2]
    observers = bins_ref.shape[0]
    count = count_ref[0]
    width = 8

    def fetch(i, _):
        for k in range(width):
            s = i * width + k
            at = cells_ref[s] // radial
            held[:, pl.ds(s, 1), :] = q_ref[:, pl.ds(at, 1), :]
        return 0

    lax.fori_loop(0, (count + width - 1) // width, fetch, 0)
    q = [held[f] for f in range(FIELDS)]
    p = gas_factor * (q[4] - 0.5 * (q[1] * q[1] + q[2] * q[2] + q[3] * q[3]) / q[0])
    turned = jnp.transpose(p)
    which = lax.broadcasted_iota(jnp.int32, (radial, slots), 0)
    here = which == (row_ref[...] & (radial - 1))
    sampled = jnp.sum(jnp.where(here, turned, 0.0), axis=0, keepdims=True) - ref_pressure
    slot = lax.broadcasted_iota(jnp.int32, (1, slots), 1)
    sampled = jnp.where(slot < count, sampled, 0.0)

    contrib = sampled * amp_ref[...]
    first = contrib.astype(jnp.bfloat16).astype(jnp.float32)
    second = contrib - first
    bins = bins_ref[...]
    low = bins & (LOW_BINS - 1)
    high = bins // LOW_BINS
    if n_ax * n_az * LOW_BINS == BINS:
        high = (high % n_az) * n_ax + high // n_az
    each = 128 // LOW_BINS
    high_count = BINS // LOW_BINS
    low_iota = lax.broadcasted_iota(jnp.int32, (LOW_BINS, slots), 0)
    high_iota = lax.broadcasted_iota(jnp.int32, (high_count, slots), 0)
    lane = lax.broadcasted_iota(jnp.int32, (high_count, 128), 1)
    for g in range(observers // each):
        left, right = [], []
        for k in range(each):
            o = g * each + k
            hit = high_iota == high[o : o + 1]
            left.append(jnp.where(hit, first[o : o + 1], 0.0).astype(jnp.bfloat16))
            left.append(jnp.where(hit, second[o : o + 1], 0.0).astype(jnp.bfloat16))
            same = low_iota == low[o : o + 1]
            right.append(jnp.where(same, 1.0, 0.0).astype(jnp.bfloat16))
        sums = lax.dot_general(
            jnp.concatenate(left, axis=0),
            jnp.concatenate(right, axis=0),
            (((1,), (1,)), ((), ())),
            preferred_element_type=jnp.float32,
        )
        total = jnp.zeros((high_count, 128), jnp.float32)
        for k in range(each):
            at = 2 * k * high_count
            both = sums[at : at + high_count] + sums[at + high_count : at + 2 * high_count]
            total = jnp.where(lane // LOW_BINS == k, both, total)
        out_ref[:, g, :] = total


def panel_sums(conserved, cells, counts, bins, amplitudes, after):
    fields, planes, sector, radial = conserved.shape
    slots, observers = bins.shape
    flat = conserved.reshape(fields, planes * sector, radial)
    high_count = BINS // LOW_BINS
    full = lambda *shape: pl.BlockSpec(shape, lambda i, *_: (0,) * len(shape))
    return pl.pallas_call(
        functools.partial(panel_kernel, lax.axis_size("ax"), lax.axis_size("az")),
        grid_spec=pltpu.PrefetchScalarGridSpec(
            num_scalar_prefetch=2,
            grid=(1,),
            in_specs=[
                full(1, slots),
                full(fields, planes * sector, radial),
                full(observers, slots),
                full(observers, slots),
                pl.BlockSpec(memory_space=pl.ANY),
            ],
            out_specs=full(high_count, observers * LOW_BINS // 128, 128),
            scratch_shapes=[pltpu.VMEM((fields, slots, radial), jnp.float32)],
        ),
        out_shape=jax.ShapeDtypeStruct(
            (high_count, observers * LOW_BINS // 128, 128), jnp.float32
        ),
        compiler_params=params(),
        cost_estimate=cost(8 * observers * slots * BINS, 4 * fields * planes * sector * radial),
        name="panel_sums",
    )(cells, counts, cells.reshape(1, slots), flat, bins.T, amplitudes.T, after)


def section_kernel(dtheta, *refs):
    az_ref, q_ref, mine_ref, theirs_ref, early_ref, late_ref, basis_ref = refs[:7]
    out_ref, axial, swirl, local, spec, smooth = refs[7:]
    fields, _, sector, radial = q_ref.shape
    step = pl.program_id(0)
    planes = pl.num_programs(0) - 2
    scale = time_step / 12.0
    chunk = min(sector, 32 * ROWS)
    lane = lax.broadcasted_iota(jnp.int32, (1, radial), 1)
    radius = lane.astype(jnp.float32) + 0.5
    inverse = 1.0 / radius
    near = 8.0 * scale * inverse
    far = scale * inverse
    near_up = jnp.where(lane < radial - 1, near, 0.0)
    near_down = jnp.where(lane >= 1, near, 0.0)
    far_up = jnp.where(lane < radial - 2, far, 0.0)
    far_down = jnp.where(lane >= 2, far, 0.0)
    source = time_step * inverse
    odd = lax.rem(az_ref[0], 2) == 1
    static_planes = axial.shape[0] - 4

    @pl.when(step == 0)
    def _():
        axial[0:2] = jnp.zeros((2,) + axial.shape[1:], jnp.float32)
        axial[planes + 2 : planes + 4] = jnp.zeros((2,) + axial.shape[1:], jnp.float32)
        spec[...] = jnp.zeros_like(spec)
        for k in range(static_planes):
            for f in range(FIELDS):
                rows = slice(k * CYCLES, (k + 1) * CYCLES)
                value = mine_ref[f, rows, :] + theirs_ref[f, rows, :]
                spec[k, f * CYCLES : (f + 1) * CYCLES, :] = value * basis_ref[sector + 2 * ROWS :, :]

    @pl.when(step < planes)
    def _():
        slot = lax.rem(step, 3)
        for f in range(FIELDS):
            early = early_ref[f, pl.ds(2 * step, 2), :]
            late = late_ref[f, pl.ds(2 * step, 2), :]
            swirl[slot, f, ROWS - 2 : ROWS, :] = jnp.where(odd, early, late)
            swirl[slot, f, ROWS + sector : ROWS + sector + 2, :] = jnp.where(odd, late, early)

        def body(i, _):
            start = pl.multiple_of(i * chunk, chunk)
            rows = pl.ds(start, chunk)
            q = [q_ref[f, 0, rows, :] for f in range(FIELDS)]
            u, v, w, p = primitives(q)
            along = carried(q, p, u, 1)
            around = carried(q, p, w, 3)
            outward = carried(q, p, v, 2)
            for f in range(FIELDS):
                axial[step + 2, f, rows, :] = along[f]
                swirl[slot, f, pl.ds(start + ROWS, chunk), :] = around[f]
                g = outward[f] * radius
                value = q[f] - near_up * pltpu.roll(g, radial - 1, 1)
                value = value + near_down * pltpu.roll(g, 1, 1)
                value = value + far_up * pltpu.roll(g, radial - 2, 1)
                value = value - far_down * pltpu.roll(g, 2, 1)
                if f == 2:
                    value = value + source * (p + q[3] * w)
                if f == 3:
                    value = value - source * (q[2] * w)
                local[slot, f, rows, :] = value
            return 0

        lax.fori_loop(0, sector // chunk, body, 0)

    @pl.when(step >= 2)
    def _():
        plane = step - 2
        slot = lax.rem(plane, 3)
        turn = scale * inverse / dtheta
        smooth[...] = lax.dot_general(
            basis_ref[ROWS : ROWS + sector, :], spec[plane], (((1,), (1,)), ((), ())),
            precision=HIGHEST, preferred_element_type=jnp.float32,
        )

        def body(i, _):
            start = pl.multiple_of(i * chunk, chunk)
            rows = pl.ds(start, chunk)
            for f in range(FIELDS):
                at = lambda k: swirl[slot, f, pl.ds(start + (ROWS + k), chunk), :]
                of = lambda k: axial[plane + 2 + k, f, rows, :]
                around = 8.0 * (at(1) - at(-1)) - (at(2) - at(-2))
                along = 8.0 * (of(1) - of(-1)) - (of(2) - of(-2))
                value = local[slot, f, rows, :] - turn * around - scale * along
                moved = smooth[rows, :]
                if f > 0:
                    moved = pltpu.roll(moved, radial - CYCLES * f, 1)
                out_ref[f, 0, rows, :] = jnp.where(lane < CYCLES, moved, value)
            return 0

        lax.fori_loop(0, sector // chunk, body, 0)


def local_section(conserved, az, mine, theirs, early, late, basis, length):
    fields, planes, sector, radial = conserved.shape
    two_back = lambda i: jnp.maximum(i - 2, 0)
    ring = (fields, 2 * planes, radial)
    last = late.shape[1] // ring[1] - 1
    full = lambda a: pl.BlockSpec(a.shape, lambda i, *_: (0,) * a.ndim)
    plane = (fields, 1, sector, radial)
    return pl.pallas_call(
        functools.partial(section_kernel, 2.0 * math.pi / length),
        grid_spec=pltpu.PrefetchScalarGridSpec(
            num_scalar_prefetch=1,
            grid=(planes + 2,),
            in_specs=[
                pl.BlockSpec(plane, lambda i, *_: (0, jnp.minimum(i, planes - 1), 0, 0)),
                full(mine),
                full(theirs),
                full(early),
                pl.BlockSpec(ring, lambda i, *_: (0, last, 0)),
                full(basis),
            ],
            out_specs=pl.BlockSpec(plane, lambda i, *_: (0, two_back(i), 0, 0)),
            scratch_shapes=[
                pltpu.VMEM((planes + 4, fields, sector, radial), jnp.float32),
                pltpu.VMEM((3, fields, sector + 2 * ROWS, radial), jnp.float32),
                pltpu.VMEM((3, fields, sector, radial), jnp.float32),
                pltpu.VMEM((planes, radial, COEFS), jnp.float32),
                pltpu.VMEM((sector, radial), jnp.float32),
            ],
        ),
        out_shape=jax.ShapeDtypeStruct(conserved.shape, jnp.float32),
        compiler_params=params(),
        cost_estimate=cost(
            600 * planes * sector * radial, 10 * 4 * fields * planes * sector * radial
        ),
        name="local_section",
    )(az, conserved, mine, theirs, early, late, basis)


def add_kernel(part_ref, low_ref, high_ref, spec_low, spec_high, basis_ref, sums_ref, *outs):
    out_ref, signal_ref, padded, turned = outs
    step = pl.program_id(0)
    fields, _, sector, radial = part_ref.shape
    groups = radial // CYCLES - 1
    tail = sector // (groups + 1)
    main = groups * tail
    lane = lax.broadcasted_iota(jnp.int32, (1, radial), 1)
    wide = lane >= CYCLES

    @pl.when(step == 0)
    def _():
        padded[...] = jnp.zeros_like(padded)
        observers, _ = turned.shape
        bins = signal_ref.shape[0]
        total = jnp.sum(sums_ref[...], axis=0)
        for o in range(observers):
            row, at = o * bins // 128, o * bins % 128
            piece = total[row : row + 1]
            turned[o : o + 1, :] = pltpu.roll(piece, 128 - at, 1) if at else piece
        signal_ref[...] = jnp.transpose(turned[...])[:bins]

    weight = basis_ref[sector + 2 * ROWS :, :]

    def go(ref, spec_ref, slot):
        for f in range(fields):
            rows = slice(slot * CYCLES, (slot + 1) * CYCLES)
            padded[f * CYCLES : (f + 1) * CYCLES, :] = spec_ref[f, rows, :] * weight
        smooth = lax.dot_general(
            basis_ref[ROWS : ROWS + sector, :], padded[...], (((1,), (1,)), ((), ())),
            precision=HIGHEST, preferred_element_type=jnp.float32,
        )
        for f in range(fields):
            inner = smooth if f == 0 else pltpu.roll(smooth, radial - CYCLES * f, 1)
            out_ref[f, 0, :main, :] = part_ref[f, 0, :main, :] + jnp.where(
                wide, ref[f, 0], inner[:main]
            )
            rest = inner[main:]
            for g in range(groups):
                moved = pltpu.roll(ref[f, 0, g * tail : (g + 1) * tail, :], CYCLES * (g + 1), 1)
                rest = jnp.where(lane // CYCLES == g + 1, moved, rest)
            out_ref[f, 0, main:, :] = part_ref[f, 0, main:, :] + rest

    for k in range(2):
        pl.when(step == k)(lambda k=k: go(low_ref, spec_low, k))
        pl.when(step == 2 + k)(lambda k=k: go(high_ref, spec_high, k))


def add_edges(section, low, high, spec_low, spec_high, basis, sums, observers):
    fields, planes, sector, radial = section.shape
    main = low.shape[2]
    bins = sums.shape[1] * sums.shape[2] // observers
    full = lambda a: pl.BlockSpec(a.shape, lambda i, *_: (0,) * a.ndim)
    plane = pl.BlockSpec(
        (fields, 1, sector, radial), lambda i, *_: (0, jnp.where(i < 2, i, planes - 4 + i), 0, 0)
    )
    return pl.pallas_call(
        add_kernel,
        grid_spec=pltpu.PrefetchScalarGridSpec(
            num_scalar_prefetch=0,
            grid=(4,),
            in_specs=[
                plane,
                pl.BlockSpec((fields, 1, main, radial), lambda i, *_: (0, jnp.minimum(i, 1), 0, 0)),
                pl.BlockSpec((fields, 1, main, radial), lambda i, *_: (0, jnp.maximum(i - 2, 0), 0, 0)),
                full(spec_low),
                full(spec_high),
                full(basis),
                full(sums),
            ],
            out_specs=[plane, pl.BlockSpec((bins, observers), lambda i, *_: (0, 0))],
            scratch_shapes=[
                pltpu.VMEM((radial, COEFS), jnp.float32),
                pltpu.VMEM((observers, 128), jnp.float32),
            ],
        ),
        out_shape=[
            jax.ShapeDtypeStruct(section.shape, jnp.float32),
            jax.ShapeDtypeStruct((bins, observers), jnp.float32),
        ],
        input_output_aliases={0: 0},
        compiler_params=params(),
        cost_estimate=cost(8 * fields * sector * radial, 4 * 12 * fields * sector * radial),
        name="add_edges",
    )(section, low, high, spec_low, spec_high, basis, sums)


def exchanged_sums(partial, observers):
    n_ax, n_az = lax.axis_size("ax"), lax.axis_size("az")
    mine = BINS // (n_ax * n_az)
    if mine != LOW_BINS:
        partial = partial.reshape(-1, observers, LOW_BINS).transpose(0, 2, 1)
        partial = partial.reshape(n_ax, n_az, mine, observers).transpose(1, 0, 3, 2)
    blocks = partial.reshape(n_az, n_ax, observers * mine // 128, 128)
    blocks = lax.all_to_all(blocks, "az", split_axis=0, concat_axis=0, tiled=True).sum(axis=0)
    return lax.all_to_all(blocks, "ax", split_axis=0, concat_axis=0, tiled=True)


def on_device(conserved, panel_cells, panel_counts, time_bins, amplitudes):
    fields, planes, sector, radial = conserved.shape
    observers = time_bins.shape[1]
    n_ax, n_az = lax.axis_size("ax"), lax.axis_size("az")
    length = sector * n_az
    up = [(i, i + 1) for i in range(n_ax - 1)]
    down = [(j, i) for i, j in up]
    az = lax.axis_index("az").astype(jnp.int32).reshape(1)
    table = basis_table(length)
    table = jnp.asarray(np.concatenate([table[-ROWS:], table, table[:ROWS]], axis=0))
    basis = lax.dynamic_slice_in_dim(table, az[0] * sector, sector + 2 * ROWS, axis=0)
    basis = jnp.concatenate([basis, jnp.asarray(mode_weights(length))], axis=0)

    pair = [(i, i ^ 1) for i in range(n_az)]
    send_up, send_down, early = edge_terms(conserved, az)
    early = lax.ppermute(early, "az", pair)
    low = lax.ppermute(send_up, "ax", up)
    high = lax.ppermute(send_down, "ax", down)

    partial = panel_sums(conserved, panel_cells, panel_counts, time_bins, amplitudes, early)
    sums = exchanged_sums(partial, observers)

    message, later = inner_terms(conserved, az, basis, length, partial)
    edge = (planes + 4) * CYCLES
    mine = jnp.concatenate([message + lax.ppermute(message, "az", pair), later], axis=1)
    pairs = [(i, (i + 1) % n_az) for i in range(1, n_az, 2)]
    theirs = lax.ppermute(mine, "az", pairs + [(j, i) for i, j in pairs])
    late = theirs
    shift = 4
    while shift < n_az:
        mine = mine + theirs
        theirs = lax.ppermute(mine, "az", [(i, (i + shift) % n_az) for i in range(n_az)])
        shift *= 2
    outside = mine[:, planes * CYCLES : edge] + theirs[:, planes * CYCLES : edge]
    spec_low = lax.ppermute(outside[:, : 2 * CYCLES], "ax", up)
    spec_high = lax.ppermute(outside[:, 2 * CYCLES :], "ax", down)

    section = local_section(pltpu.with_memory_space_constraint(conserved, pltpu.HBM), az, mine, theirs, early, late, basis, length)
    section, signal = add_edges(
        section, low, high, spec_low, spec_high, basis, sums, observers
    )
    return (section, signal.T)


def solution(mesh):
    placed = (
        P(None, "ax", "az", None),
        P(("ax", "az")),
        P(("ax", "az")),
        P(("ax", "az"), None),
        P(("ax", "az"), None),
    )
    return jax.shard_map(
        on_device,
        mesh=mesh,
        in_specs=placed,
        out_specs=(P(None, "ax", "az", None), P(None, ("ax", "az"))),
        check_vma=False,
    )
```

```python
import functools
import math

import jax
import jax.numpy as jnp
import numpy as np
from jax import lax
from jax.experimental import pallas as pl
from jax.experimental.pallas import tpu as pltpu
from jax.sharding import PartitionSpec as P

CYCLES = 8
BINS = 1024
LOW_BINS = 32
FIELDS = 5
MODES = 8 * CYCLES
COEFS = 2 * MODES
ROWS = 8

gas_factor = 0.4
time_step = 0.02
ref_pressure = 0.95
VMEM_BYTES = 48 * 1024 * 1024

HIGHEST = lax.Precision.HIGHEST


def params(**more):
    return pltpu.CompilerParams(vmem_limit_bytes=VMEM_BYTES, **more)


def cost(flops, touched):
    return pl.CostEstimate(flops=flops, bytes_accessed=touched, transcendentals=0)


def basis_table(length):
    phase = (np.arange(length)[:, None] * np.arange(MODES)[None, :] % length) * (
        2.0 * math.pi / length
    )
    return np.concatenate([np.cos(phase), np.sin(phase)], axis=1).astype(np.float32)


def mode_weights(length):
    modes = np.arange(MODES).astype(np.float64)
    cutoff = 4.0 * (np.arange(CYCLES) + 1.0)
    weight = np.exp(-((modes[None, :] / cutoff[:, None]) ** 8))
    weight = weight * np.where(modes == 0, 1.0, 2.0)[None, :] / length
    return np.concatenate([weight, weight], axis=1).astype(np.float32)


def primitives(q):
    inverse = 1.0 / q[0]
    u, v, w = q[1] * inverse, q[2] * inverse, q[3] * inverse
    p = gas_factor * (q[4] - 0.5 * (q[1] * u + q[2] * v + q[3] * w))
    return u, v, w, p


def carried(q, p, speed, heading):
    flux = [q[0] * speed, q[1] * speed, q[2] * speed, q[3] * speed, (q[4] + p) * speed]
    flux[heading] = flux[heading] + p
    return flux


def swirl_rows(ref, low):
    for k in range(ref.shape[1]):
        q = [ref[f, k] for f in range(FIELDS)]
        _, _, w, p = primitives(q)
        flux = carried(q, p, w, 3)
        yield k, [jnp.where(low, f[:2], f[ROWS - 2 :]) for f in flux]


def edge_kernel(az_ref, q_ref, rim_ref, up_ref, down_ref, early_ref):
    sector, radial = q_ref.shape[2:]
    groups = radial // CYCLES - 1
    tail = sector * CYCLES // radial
    scale = time_step / 12.0
    lane = lax.broadcasted_iota(jnp.int32, (1, radial), 1)

    def go(up, send):
        def terms(start):
            rows = pl.ds(start, tail)
            flux = []
            for plane in range(2):
                q = [q_ref[f, plane, rows, :] for f in range(FIELDS)]
                u, _, _, p = primitives(q)
                flux.append(carried(q, p, u, 1))
            near, far = (flux[1], flux[0]) if up else (flux[0], flux[1])
            whole, part = [], []
            for f in range(FIELDS):
                wide = scale * (8.0 * near[f] - far[f])
                narrow = scale * near[f]
                whole.append(wide if up else -wide)
                part.append(-narrow if up else narrow)
            return (whole, part) if up else (part, whole)

        last = terms(groups * tail)
        for g in range(groups):
            slots = terms(g * tail)
            shift = radial - CYCLES * (g + 1)
            for s in range(2):
                for f in range(FIELDS):
                    moved = pltpu.roll(last[s][f], shift, 1)
                    send[f, s, pl.ds(g * tail, tail), :] = jnp.where(
                        lane < CYCLES, moved, slots[s][f]
                    )

    @pl.when(pl.program_id(0) == 0)
    def _():
        go(True, up_ref)
        for k, flux in swirl_rows(rim_ref, lax.rem(az_ref[0], 2) == 1):
            for f in range(FIELDS):
                early_ref[f, 2 * k : 2 * k + 2, :] = flux[f]

    pl.when(pl.program_id(0) == 1)(lambda: go(False, down_ref))


def edge_terms(conserved, az):
    fields, planes, sector, radial = conserved.shape
    out = jax.ShapeDtypeStruct((fields, 2, sector - sector * CYCLES // radial, radial), jnp.float32)
    early = jax.ShapeDtypeStruct((fields, 2 * planes, radial), jnp.float32)
    last = sector // ROWS - 1
    wide = pl.BlockSpec(out.shape, lambda i, *_: (0, 0, 0, 0))
    return pl.pallas_call(
        edge_kernel,
        grid_spec=pltpu.PrefetchScalarGridSpec(
            num_scalar_prefetch=1,
            grid=(2,),
            in_specs=[
                pl.BlockSpec(
                    (fields, 2, sector, radial), lambda i, az: (0, (planes // 2 - 1) * (1 - i), 0, 0)
                ),
                pl.BlockSpec(
                    (fields, planes, ROWS, radial),
                    lambda i, az: (0, 0, last * (1 - lax.rem(az[0], 2)), 0),
                ),
            ],
            out_specs=[wide, wide, pl.BlockSpec(early.shape, lambda i, *_: (0, 0, 0))],
        ),
        out_shape=[out, out, early],
        compiler_params=params(),
        cost_estimate=cost(400 * sector * radial, 4 * 8 * fields * sector * radial),
        name="edge_terms",
    )(az, conserved, conserved)


def inner_kernel(dtheta, *refs):
    az_ref, q_ref, rim_ref, basis_ref, _ = refs[:5]
    message_ref, later_ref, local, swirl, outside = refs[5:]
    fields, planes, sector, radial = q_ref.shape
    group = 2 * CYCLES
    scale = time_step / 12.0
    chunk = min(sector, 32 * ROWS)
    lane = lax.broadcasted_iota(jnp.int32, (1, radial), 1)
    cycle = lane & (group - 1)
    plane = lane // group
    radius = cycle.astype(jnp.float32) + 0.5
    inverse = 1.0 / radius
    near = 8.0 * scale * inverse
    far = scale * inverse
    near_down = jnp.where(cycle >= 1, near, 0.0)
    far_down = jnp.where(cycle >= 2, far, 0.0)
    source = time_step * inverse
    turn = scale * inverse / dtheta

    def split(there, value):
        return jnp.where(there, value, 0.0), jnp.where(there, 0.0, value)

    behind, behind_out = split(plane >= 1, 8.0 * scale)
    behind2, behind2_out = split(plane >= 2, scale)
    ahead, ahead_out = split(plane < planes - 1, 8.0 * scale)
    ahead2, ahead2_out = split(plane < planes - 2, scale)

    zeros = jnp.zeros((FIELDS, 2 * ROWS, radial), jnp.float32)
    swirl[:, : 2 * ROWS, :] = zeros
    swirl[:, 2 * ROWS + sector :, :] = zeros
    local[:, :ROWS, :] = zeros[:, :ROWS]
    local[:, ROWS + sector :, :] = zeros[:, :ROWS]

    def body(i, _):
        start = pl.multiple_of(i * chunk, chunk)
        rows = pl.ds(start, chunk)
        q = []
        for f in range(FIELDS):
            packed = q_ref[f, 0, rows, :]
            for k in range(1, planes):
                moved = pltpu.roll(q_ref[f, k, rows, :], group * k, 1)
                packed = jnp.where(plane == k, moved, packed)
            q.append(packed)
        u, v, w, p = primitives(q)
        along = carried(q, p, u, 1)
        around = carried(q, p, w, 3)
        outward = carried(q, p, v, 2)
        for f in range(FIELDS):
            swirl[f, pl.ds(start + 2 * ROWS, chunk), :] = around[f]
            g = outward[f] * radius
            value = q[f] - near * pltpu.roll(g, radial - 1, 1)
            value = value + near_down * pltpu.roll(g, 1, 1)
            value = value + far * pltpu.roll(g, radial - 2, 1)
            value = value - far_down * pltpu.roll(g, 2, 1)
            if f == 2:
                value = value + source * (p + q[3] * w)
            if f == 3:
                value = value - source * (q[2] * w)
            up1 = pltpu.roll(along[f], group, 1)
            up2 = pltpu.roll(along[f], 2 * group, 1)
            down1 = pltpu.roll(along[f], radial - group, 1)
            down2 = pltpu.roll(along[f], radial - 2 * group, 1)
            value = value + behind * up1 - behind2 * up2 - ahead * down1 + ahead2 * down2
            local[f, pl.ds(start + ROWS, chunk), :] = value
            outside[f, rows, :] = (
                behind_out * up1 - behind2_out * up2 - ahead_out * down1 + ahead2_out * down2
            )
        return 0

    lax.fori_loop(0, sector // chunk, body, 0)

    def rest(start, size):
        for f in range(FIELDS):
            at = lambda k: swirl[f, pl.ds(start + (ROWS + k), size), :]
            around = 8.0 * (at(1) - at(-1)) - (at(2) - at(-2))
            rows = pl.ds(start, size)
            local[f, rows, :] = local[f, rows, :] - turn * around

    rest(0, ROWS)
    rest(ROWS + sector, ROWS)

    def body2(i, _):
        rest(pl.multiple_of(i * chunk, chunk) + ROWS, chunk)
        return 0

    lax.fori_loop(0, sector // chunk, body2, 0)

    def transform(rows, table):
        return lax.dot_general(
            rows, table, (((0,), (0,)), ((), ())),
            precision=HIGHEST, preferred_element_type=jnp.float32,
        )

    for f in range(FIELDS):
        own = transform(local[f], basis_ref[: sector + 2 * ROWS, :])
        for k in range(planes):
            message_ref[f, k * CYCLES : (k + 1) * CYCLES, :] = own[k * group : k * group + CYCLES]
        other = transform(outside[f], basis_ref[ROWS : ROWS + sector, :])
        for s, k in enumerate((0, 1, planes - 2, planes - 1)):
            at = (planes + s) * CYCLES
            message_ref[f, at : at + CYCLES, :] = other[k * group : k * group + CYCLES]

    for k, flux in swirl_rows(rim_ref, lax.rem(az_ref[0], 2) == 0):
        for f in range(FIELDS):
            later_ref[f, 2 * k : 2 * k + 2, :] = flux[f]


def inner_terms(conserved, az, basis, length, after):
    fields, planes, sector, radial = conserved.shape
    message = (fields, (planes + 4) * CYCLES, COEFS)
    later = (fields, 2 * planes, radial)
    full = lambda *shape: pl.BlockSpec(shape, lambda i, *_: (0,) * len(shape))
    tiles = sector // ROWS
    return pl.pallas_call(
        functools.partial(inner_kernel, 2.0 * math.pi / length),
        grid_spec=pltpu.PrefetchScalarGridSpec(
            num_scalar_prefetch=1,
            grid=(1,),
            in_specs=[
                full(*conserved.shape),
                pl.BlockSpec(
                    (fields, planes, ROWS, radial),
                    lambda i, az: (0, 0, (tiles - 1) * lax.rem(az[0], 2), 0),
                ),
                full(*basis.shape),
                pl.BlockSpec(memory_space=pl.ANY),
            ],
            out_specs=[full(*message), full(*later)],
            scratch_shapes=[
                pltpu.VMEM((fields, sector + 2 * ROWS, radial), jnp.float32),
                pltpu.VMEM((fields, sector + 4 * ROWS, radial), jnp.float32),
                pltpu.VMEM((fields, sector, radial), jnp.float32),
            ],
        ),
        out_shape=[
            jax.ShapeDtypeStruct(message, jnp.float32),
            jax.ShapeDtypeStruct(later, jnp.float32),
        ],
        compiler_params=params(),
        cost_estimate=cost(60 * sector * radial * COEFS, 4 * fields * planes * sector * radial),
        name="inner_terms",
    )(az, conserved, conserved, basis, after)


def panel_kernel(n_ax, n_az, cells_ref, count_ref, row_ref, q_ref, bins_ref, amp_ref, _, out_ref, held):
    slots = row_ref.shape[1]
    radial = q_ref.shape[2]
    observers = bins_ref.shape[0]
    count = count_ref[0]
    width = 8

    def fetch(i, _):
        for k in range(width):
            s = i * width + k
            at = cells_ref[s] // radial
            held[:, pl.ds(s, 1), :] = q_ref[:, pl.ds(at, 1), :]
        return 0

    lax.fori_loop(0, (count + width - 1) // width, fetch, 0)
    q = [held[f] for f in range(FIELDS)]
    p = gas_factor * (q[4] - 0.5 * (q[1] * q[1] + q[2] * q[2] + q[3] * q[3]) / q[0])
    turned = jnp.transpose(p)
    which = lax.broadcasted_iota(jnp.int32, (radial, slots), 0)
    here = which == (row_ref[...] & (radial - 1))
    sampled = jnp.sum(jnp.where(here, turned, 0.0), axis=0, keepdims=True) - ref_pressure
    slot = lax.broadcasted_iota(jnp.int32, (1, slots), 1)
    sampled = jnp.where(slot < count, sampled, 0.0)

    contrib = sampled * amp_ref[...]
    first = contrib.astype(jnp.bfloat16).astype(jnp.float32)
    second = contrib - first
    bins = bins_ref[...]
    low = bins & (LOW_BINS - 1)
    high = bins // LOW_BINS
    if n_ax * n_az * LOW_BINS == BINS:
        high = (high % n_az) * n_ax + high // n_az
    each = 128 // LOW_BINS
    high_count = BINS // LOW_BINS
    low_iota = lax.broadcasted_iota(jnp.int32, (LOW_BINS, slots), 0)
    high_iota = lax.broadcasted_iota(jnp.int32, (high_count, slots), 0)
    lane = lax.broadcasted_iota(jnp.int32, (high_count, 128), 1)
    for g in range(observers // each):
        left, right = [], []
        for k in range(each):
            o = g * each + k
            hit = high_iota == high[o : o + 1]
            left.append(jnp.where(hit, first[o : o + 1], 0.0).astype(jnp.bfloat16))
            left.append(jnp.where(hit, second[o : o + 1], 0.0).astype(jnp.bfloat16))
            same = low_iota == low[o : o + 1]
            right.append(jnp.where(same, 1.0, 0.0).astype(jnp.bfloat16))
        sums = lax.dot_general(
            jnp.concatenate(left, axis=0),
            jnp.concatenate(right, axis=0),
            (((1,), (1,)), ((), ())),
            preferred_element_type=jnp.float32,
        )
        total = jnp.zeros((high_count, 128), jnp.float32)
        for k in range(each):
            at = 2 * k * high_count
            both = sums[at : at + high_count] + sums[at + high_count : at + 2 * high_count]
            total = jnp.where(lane // LOW_BINS == k, both, total)
        out_ref[:, g, :] = total


def panel_sums(conserved, cells, counts, bins, amplitudes, after):
    fields, planes, sector, radial = conserved.shape
    slots, observers = bins.shape
    flat = conserved.reshape(fields, planes * sector, radial)
    high_count = BINS // LOW_BINS
    full = lambda *shape: pl.BlockSpec(shape, lambda i, *_: (0,) * len(shape))
    return pl.pallas_call(
        functools.partial(panel_kernel, lax.axis_size("ax"), lax.axis_size("az")),
        grid_spec=pltpu.PrefetchScalarGridSpec(
            num_scalar_prefetch=2,
            grid=(1,),
            in_specs=[
                full(1, slots),
                full(fields, planes * sector, radial),
                full(observers, slots),
                full(observers, slots),
                pl.BlockSpec(memory_space=pl.ANY),
            ],
            out_specs=full(high_count, observers * LOW_BINS // 128, 128),
            scratch_shapes=[pltpu.VMEM((fields, slots, radial), jnp.float32)],
        ),
        out_shape=jax.ShapeDtypeStruct(
            (high_count, observers * LOW_BINS // 128, 128), jnp.float32
        ),
        compiler_params=params(),
        cost_estimate=cost(8 * observers * slots * BINS, 4 * fields * planes * sector * radial),
        name="panel_sums",
    )(cells, counts, cells.reshape(1, slots), flat, bins.T, amplitudes.T, after)


def section_kernel(dtheta, *refs):
    az_ref, q_ref, mine_ref, theirs_ref, early_ref, late_ref, basis_ref = refs[:7]
    out_ref, axial, swirl, local, spec, smooth = refs[7:]
    fields, _, sector, radial = q_ref.shape
    step = pl.program_id(0)
    planes = pl.num_programs(0) - 2
    scale = time_step / 12.0
    chunk = min(sector, 32 * ROWS)
    lane = lax.broadcasted_iota(jnp.int32, (1, radial), 1)
    radius = lane.astype(jnp.float32) + 0.5
    inverse = 1.0 / radius
    near = 8.0 * scale * inverse
    far = scale * inverse
    near_up = jnp.where(lane < radial - 1, near, 0.0)
    near_down = jnp.where(lane >= 1, near, 0.0)
    far_up = jnp.where(lane < radial - 2, far, 0.0)
    far_down = jnp.where(lane >= 2, far, 0.0)
    source = time_step * inverse
    odd = lax.rem(az_ref[0], 2) == 1
    static_planes = axial.shape[0] - 4

    @pl.when(step == 0)
    def _():
        axial[0:2] = jnp.zeros((2,) + axial.shape[1:], jnp.float32)
        axial[planes + 2 : planes + 4] = jnp.zeros((2,) + axial.shape[1:], jnp.float32)
        spec[...] = jnp.zeros_like(spec)
        for k in range(static_planes):
            for f in range(FIELDS):
                rows = slice(k * CYCLES, (k + 1) * CYCLES)
                value = mine_ref[f, rows, :] + theirs_ref[f, rows, :]
                spec[k, f * CYCLES : (f + 1) * CYCLES, :] = value * basis_ref[sector + 2 * ROWS :, :]

    @pl.when(step < planes)
    def _():
        slot = lax.rem(step, 3)
        for f in range(FIELDS):
            early = early_ref[f, pl.ds(2 * step, 2), :]
            late = late_ref[f, pl.ds(2 * step, 2), :]
            swirl[slot, f, ROWS - 2 : ROWS, :] = jnp.where(odd, early, late)
            swirl[slot, f, ROWS + sector : ROWS + sector + 2, :] = jnp.where(odd, late, early)

        def body(i, _):
            start = pl.multiple_of(i * chunk, chunk)
            rows = pl.ds(start, chunk)
            q = [q_ref[f, 0, rows, :] for f in range(FIELDS)]
            u, v, w, p = primitives(q)
            along = carried(q, p, u, 1)
            around = carried(q, p, w, 3)
            outward = carried(q, p, v, 2)
            for f in range(FIELDS):
                axial[step + 2, f, rows, :] = along[f]
                swirl[slot, f, pl.ds(start + ROWS, chunk), :] = around[f]
                g = outward[f] * radius
                value = q[f] - near_up * pltpu.roll(g, radial - 1, 1)
                value = value + near_down * pltpu.roll(g, 1, 1)
                value = value + far_up * pltpu.roll(g, radial - 2, 1)
                value = value - far_down * pltpu.roll(g, 2, 1)
                if f == 2:
                    value = value + source * (p + q[3] * w)
                if f == 3:
                    value = value - source * (q[2] * w)
                local[slot, f, rows, :] = value
            return 0

        lax.fori_loop(0, sector // chunk, body, 0)

    @pl.when(step >= 2)
    def _():
        plane = step - 2
        slot = lax.rem(plane, 3)
        turn = scale * inverse / dtheta
        smooth[...] = lax.dot_general(
            basis_ref[ROWS : ROWS + sector, :], spec[plane], (((1,), (1,)), ((), ())),
            precision=HIGHEST, preferred_element_type=jnp.float32,
        )

        def body(i, _):
            start = pl.multiple_of(i * chunk, chunk)
            rows = pl.ds(start, chunk)
            for f in range(FIELDS):
                at = lambda k: swirl[slot, f, pl.ds(start + (ROWS + k), chunk), :]
                of = lambda k: axial[plane + 2 + k, f, rows, :]
                around = 8.0 * (at(1) - at(-1)) - (at(2) - at(-2))
                along = 8.0 * (of(1) - of(-1)) - (of(2) - of(-2))
                value = local[slot, f, rows, :] - turn * around - scale * along
                moved = smooth[rows, :]
                if f > 0:
                    moved = pltpu.roll(moved, radial - CYCLES * f, 1)
                out_ref[f, 0, rows, :] = jnp.where(lane < CYCLES, moved, value)
            return 0

        lax.fori_loop(0, sector // chunk, body, 0)


def local_section(conserved, az, mine, theirs, early, late, basis, length):
    fields, planes, sector, radial = conserved.shape
    two_back = lambda i: jnp.maximum(i - 2, 0)
    ring = (fields, 2 * planes, radial)
    last = late.shape[1] // ring[1] - 1
    full = lambda a: pl.BlockSpec(a.shape, lambda i, *_: (0,) * a.ndim)
    plane = (fields, 1, sector, radial)
    return pl.pallas_call(
        functools.partial(section_kernel, 2.0 * math.pi / length),
        grid_spec=pltpu.PrefetchScalarGridSpec(
            num_scalar_prefetch=1,
            grid=(planes + 2,),
            in_specs=[
                pl.BlockSpec(plane, lambda i, *_: (0, jnp.minimum(i, planes - 1), 0, 0)),
                full(mine),
                full(theirs),
                full(early),
                pl.BlockSpec(ring, lambda i, *_: (0, last, 0)),
                full(basis),
            ],
            out_specs=pl.BlockSpec(plane, lambda i, *_: (0, two_back(i), 0, 0)),
            scratch_shapes=[
                pltpu.VMEM((planes + 4, fields, sector, radial), jnp.float32),
                pltpu.VMEM((3, fields, sector + 2 * ROWS, radial), jnp.float32),
                pltpu.VMEM((3, fields, sector, radial), jnp.float32),
                pltpu.VMEM((planes, radial, COEFS), jnp.float32),
                pltpu.VMEM((sector, radial), jnp.float32),
            ],
        ),
        out_shape=jax.ShapeDtypeStruct(conserved.shape, jnp.float32),
        compiler_params=params(),
        cost_estimate=cost(
            600 * planes * sector * radial, 10 * 4 * fields * planes * sector * radial
        ),
        name="local_section",
    )(az, conserved, mine, theirs, early, late, basis)


def add_kernel(part_ref, low_ref, high_ref, spec_low, spec_high, basis_ref, sums_ref, *outs):
    out_ref, signal_ref, padded, turned = outs
    step = pl.program_id(0)
    fields, _, sector, radial = part_ref.shape
    groups = radial // CYCLES - 1
    tail = sector // (groups + 1)
    main = groups * tail
    lane = lax.broadcasted_iota(jnp.int32, (1, radial), 1)
    wide = lane >= CYCLES

    @pl.when(step == 0)
    def _():
        padded[...] = jnp.zeros_like(padded)
        observers, _ = turned.shape
        bins = signal_ref.shape[0]
        total = jnp.sum(sums_ref[...], axis=0)
        for o in range(observers):
            row, at = o * bins // 128, o * bins % 128
            piece = total[row : row + 1]
            turned[o : o + 1, :] = pltpu.roll(piece, 128 - at, 1) if at else piece
        signal_ref[...] = jnp.transpose(turned[...])[:bins]

    weight = basis_ref[sector + 2 * ROWS :, :]

    def go(ref, spec_ref, slot):
        for f in range(fields):
            rows = slice(slot * CYCLES, (slot + 1) * CYCLES)
            padded[f * CYCLES : (f + 1) * CYCLES, :] = spec_ref[f, rows, :] * weight
        smooth = lax.dot_general(
            basis_ref[ROWS : ROWS + sector, :], padded[...], (((1,), (1,)), ((), ())),
            precision=HIGHEST, preferred_element_type=jnp.float32,
        )
        for f in range(fields):
            inner = smooth if f == 0 else pltpu.roll(smooth, radial - CYCLES * f, 1)
            out_ref[f, 0, :main, :] = part_ref[f, 0, :main, :] + jnp.where(
                wide, ref[f, 0], inner[:main]
            )
            rest = inner[main:]
            for g in range(groups):
                moved = pltpu.roll(ref[f, 0, g * tail : (g + 1) * tail, :], CYCLES * (g + 1), 1)
                rest = jnp.where(lane // CYCLES == g + 1, moved, rest)
            out_ref[f, 0, main:, :] = part_ref[f, 0, main:, :] + rest

    for k in range(2):
        pl.when(step == k)(lambda k=k: go(low_ref, spec_low, k))
        pl.when(step == 2 + k)(lambda k=k: go(high_ref, spec_high, k))


def add_edges(section, low, high, spec_low, spec_high, basis, sums, observers):
    fields, planes, sector, radial = section.shape
    main = low.shape[2]
    bins = sums.shape[1] * sums.shape[2] // observers
    full = lambda a: pl.BlockSpec(a.shape, lambda i, *_: (0,) * a.ndim)
    plane = pl.BlockSpec(
        (fields, 1, sector, radial), lambda i, *_: (0, jnp.where(i < 2, i, planes - 4 + i), 0, 0)
    )
    return pl.pallas_call(
        add_kernel,
        grid_spec=pltpu.PrefetchScalarGridSpec(
            num_scalar_prefetch=0,
            grid=(4,),
            in_specs=[
                plane,
                pl.BlockSpec((fields, 1, main, radial), lambda i, *_: (0, jnp.minimum(i, 1), 0, 0)),
                pl.BlockSpec((fields, 1, main, radial), lambda i, *_: (0, jnp.maximum(i - 2, 0), 0, 0)),
                full(spec_low),
                full(spec_high),
                full(basis),
                full(sums),
            ],
            out_specs=[plane, pl.BlockSpec((bins, observers), lambda i, *_: (0, 0))],
            scratch_shapes=[
                pltpu.VMEM((radial, COEFS), jnp.float32),
                pltpu.VMEM((observers, 128), jnp.float32),
            ],
        ),
        out_shape=[
            jax.ShapeDtypeStruct(section.shape, jnp.float32),
            jax.ShapeDtypeStruct((bins, observers), jnp.float32),
        ],
        input_output_aliases={0: 0},
        compiler_params=params(),
        cost_estimate=cost(8 * fields * sector * radial, 4 * 12 * fields * sector * radial),
        name="add_edges",
    )(section, low, high, spec_low, spec_high, basis, sums)


def exchanged_sums(partial, observers):
    n_ax, n_az = lax.axis_size("ax"), lax.axis_size("az")
    mine = BINS // (n_ax * n_az)
    if mine != LOW_BINS:
        partial = partial.reshape(-1, observers, LOW_BINS).transpose(0, 2, 1)
        partial = partial.reshape(n_ax, n_az, mine, observers).transpose(1, 0, 3, 2)
    blocks = partial.reshape(n_az, n_ax, observers * mine // 128, 128)
    blocks = lax.all_to_all(blocks, "az", split_axis=0, concat_axis=0, tiled=True).sum(axis=0)
    return lax.all_to_all(blocks, "ax", split_axis=0, concat_axis=0, tiled=True)


def on_device(conserved, panel_cells, panel_counts, time_bins, amplitudes):
    fields, planes, sector, radial = conserved.shape
    observers = time_bins.shape[1]
    n_ax, n_az = lax.axis_size("ax"), lax.axis_size("az")
    length = sector * n_az
    up = [(i, i + 1) for i in range(n_ax - 1)]
    down = [(j, i) for i, j in up]
    az = lax.axis_index("az").astype(jnp.int32).reshape(1)
    table = basis_table(length)
    table = jnp.asarray(np.concatenate([table[-ROWS:], table, table[:ROWS]], axis=0))
    basis = lax.dynamic_slice_in_dim(table, az[0] * sector, sector + 2 * ROWS, axis=0)
    basis = jnp.concatenate([basis, jnp.asarray(mode_weights(length))], axis=0)

    pair = [(i, i ^ 1) for i in range(n_az)]
    send_up, send_down, early = edge_terms(conserved, az)
    early = lax.ppermute(early, "az", pair)
    low = lax.ppermute(send_up, "ax", up)
    high = lax.ppermute(send_down, "ax", down)

    message, later = inner_terms(conserved, az, basis, length, early)
    edge = (planes + 4) * CYCLES
    partial = panel_sums(conserved, panel_cells, panel_counts, time_bins, amplitudes, message)
    sums = exchanged_sums(partial, observers)

    mine = jnp.concatenate([message + lax.ppermute(message, "az", pair), later], axis=1)
    pairs = [(i, (i + 1) % n_az) for i in range(1, n_az, 2)]
    theirs = lax.ppermute(mine, "az", pairs + [(j, i) for i, j in pairs])
    late = theirs
    shift = 4
    while shift < n_az:
        mine = mine + theirs
        theirs = lax.ppermute(mine, "az", [(i, (i + shift) % n_az) for i in range(n_az)])
        shift *= 2
    outside = mine[:, planes * CYCLES : edge] + theirs[:, planes * CYCLES : edge]
    spec_low = lax.ppermute(outside[:, : 2 * CYCLES], "ax", up)
    spec_high = lax.ppermute(outside[:, 2 * CYCLES :], "ax", down)

    section = local_section(pltpu.with_memory_space_constraint(conserved, pltpu.HBM), az, mine, theirs, early, late, basis, length)
    section, signal = add_edges(
        section, low, high, spec_low, spec_high, basis, sums, observers
    )
    return (section, signal.T)


def solution(mesh):
    placed = (
        P(None, "ax", "az", None),
        P(("ax", "az")),
        P(("ax", "az")),
        P(("ax", "az"), None),
        P(("ax", "az"), None),
    )
    return jax.shard_map(
        on_device,
        mesh=mesh,
        in_specs=placed,
        out_specs=(P(None, "ax", "az", None), P(None, ("ax", "az"))),
        check_vma=False,
    )
```

```python
import functools
import math

import jax
import jax.numpy as jnp
import numpy as np
from jax import lax
from jax.experimental import pallas as pl
from jax.experimental.pallas import tpu as pltpu
from jax.sharding import PartitionSpec as P

CYCLES = 8
BINS = 1024
LOW_BINS = 32
FIELDS = 5
MODES = 8 * CYCLES
COEFS = 2 * MODES
ROWS = 8

gas_factor = 0.4
time_step = 0.02
ref_pressure = 0.95
VMEM_BYTES = 48 * 1024 * 1024

HIGHEST = lax.Precision.HIGHEST


def params(**more):
    return pltpu.CompilerParams(vmem_limit_bytes=VMEM_BYTES, **more)


def cost(flops, touched):
    return pl.CostEstimate(flops=flops, bytes_accessed=touched, transcendentals=0)


def basis_table(length):
    phase = (np.arange(length)[:, None] * np.arange(MODES)[None, :] % length) * (
        2.0 * math.pi / length
    )
    return np.concatenate([np.cos(phase), np.sin(phase)], axis=1).astype(np.float32)


def mode_weights(length):
    modes = np.arange(MODES).astype(np.float64)
    cutoff = 4.0 * (np.arange(CYCLES) + 1.0)
    weight = np.exp(-((modes[None, :] / cutoff[:, None]) ** 8))
    weight = weight * np.where(modes == 0, 1.0, 2.0)[None, :] / length
    return np.concatenate([weight, weight], axis=1).astype(np.float32)


def primitives(q):
    inverse = 1.0 / q[0]
    u, v, w = q[1] * inverse, q[2] * inverse, q[3] * inverse
    p = gas_factor * (q[4] - 0.5 * (q[1] * u + q[2] * v + q[3] * w))
    return u, v, w, p


def carried(q, p, speed, heading):
    flux = [q[0] * speed, q[1] * speed, q[2] * speed, q[3] * speed, (q[4] + p) * speed]
    flux[heading] = flux[heading] + p
    return flux


def swirl_rows(ref, low):
    for k in range(ref.shape[1]):
        q = [ref[f, k] for f in range(FIELDS)]
        _, _, w, p = primitives(q)
        flux = carried(q, p, w, 3)
        yield k, [jnp.where(low, f[:2], f[ROWS - 2 :]) for f in flux]


def edge_kernel(az_ref, top_ref, bottom_ref, rim_ref, up_ref, down_ref, early_ref):
    sector, radial = top_ref.shape[2:]
    groups = radial // CYCLES - 1
    tail = sector * CYCLES // radial
    scale = time_step / 12.0
    lane = lax.broadcasted_iota(jnp.int32, (1, radial), 1)

    def go(up, q_ref, send):
        def terms(start):
            rows = pl.ds(start, tail)
            flux = []
            for plane in range(2):
                q = [q_ref[f, plane, rows, :] for f in range(FIELDS)]
                u, _, _, p = primitives(q)
                flux.append(carried(q, p, u, 1))
            near, far = (flux[1], flux[0]) if up else (flux[0], flux[1])
            whole, part = [], []
            for f in range(FIELDS):
                wide = scale * (8.0 * near[f] - far[f])
                narrow = scale * near[f]
                whole.append(wide if up else -wide)
                part.append(-narrow if up else narrow)
            return (whole, part) if up else (part, whole)

        last = terms(groups * tail)
        for g in range(groups):
            slots = terms(g * tail)
            shift = radial - CYCLES * (g + 1)
            for s in range(2):
                for f in range(FIELDS):
                    moved = pltpu.roll(last[s][f], shift, 1)
                    send[f, s, pl.ds(g * tail, tail), :] = jnp.where(
                        lane < CYCLES, moved, slots[s][f]
                    )

    go(True, top_ref, up_ref)
    go(False, bottom_ref, down_ref)
    for k, flux in swirl_rows(rim_ref, lax.rem(az_ref[0], 2) == 1):
        for f in range(FIELDS):
            early_ref[f, 2 * k : 2 * k + 2, :] = flux[f]


def edge_terms(conserved, az):
    fields, planes, sector, radial = conserved.shape
    out = jax.ShapeDtypeStruct((fields, 2, sector - sector * CYCLES // radial, radial), jnp.float32)
    early = jax.ShapeDtypeStruct((fields, 2 * planes, radial), jnp.float32)
    last = sector // ROWS - 1
    wide = pl.BlockSpec(out.shape, lambda i, *_: (0, 0, 0, 0))
    return pl.pallas_call(
        edge_kernel,
        grid_spec=pltpu.PrefetchScalarGridSpec(
            num_scalar_prefetch=1,
            grid=(1,),
            in_specs=[
                pl.BlockSpec((fields, 2, sector, radial), lambda i, az: (0, planes // 2 - 1, 0, 0)),
                pl.BlockSpec((fields, 2, sector, radial), lambda i, az: (0, 0, 0, 0)),
                pl.BlockSpec(
                    (fields, planes, ROWS, radial),
                    lambda i, az: (0, 0, last * (1 - lax.rem(az[0], 2)), 0),
                ),
            ],
            out_specs=[wide, wide, pl.BlockSpec(early.shape, lambda i, *_: (0, 0, 0))],
        ),
        out_shape=[out, out, early],
        compiler_params=params(),
        cost_estimate=cost(400 * sector * radial, 4 * 8 * fields * sector * radial),
        name="edge_terms",
    )(az, conserved, conserved, conserved)


def inner_kernel(dtheta, *refs):
    az_ref, q_ref, rim_ref, basis_ref, _ = refs[:5]
    message_ref, later_ref, local, swirl, outside = refs[5:]
    fields, planes, sector, radial = q_ref.shape
    group = 2 * CYCLES
    scale = time_step / 12.0
    chunk = min(sector, 32 * ROWS)
    lane = lax.broadcasted_iota(jnp.int32, (1, radial), 1)
    cycle = lane & (group - 1)
    plane = lane // group
    radius = cycle.astype(jnp.float32) + 0.5
    inverse = 1.0 / radius
    near = 8.0 * scale * inverse
    far = scale * inverse
    near_down = jnp.where(cycle >= 1, near, 0.0)
    far_down = jnp.where(cycle >= 2, far, 0.0)
    source = time_step * inverse
    turn = scale * inverse / dtheta

    def split(there, value):
        return jnp.where(there, value, 0.0), jnp.where(there, 0.0, value)

    behind, behind_out = split(plane >= 1, 8.0 * scale)
    behind2, behind2_out = split(plane >= 2, scale)
    ahead, ahead_out = split(plane < planes - 1, 8.0 * scale)
    ahead2, ahead2_out = split(plane < planes - 2, scale)

    zeros = jnp.zeros((FIELDS, 2 * ROWS, radial), jnp.float32)
    swirl[:, : 2 * ROWS, :] = zeros
    swirl[:, 2 * ROWS + sector :, :] = zeros
    local[:, :ROWS, :] = zeros[:, :ROWS]
    local[:, ROWS + sector :, :] = zeros[:, :ROWS]

    def body(i, _):
        start = pl.multiple_of(i * chunk, chunk)
        rows = pl.ds(start, chunk)
        q = []
        for f in range(FIELDS):
            packed = q_ref[f, 0, rows, :]
            for k in range(1, planes):
                moved = pltpu.roll(q_ref[f, k, rows, :], group * k, 1)
                packed = jnp.where(plane == k, moved, packed)
            q.append(packed)
        u, v, w, p = primitives(q)
        along = carried(q, p, u, 1)
        around = carried(q, p, w, 3)
        outward = carried(q, p, v, 2)
        for f in range(FIELDS):
            swirl[f, pl.ds(start + 2 * ROWS, chunk), :] = around[f]
            g = outward[f] * radius
            value = q[f] - near * pltpu.roll(g, radial - 1, 1)
            value = value + near_down * pltpu.roll(g, 1, 1)
            value = value + far * pltpu.roll(g, radial - 2, 1)
            value = value - far_down * pltpu.roll(g, 2, 1)
            if f == 2:
                value = value + source * (p + q[3] * w)
            if f == 3:
                value = value - source * (q[2] * w)
            up1 = pltpu.roll(along[f], group, 1)
            up2 = pltpu.roll(along[f], 2 * group, 1)
            down1 = pltpu.roll(along[f], radial - group, 1)
            down2 = pltpu.roll(along[f], radial - 2 * group, 1)
            value = value + behind * up1 - behind2 * up2 - ahead * down1 + ahead2 * down2
            local[f, pl.ds(start + ROWS, chunk), :] = value
            outside[f, rows, :] = (
                behind_out * up1 - behind2_out * up2 - ahead_out * down1 + ahead2_out * down2
            )
        return 0

    lax.fori_loop(0, sector // chunk, body, 0)

    def rest(start, size):
        for f in range(FIELDS):
            at = lambda k: swirl[f, pl.ds(start + (ROWS + k), size), :]
            around = 8.0 * (at(1) - at(-1)) - (at(2) - at(-2))
            rows = pl.ds(start, size)
            local[f, rows, :] = local[f, rows, :] - turn * around

    rest(0, ROWS)
    rest(ROWS + sector, ROWS)

    def body2(i, _):
        rest(pl.multiple_of(i * chunk, chunk) + ROWS, chunk)
        return 0

    lax.fori_loop(0, sector // chunk, body2, 0)

    def transform(rows, table):
        return lax.dot_general(
            rows, table, (((0,), (0,)), ((), ())),
            precision=HIGHEST, preferred_element_type=jnp.float32,
        )

    for f in range(FIELDS):
        own = transform(local[f], basis_ref[: sector + 2 * ROWS, :])
        for k in range(planes):
            message_ref[f, k * CYCLES : (k + 1) * CYCLES, :] = own[k * group : k * group + CYCLES]
        other = transform(outside[f], basis_ref[ROWS : ROWS + sector, :])
        for s, k in enumerate((0, 1, planes - 2, planes - 1)):
            at = (planes + s) * CYCLES
            message_ref[f, at : at + CYCLES, :] = other[k * group : k * group + CYCLES]

    for k, flux in swirl_rows(rim_ref, lax.rem(az_ref[0], 2) == 0):
        for f in range(FIELDS):
            later_ref[f, 2 * k : 2 * k + 2, :] = flux[f]


def inner_terms(conserved, az, basis, length, after):
    fields, planes, sector, radial = conserved.shape
    message = (fields, (planes + 4) * CYCLES, COEFS)
    later = (fields, 2 * planes, radial)
    full = lambda *shape: pl.BlockSpec(shape, lambda i, *_: (0,) * len(shape))
    tiles = sector // ROWS
    return pl.pallas_call(
        functools.partial(inner_kernel, 2.0 * math.pi / length),
        grid_spec=pltpu.PrefetchScalarGridSpec(
            num_scalar_prefetch=1,
            grid=(1,),
            in_specs=[
                full(*conserved.shape),
                pl.BlockSpec(
                    (fields, planes, ROWS, radial),
                    lambda i, az: (0, 0, (tiles - 1) * lax.rem(az[0], 2), 0),
                ),
                full(*basis.shape),
                pl.BlockSpec(memory_space=pl.ANY),
            ],
            out_specs=[full(*message), full(*later)],
            scratch_shapes=[
                pltpu.VMEM((fields, sector + 2 * ROWS, radial), jnp.float32),
                pltpu.VMEM((fields, sector + 4 * ROWS, radial), jnp.float32),
                pltpu.VMEM((fields, sector, radial), jnp.float32),
            ],
        ),
        out_shape=[
            jax.ShapeDtypeStruct(message, jnp.float32),
            jax.ShapeDtypeStruct(later, jnp.float32),
        ],
        compiler_params=params(),
        cost_estimate=cost(60 * sector * radial * COEFS, 4 * fields * planes * sector * radial),
        name="inner_terms",
    )(az, conserved, conserved, basis, after)


def panel_kernel(n_ax, n_az, cells_ref, count_ref, row_ref, q_ref, bins_ref, amp_ref, _, out_ref, held):
    slots = row_ref.shape[1]
    radial = q_ref.shape[2]
    observers = bins_ref.shape[0]
    count = count_ref[0]
    width = 8

    def fetch(i, _):
        for k in range(width):
            s = i * width + k
            at = cells_ref[s] // radial
            held[:, pl.ds(s, 1), :] = q_ref[:, pl.ds(at, 1), :]
        return 0

    lax.fori_loop(0, (count + width - 1) // width, fetch, 0)
    q = [held[f] for f in range(FIELDS)]
    p = gas_factor * (q[4] - 0.5 * (q[1] * q[1] + q[2] * q[2] + q[3] * q[3]) / q[0])
    turned = jnp.transpose(p)
    which = lax.broadcasted_iota(jnp.int32, (radial, slots), 0)
    here = which == (row_ref[...] & (radial - 1))
    sampled = jnp.sum(jnp.where(here, turned, 0.0), axis=0, keepdims=True) - ref_pressure
    slot = lax.broadcasted_iota(jnp.int32, (1, slots), 1)
    sampled = jnp.where(slot < count, sampled, 0.0)

    contrib = sampled * amp_ref[...]
    first = contrib.astype(jnp.bfloat16).astype(jnp.float32)
    second = contrib - first
    bins = bins_ref[...]
    low = bins & (LOW_BINS - 1)
    high = bins // LOW_BINS
    if n_ax * n_az * LOW_BINS == BINS:
        high = (high % n_az) * n_ax + high // n_az
    each = 128 // LOW_BINS
    high_count = BINS // LOW_BINS
    low_iota = lax.broadcasted_iota(jnp.int32, (LOW_BINS, slots), 0)
    high_iota = lax.broadcasted_iota(jnp.int32, (high_count, slots), 0)
    lane = lax.broadcasted_iota(jnp.int32, (high_count, 128), 1)
    for g in range(observers // each):
        left, right = [], []
        for k in range(each):
            o = g * each + k
            hit = high_iota == high[o : o + 1]
            left.append(jnp.where(hit, first[o : o + 1], 0.0).astype(jnp.bfloat16))
            left.append(jnp.where(hit, second[o : o + 1], 0.0).astype(jnp.bfloat16))
            same = low_iota == low[o : o + 1]
            right.append(jnp.where(same, 1.0, 0.0).astype(jnp.bfloat16))
        sums = lax.dot_general(
            jnp.concatenate(left, axis=0),
            jnp.concatenate(right, axis=0),
            (((1,), (1,)), ((), ())),
            preferred_element_type=jnp.float32,
        )
        total = jnp.zeros((high_count, 128), jnp.float32)
        for k in range(each):
            at = 2 * k * high_count
            both = sums[at : at + high_count] + sums[at + high_count : at + 2 * high_count]
            total = jnp.where(lane // LOW_BINS == k, both, total)
        out_ref[:, g, :] = total


def panel_sums(conserved, cells, counts, bins, amplitudes, after):
    fields, planes, sector, radial = conserved.shape
    slots, observers = bins.shape
    flat = conserved.reshape(fields, planes * sector, radial)
    high_count = BINS // LOW_BINS
    full = lambda *shape: pl.BlockSpec(shape, lambda i, *_: (0,) * len(shape))
    return pl.pallas_call(
        functools.partial(panel_kernel, lax.axis_size("ax"), lax.axis_size("az")),
        grid_spec=pltpu.PrefetchScalarGridSpec(
            num_scalar_prefetch=2,
            grid=(1,),
            in_specs=[
                full(1, slots),
                full(fields, planes * sector, radial),
                full(observers, slots),
                full(observers, slots),
                pl.BlockSpec(memory_space=pl.ANY),
            ],
            out_specs=full(high_count, observers * LOW_BINS // 128, 128),
            scratch_shapes=[pltpu.VMEM((fields, slots, radial), jnp.float32)],
        ),
        out_shape=jax.ShapeDtypeStruct(
            (high_count, observers * LOW_BINS // 128, 128), jnp.float32
        ),
        compiler_params=params(),
        cost_estimate=cost(8 * observers * slots * BINS, 4 * fields * planes * sector * radial),
        name="panel_sums",
    )(cells, counts, cells.reshape(1, slots), flat, bins.T, amplitudes.T, after)


def section_kernel(dtheta, *refs):
    az_ref, q_ref, mine_ref, theirs_ref, early_ref, late_ref, basis_ref = refs[:7]
    out_ref, axial, swirl, local, spec, smooth = refs[7:]
    fields, _, sector, radial = q_ref.shape
    step = pl.program_id(0)
    planes = pl.num_programs(0) - 2
    scale = time_step / 12.0
    chunk = min(sector, 32 * ROWS)
    lane = lax.broadcasted_iota(jnp.int32, (1, radial), 1)
    radius = lane.astype(jnp.float32) + 0.5
    inverse = 1.0 / radius
    near = 8.0 * scale * inverse
    far = scale * inverse
    near_up = jnp.where(lane < radial - 1, near, 0.0)
    near_down = jnp.where(lane >= 1, near, 0.0)
    far_up = jnp.where(lane < radial - 2, far, 0.0)
    far_down = jnp.where(lane >= 2, far, 0.0)
    source = time_step * inverse
    odd = lax.rem(az_ref[0], 2) == 1
    static_planes = axial.shape[0] - 4

    @pl.when(step == 0)
    def _():
        axial[0:2] = jnp.zeros((2,) + axial.shape[1:], jnp.float32)
        axial[planes + 2 : planes + 4] = jnp.zeros((2,) + axial.shape[1:], jnp.float32)
        spec[...] = jnp.zeros_like(spec)
        for k in range(static_planes):
            for f in range(FIELDS):
                rows = slice(k * CYCLES, (k + 1) * CYCLES)
                value = mine_ref[f, rows, :] + theirs_ref[f, rows, :]
                spec[k, f * CYCLES : (f + 1) * CYCLES, :] = value * basis_ref[sector + 2 * ROWS :, :]

    @pl.when(step < planes)
    def _():
        slot = lax.rem(step, 3)
        for f in range(FIELDS):
            early = early_ref[f, pl.ds(2 * step, 2), :]
            late = late_ref[f, pl.ds(2 * step, 2), :]
            swirl[slot, f, ROWS - 2 : ROWS, :] = jnp.where(odd, early, late)
            swirl[slot, f, ROWS + sector : ROWS + sector + 2, :] = jnp.where(odd, late, early)

        def body(i, _):
            start = pl.multiple_of(i * chunk, chunk)
            rows = pl.ds(start, chunk)
            q = [q_ref[f, 0, rows, :] for f in range(FIELDS)]
            u, v, w, p = primitives(q)
            along = carried(q, p, u, 1)
            around = carried(q, p, w, 3)
            outward = carried(q, p, v, 2)
            for f in range(FIELDS):
                axial[step + 2, f, rows, :] = along[f]
                swirl[slot, f, pl.ds(start + ROWS, chunk), :] = around[f]
                g = outward[f] * radius
                value = q[f] - near_up * pltpu.roll(g, radial - 1, 1)
                value = value + near_down * pltpu.roll(g, 1, 1)
                value = value + far_up * pltpu.roll(g, radial - 2, 1)
                value = value - far_down * pltpu.roll(g, 2, 1)
                if f == 2:
                    value = value + source * (p + q[3] * w)
                if f == 3:
                    value = value - source * (q[2] * w)
                local[slot, f, rows, :] = value
            return 0

        lax.fori_loop(0, sector // chunk, body, 0)

    @pl.when(step >= 2)
    def _():
        plane = step - 2
        slot = lax.rem(plane, 3)
        turn = scale * inverse / dtheta
        smooth[...] = lax.dot_general(
            basis_ref[ROWS : ROWS + sector, :], spec[plane], (((1,), (1,)), ((), ())),
            precision=HIGHEST, preferred_element_type=jnp.float32,
        )

        def body(i, _):
            start = pl.multiple_of(i * chunk, chunk)
            rows = pl.ds(start, chunk)
            for f in range(FIELDS):
                at = lambda k: swirl[slot, f, pl.ds(start + (ROWS + k), chunk), :]
                of = lambda k: axial[plane + 2 + k, f, rows, :]
                around = 8.0 * (at(1) - at(-1)) - (at(2) - at(-2))
                along = 8.0 * (of(1) - of(-1)) - (of(2) - of(-2))
                value = local[slot, f, rows, :] - turn * around - scale * along
                moved = smooth[rows, :]
                if f > 0:
                    moved = pltpu.roll(moved, radial - CYCLES * f, 1)
                out_ref[f, 0, rows, :] = jnp.where(lane < CYCLES, moved, value)
            return 0

        lax.fori_loop(0, sector // chunk, body, 0)


def local_section(conserved, az, mine, theirs, early, late, basis, length):
    fields, planes, sector, radial = conserved.shape
    two_back = lambda i: jnp.maximum(i - 2, 0)
    ring = (fields, 2 * planes, radial)
    last = late.shape[1] // ring[1] - 1
    full = lambda a: pl.BlockSpec(a.shape, lambda i, *_: (0,) * a.ndim)
    plane = (fields, 1, sector, radial)
    return pl.pallas_call(
        functools.partial(section_kernel, 2.0 * math.pi / length),
        grid_spec=pltpu.PrefetchScalarGridSpec(
            num_scalar_prefetch=1,
            grid=(planes + 2,),
            in_specs=[
                pl.BlockSpec(plane, lambda i, *_: (0, jnp.minimum(i, planes - 1), 0, 0)),
                full(mine),
                full(theirs),
                full(early),
                pl.BlockSpec(ring, lambda i, *_: (0, last, 0)),
                full(basis),
            ],
            out_specs=pl.BlockSpec(plane, lambda i, *_: (0, two_back(i), 0, 0)),
            scratch_shapes=[
                pltpu.VMEM((planes + 4, fields, sector, radial), jnp.float32),
                pltpu.VMEM((3, fields, sector + 2 * ROWS, radial), jnp.float32),
                pltpu.VMEM((3, fields, sector, radial), jnp.float32),
                pltpu.VMEM((planes, radial, COEFS), jnp.float32),
                pltpu.VMEM((sector, radial), jnp.float32),
            ],
        ),
        out_shape=jax.ShapeDtypeStruct(conserved.shape, jnp.float32),
        compiler_params=params(),
        cost_estimate=cost(
            600 * planes * sector * radial, 10 * 4 * fields * planes * sector * radial
        ),
        name="local_section",
    )(az, conserved, mine, theirs, early, late, basis)


def add_kernel(part_ref, low_ref, high_ref, spec_low, spec_high, basis_ref, sums_ref, *outs):
    out_ref, signal_ref, padded, turned = outs
    step = pl.program_id(0)
    fields, _, sector, radial = part_ref.shape
    groups = radial // CYCLES - 1
    tail = sector // (groups + 1)
    main = groups * tail
    lane = lax.broadcasted_iota(jnp.int32, (1, radial), 1)
    wide = lane >= CYCLES

    @pl.when(step == 0)
    def _():
        padded[...] = jnp.zeros_like(padded)
        observers, _ = turned.shape
        bins = signal_ref.shape[0]
        total = jnp.sum(sums_ref[...], axis=0)
        for o in range(observers):
            row, at = o * bins // 128, o * bins % 128
            piece = total[row : row + 1]
            turned[o : o + 1, :] = pltpu.roll(piece, 128 - at, 1) if at else piece
        signal_ref[...] = jnp.transpose(turned[...])[:bins]

    weight = basis_ref[sector + 2 * ROWS :, :]

    def go(ref, spec_ref, slot):
        for f in range(fields):
            rows = slice(slot * CYCLES, (slot + 1) * CYCLES)
            padded[f * CYCLES : (f + 1) * CYCLES, :] = spec_ref[f, rows, :] * weight
        smooth = lax.dot_general(
            basis_ref[ROWS : ROWS + sector, :], padded[...], (((1,), (1,)), ((), ())),
            precision=HIGHEST, preferred_element_type=jnp.float32,
        )
        for f in range(fields):
            inner = smooth if f == 0 else pltpu.roll(smooth, radial - CYCLES * f, 1)
            out_ref[f, slot, :main, :] = part_ref[f, slot, :main, :] + jnp.where(
                wide, ref[f, slot], inner[:main]
            )
            rest = inner[main:]
            for g in range(groups):
                moved = pltpu.roll(ref[f, slot, g * tail : (g + 1) * tail, :], CYCLES * (g + 1), 1)
                rest = jnp.where(lane // CYCLES == g + 1, moved, rest)
            out_ref[f, slot, main:, :] = part_ref[f, slot, main:, :] + rest

    for k in range(2):
        pl.when(step == 0)(lambda k=k: go(low_ref, spec_low, k))
        pl.when(step == 1)(lambda k=k: go(high_ref, spec_high, k))


def add_edges(section, low, high, spec_low, spec_high, basis, sums, observers):
    fields, planes, sector, radial = section.shape
    bins = sums.shape[1] * sums.shape[2] // observers
    full = lambda a: pl.BlockSpec(a.shape, lambda i, *_: (0,) * a.ndim)
    plane = pl.BlockSpec(
        (fields, 2, sector, radial), lambda i, *_: (0, (planes // 2 - 1) * i, 0, 0)
    )
    return pl.pallas_call(
        add_kernel,
        grid_spec=pltpu.PrefetchScalarGridSpec(
            num_scalar_prefetch=0,
            grid=(2,),
            in_specs=[
                plane,
                full(low),
                full(high),
                full(spec_low),
                full(spec_high),
                full(basis),
                full(sums),
            ],
            out_specs=[plane, pl.BlockSpec((bins, observers), lambda i, *_: (0, 0))],
            scratch_shapes=[
                pltpu.VMEM((radial, COEFS), jnp.float32),
                pltpu.VMEM((observers, 128), jnp.float32),
            ],
        ),
        out_shape=[
            jax.ShapeDtypeStruct(section.shape, jnp.float32),
            jax.ShapeDtypeStruct((bins, observers), jnp.float32),
        ],
        input_output_aliases={0: 0},
        compiler_params=params(),
        cost_estimate=cost(8 * fields * sector * radial, 4 * 12 * fields * sector * radial),
        name="add_edges",
    )(section, low, high, spec_low, spec_high, basis, sums)


def exchanged_sums(partial, observers):
    n_ax, n_az = lax.axis_size("ax"), lax.axis_size("az")
    mine = BINS // (n_ax * n_az)
    if mine != LOW_BINS:
        partial = partial.reshape(-1, observers, LOW_BINS).transpose(0, 2, 1)
        partial = partial.reshape(n_ax, n_az, mine, observers).transpose(1, 0, 3, 2)
    blocks = partial.reshape(n_az, n_ax, observers * mine // 128, 128)
    blocks = lax.all_to_all(blocks, "az", split_axis=0, concat_axis=0, tiled=True).sum(axis=0)
    return lax.all_to_all(blocks, "ax", split_axis=0, concat_axis=0, tiled=True)


def on_device(conserved, panel_cells, panel_counts, time_bins, amplitudes):
    fields, planes, sector, radial = conserved.shape
    observers = time_bins.shape[1]
    n_ax, n_az = lax.axis_size("ax"), lax.axis_size("az")
    length = sector * n_az
    up = [(i, i + 1) for i in range(n_ax - 1)]
    down = [(j, i) for i, j in up]
    az = lax.axis_index("az").astype(jnp.int32).reshape(1)
    table = basis_table(length)
    table = jnp.asarray(np.concatenate([table[-ROWS:], table, table[:ROWS]], axis=0))
    basis = lax.dynamic_slice_in_dim(table, az[0] * sector, sector + 2 * ROWS, axis=0)
    basis = jnp.concatenate([basis, jnp.asarray(mode_weights(length))], axis=0)

    pair = [(i, i ^ 1) for i in range(n_az)]
    send_up, send_down, early = edge_terms(conserved, az)
    early = lax.ppermute(early, "az", pair)
    low = lax.ppermute(send_up, "ax", up)
    high = lax.ppermute(send_down, "ax", down)

    message, later = inner_terms(conserved, az, basis, length, early)
    edge = (planes + 4) * CYCLES
    partial = panel_sums(conserved, panel_cells, panel_counts, time_bins, amplitudes, message)
    sums = exchanged_sums(partial, observers)

    mine = jnp.concatenate([message + lax.ppermute(message, "az", pair), later], axis=1)
    pairs = [(i, (i + 1) % n_az) for i in range(1, n_az, 2)]
    theirs = lax.ppermute(mine, "az", pairs + [(j, i) for i, j in pairs])
    late = theirs
    shift = 4
    while shift < n_az:
        mine = mine + theirs
        theirs = lax.ppermute(mine, "az", [(i, (i + shift) % n_az) for i in range(n_az)])
        shift *= 2
    outside = mine[:, planes * CYCLES : edge] + theirs[:, planes * CYCLES : edge]
    spec_low = lax.ppermute(outside[:, : 2 * CYCLES], "ax", up)
    spec_high = lax.ppermute(outside[:, 2 * CYCLES :], "ax", down)

    section = local_section(pltpu.with_memory_space_constraint(conserved, pltpu.HBM), az, mine, theirs, early, late, basis, length)
    section, signal = add_edges(
        section, low, high, spec_low, spec_high, basis, sums, observers
    )
    return (section, signal.T)


def solution(mesh):
    placed = (
        P(None, "ax", "az", None),
        P(("ax", "az")),
        P(("ax", "az")),
        P(("ax", "az"), None),
        P(("ax", "az"), None),
    )
    return jax.shard_map(
        on_device,
        mesh=mesh,
        in_specs=placed,
        out_specs=(P(None, "ax", "az", None), P(None, ("ax", "az"))),
        check_vma=False,
    )
```

```python
import functools
import math

import jax
import jax.numpy as jnp
import numpy as np
from jax import lax
from jax.experimental import pallas as pl
from jax.experimental.pallas import tpu as pltpu
from jax.sharding import PartitionSpec as P

CYCLES = 8
BINS = 1024
LOW_BINS = 32
FIELDS = 5
MODES = 8 * CYCLES
COEFS = 2 * MODES
ROWS = 8

gas_factor = 0.4
time_step = 0.02
ref_pressure = 0.95
VMEM_BYTES = 48 * 1024 * 1024

HIGHEST = lax.Precision.HIGHEST


def params(**more):
    return pltpu.CompilerParams(vmem_limit_bytes=VMEM_BYTES, **more)


def cost(flops, touched):
    return pl.CostEstimate(flops=flops, bytes_accessed=touched, transcendentals=0)


def basis_table(length):
    phase = (np.arange(length)[:, None] * np.arange(MODES)[None, :] % length) * (
        2.0 * math.pi / length
    )
    return np.concatenate([np.cos(phase), np.sin(phase)], axis=1).astype(np.float32)


def mode_weights(length):
    modes = np.arange(MODES).astype(np.float64)
    cutoff = 4.0 * (np.arange(CYCLES) + 1.0)
    weight = np.exp(-((modes[None, :] / cutoff[:, None]) ** 8))
    weight = weight * np.where(modes == 0, 1.0, 2.0)[None, :] / length
    return np.concatenate([weight, weight], axis=1).astype(np.float32)


def primitives(q):
    inverse = 1.0 / q[0]
    u, v, w = q[1] * inverse, q[2] * inverse, q[3] * inverse
    p = gas_factor * (q[4] - 0.5 * (q[1] * u + q[2] * v + q[3] * w))
    return u, v, w, p


def carried(q, p, speed, heading):
    flux = [q[0] * speed, q[1] * speed, q[2] * speed, q[3] * speed, (q[4] + p) * speed]
    flux[heading] = flux[heading] + p
    return flux


def swirl_rows(ref, low):
    for k in range(ref.shape[1]):
        q = [ref[f, k] for f in range(FIELDS)]
        _, _, w, p = primitives(q)
        flux = carried(q, p, w, 3)
        yield k, [jnp.where(low, f[:2], f[ROWS - 2 :]) for f in flux]


def edge_kernel(az_ref, top_ref, bottom_ref, rim_ref, up_ref, down_ref, early_ref):
    sector, radial = top_ref.shape[2:]
    groups = radial // CYCLES - 1
    tail = sector * CYCLES // radial
    scale = time_step / 12.0
    lane = lax.broadcasted_iota(jnp.int32, (1, radial), 1)

    def go(up, q_ref, send):
        def terms(start):
            rows = pl.ds(start, tail)
            flux = []
            for plane in range(2):
                q = [q_ref[f, plane, rows, :] for f in range(FIELDS)]
                u, _, _, p = primitives(q)
                flux.append(carried(q, p, u, 1))
            near, far = (flux[1], flux[0]) if up else (flux[0], flux[1])
            whole, part = [], []
            for f in range(FIELDS):
                wide = scale * (8.0 * near[f] - far[f])
                narrow = scale * near[f]
                whole.append(wide if up else -wide)
                part.append(-narrow if up else narrow)
            return (whole, part) if up else (part, whole)

        last = terms(groups * tail)
        for g in range(groups):
            slots = terms(g * tail)
            shift = radial - CYCLES * (g + 1)
            for s in range(2):
                for f in range(FIELDS):
                    moved = pltpu.roll(last[s][f], shift, 1)
                    send[f, s, pl.ds(g * tail, tail), :] = jnp.where(
                        lane < CYCLES, moved, slots[s][f]
                    )

    go(True, top_ref, up_ref)
    go(False, bottom_ref, down_ref)
    for k, flux in swirl_rows(rim_ref, lax.rem(az_ref[0], 2) == 1):
        for f in range(FIELDS):
            early_ref[f, 2 * k : 2 * k + 2, :] = flux[f]


def edge_terms(conserved, az):
    fields, planes, sector, radial = conserved.shape
    out = jax.ShapeDtypeStruct((fields, 2, sector - sector * CYCLES // radial, radial), jnp.float32)
    early = jax.ShapeDtypeStruct((fields, 2 * planes, radial), jnp.float32)
    last = sector // ROWS - 1
    wide = pl.BlockSpec(out.shape, lambda i, *_: (0, 0, 0, 0))
    return pl.pallas_call(
        edge_kernel,
        grid_spec=pltpu.PrefetchScalarGridSpec(
            num_scalar_prefetch=1,
            grid=(1,),
            in_specs=[
                pl.BlockSpec((fields, 2, sector, radial), lambda i, az: (0, planes // 2 - 1, 0, 0)),
                pl.BlockSpec((fields, 2, sector, radial), lambda i, az: (0, 0, 0, 0)),
                pl.BlockSpec(
                    (fields, planes, ROWS, radial),
                    lambda i, az: (0, 0, last * (1 - lax.rem(az[0], 2)), 0),
                ),
            ],
            out_specs=[wide, wide, pl.BlockSpec(early.shape, lambda i, *_: (0, 0, 0))],
        ),
        out_shape=[out, out, early],
        compiler_params=params(),
        cost_estimate=cost(400 * sector * radial, 4 * 8 * fields * sector * radial),
        name="edge_terms",
    )(az, conserved, conserved, conserved)


def inner_kernel(dtheta, *refs):
    az_ref, q_ref, rim_ref, basis_ref, _ = refs[:5]
    message_ref, later_ref, local, swirl, outside = refs[5:]
    fields, planes, sector, radial = q_ref.shape
    group = 2 * CYCLES
    scale = time_step / 12.0
    chunk = min(sector, 32 * ROWS)
    lane = lax.broadcasted_iota(jnp.int32, (1, radial), 1)
    cycle = lane & (group - 1)
    plane = lane // group
    radius = cycle.astype(jnp.float32) + 0.5
    inverse = 1.0 / radius
    near = 8.0 * scale * inverse
    far = scale * inverse
    near_down = jnp.where(cycle >= 1, near, 0.0)
    far_down = jnp.where(cycle >= 2, far, 0.0)
    source = time_step * inverse
    turn = scale * inverse / dtheta

    def split(there, value):
        return jnp.where(there, value, 0.0), jnp.where(there, 0.0, value)

    behind, behind_out = split(plane >= 1, 8.0 * scale)
    behind2, behind2_out = split(plane >= 2, scale)
    ahead, ahead_out = split(plane < planes - 1, 8.0 * scale)
    ahead2, ahead2_out = split(plane < planes - 2, scale)

    zeros = jnp.zeros((FIELDS, 2 * ROWS, radial), jnp.float32)
    swirl[:, : 2 * ROWS, :] = zeros
    swirl[:, 2 * ROWS + sector :, :] = zeros
    local[:, :ROWS, :] = zeros[:, :ROWS]
    local[:, ROWS + sector :, :] = zeros[:, :ROWS]

    def body(i, _):
        start = pl.multiple_of(i * chunk, chunk)
        rows = pl.ds(start, chunk)
        q = []
        for f in range(FIELDS):
            packed = q_ref[f, 0, rows, :]
            for k in range(1, planes):
                moved = pltpu.roll(q_ref[f, k, rows, :], group * k, 1)
                packed = jnp.where(plane == k, moved, packed)
            q.append(packed)
        u, v, w, p = primitives(q)
        along = carried(q, p, u, 1)
        around = carried(q, p, w, 3)
        outward = carried(q, p, v, 2)
        for f in range(FIELDS):
            swirl[f, pl.ds(start + 2 * ROWS, chunk), :] = around[f]
            g = outward[f] * radius
            value = q[f] - near * pltpu.roll(g, radial - 1, 1)
            value = value + near_down * pltpu.roll(g, 1, 1)
            value = value + far * pltpu.roll(g, radial - 2, 1)
            value = value - far_down * pltpu.roll(g, 2, 1)
            if f == 2:
                value = value + source * (p + q[3] * w)
            if f == 3:
                value = value - source * (q[2] * w)
            up1 = pltpu.roll(along[f], group, 1)
            up2 = pltpu.roll(along[f], 2 * group, 1)
            down1 = pltpu.roll(along[f], radial - group, 1)
            down2 = pltpu.roll(along[f], radial - 2 * group, 1)
            value = value + behind * up1 - behind2 * up2 - ahead * down1 + ahead2 * down2
            local[f, pl.ds(start + ROWS, chunk), :] = value
            outside[f, rows, :] = (
                behind_out * up1 - behind2_out * up2 - ahead_out * down1 + ahead2_out * down2
            )
        return 0

    lax.fori_loop(0, sector // chunk, body, 0)

    def rest(start, size):
        for f in range(FIELDS):
            at = lambda k: swirl[f, pl.ds(start + (ROWS + k), size), :]
            around = 8.0 * (at(1) - at(-1)) - (at(2) - at(-2))
            rows = pl.ds(start, size)
            local[f, rows, :] = local[f, rows, :] - turn * around

    rest(0, ROWS)
    rest(ROWS + sector, ROWS)

    def body2(i, _):
        rest(pl.multiple_of(i * chunk, chunk) + ROWS, chunk)
        return 0

    lax.fori_loop(0, sector // chunk, body2, 0)

    def transform(rows, table):
        return lax.dot_general(
            rows, table, (((0,), (0,)), ((), ())),
            precision=HIGHEST, preferred_element_type=jnp.float32,
        )

    for f in range(FIELDS):
        own = transform(local[f], basis_ref[: sector + 2 * ROWS, :])
        for k in range(planes):
            message_ref[f, k * CYCLES : (k + 1) * CYCLES, :] = own[k * group : k * group + CYCLES]
        other = transform(outside[f], basis_ref[ROWS : ROWS + sector, :])
        for s, k in enumerate((0, 1, planes - 2, planes - 1)):
            at = (planes + s) * CYCLES
            message_ref[f, at : at + CYCLES, :] = other[k * group : k * group + CYCLES]

    for k, flux in swirl_rows(rim_ref, lax.rem(az_ref[0], 2) == 0):
        for f in range(FIELDS):
            later_ref[f, 2 * k : 2 * k + 2, :] = flux[f]


def inner_terms(conserved, az, basis, length, after):
    fields, planes, sector, radial = conserved.shape
    message = (fields, (planes + 4) * CYCLES, COEFS)
    later = (fields, 2 * planes, radial)
    full = lambda *shape: pl.BlockSpec(shape, lambda i, *_: (0,) * len(shape))
    tiles = sector // ROWS
    return pl.pallas_call(
        functools.partial(inner_kernel, 2.0 * math.pi / length),
        grid_spec=pltpu.PrefetchScalarGridSpec(
            num_scalar_prefetch=1,
            grid=(1,),
            in_specs=[
                full(*conserved.shape),
                pl.BlockSpec(
                    (fields, planes, ROWS, radial),
                    lambda i, az: (0, 0, (tiles - 1) * lax.rem(az[0], 2), 0),
                ),
                full(*basis.shape),
                pl.BlockSpec(memory_space=pl.ANY),
            ],
            out_specs=[full(*message), full(*later)],
            scratch_shapes=[
                pltpu.VMEM((fields, sector + 2 * ROWS, radial), jnp.float32),
                pltpu.VMEM((fields, sector + 4 * ROWS, radial), jnp.float32),
                pltpu.VMEM((fields, sector, radial), jnp.float32),
            ],
        ),
        out_shape=[
            jax.ShapeDtypeStruct(message, jnp.float32),
            jax.ShapeDtypeStruct(later, jnp.float32),
        ],
        compiler_params=params(),
        cost_estimate=cost(60 * sector * radial * COEFS, 4 * fields * planes * sector * radial),
        name="inner_terms",
    )(az, conserved, conserved, basis, after)


def panel_kernel(n_ax, n_az, cells_ref, count_ref, row_ref, q_ref, bins_ref, amp_ref, _, out_ref, held):
    slots = row_ref.shape[1]
    radial = q_ref.shape[2]
    observers = bins_ref.shape[0]
    count = count_ref[0]
    width = 8

    def fetch(i, _):
        for k in range(width):
            s = i * width + k
            at = cells_ref[s] // radial
            held[:, pl.ds(s, 1), :] = q_ref[:, pl.ds(at, 1), :]
        return 0

    lax.fori_loop(0, (count + width - 1) // width, fetch, 0)
    q = [held[f] for f in range(FIELDS)]
    p = gas_factor * (q[4] - 0.5 * (q[1] * q[1] + q[2] * q[2] + q[3] * q[3]) / q[0])
    turned = jnp.transpose(p)
    which = lax.broadcasted_iota(jnp.int32, (radial, slots), 0)
    here = which == (row_ref[...] & (radial - 1))
    sampled = jnp.sum(jnp.where(here, turned, 0.0), axis=0, keepdims=True) - ref_pressure
    slot = lax.broadcasted_iota(jnp.int32, (1, slots), 1)
    sampled = jnp.where(slot < count, sampled, 0.0)

    contrib = sampled * amp_ref[...]
    first = contrib.astype(jnp.bfloat16).astype(jnp.float32)
    second = contrib - first
    bins = bins_ref[...]
    low = bins & (LOW_BINS - 1)
    high = bins // LOW_BINS
    if n_ax * n_az * LOW_BINS == BINS:
        high = (high % n_az) * n_ax + high // n_az
    each = 128 // LOW_BINS
    high_count = BINS // LOW_BINS
    low_iota = lax.broadcasted_iota(jnp.int32, (LOW_BINS, slots), 0)
    high_iota = lax.broadcasted_iota(jnp.int32, (high_count, slots), 0)
    lane = lax.broadcasted_iota(jnp.int32, (high_count, 128), 1)
    for g in range(observers // each):
        left, right = [], []
        for k in range(each):
            o = g * each + k
            hit = high_iota == high[o : o + 1]
            left.append(jnp.where(hit, first[o : o + 1], 0.0).astype(jnp.bfloat16))
            left.append(jnp.where(hit, second[o : o + 1], 0.0).astype(jnp.bfloat16))
            same = low_iota == low[o : o + 1]
            right.append(jnp.where(same, 1.0, 0.0).astype(jnp.bfloat16))
        sums = lax.dot_general(
            jnp.concatenate(left, axis=0),
            jnp.concatenate(right, axis=0),
            (((1,), (1,)), ((), ())),
            preferred_element_type=jnp.float32,
        )
        total = jnp.zeros((high_count, 128), jnp.float32)
        for k in range(each):
            at = 2 * k * high_count
            both = sums[at : at + high_count] + sums[at + high_count : at + 2 * high_count]
            total = jnp.where(lane // LOW_BINS == k, both, total)
        out_ref[:, g, :] = total


def panel_sums(conserved, cells, counts, bins, amplitudes, after):
    fields, planes, sector, radial = conserved.shape
    slots, observers = bins.shape
    flat = conserved.reshape(fields, planes * sector, radial)
    high_count = BINS // LOW_BINS
    full = lambda *shape: pl.BlockSpec(shape, lambda i, *_: (0,) * len(shape))
    return pl.pallas_call(
        functools.partial(panel_kernel, lax.axis_size("ax"), lax.axis_size("az")),
        grid_spec=pltpu.PrefetchScalarGridSpec(
            num_scalar_prefetch=2,
            grid=(1,),
            in_specs=[
                full(1, slots),
                full(fields, planes * sector, radial),
                full(observers, slots),
                full(observers, slots),
                pl.BlockSpec(memory_space=pl.ANY),
            ],
            out_specs=full(high_count, observers * LOW_BINS // 128, 128),
            scratch_shapes=[pltpu.VMEM((fields, slots, radial), jnp.float32)],
        ),
        out_shape=jax.ShapeDtypeStruct(
            (high_count, observers * LOW_BINS // 128, 128), jnp.float32
        ),
        compiler_params=params(),
        cost_estimate=cost(8 * observers * slots * BINS, 4 * fields * planes * sector * radial),
        name="panel_sums",
    )(cells, counts, cells.reshape(1, slots), flat, bins.T, amplitudes.T, after)


def section_kernel(dtheta, *refs):
    az_ref, q_ref, mine_ref, theirs_ref, early_ref, late_ref, basis_ref = refs[:7]
    out_ref, axial, swirl, local, spec, smooth = refs[7:]
    fields, _, sector, radial = q_ref.shape
    step = pl.program_id(0)
    planes = pl.num_programs(0) - 2
    scale = time_step / 12.0
    chunk = min(sector, 32 * ROWS)
    lane = lax.broadcasted_iota(jnp.int32, (1, radial), 1)
    radius = lane.astype(jnp.float32) + 0.5
    inverse = 1.0 / radius
    near = 8.0 * scale * inverse
    far = scale * inverse
    near_up = jnp.where(lane < radial - 1, near, 0.0)
    near_down = jnp.where(lane >= 1, near, 0.0)
    far_up = jnp.where(lane < radial - 2, far, 0.0)
    far_down = jnp.where(lane >= 2, far, 0.0)
    source = time_step * inverse
    odd = lax.rem(az_ref[0], 2) == 1
    static_planes = axial.shape[0] - 4

    @pl.when(step == 0)
    def _():
        axial[0:2] = jnp.zeros((2,) + axial.shape[1:], jnp.float32)
        axial[planes + 2 : planes + 4] = jnp.zeros((2,) + axial.shape[1:], jnp.float32)
        spec[...] = jnp.zeros_like(spec)
        for k in range(static_planes):
            for f in range(FIELDS):
                rows = slice(k * CYCLES, (k + 1) * CYCLES)
                value = mine_ref[f, rows, :] + theirs_ref[f, rows, :]
                spec[k, f * CYCLES : (f + 1) * CYCLES, :] = value * basis_ref[sector + 2 * ROWS :, :]

    @pl.when(step < planes)
    def _():
        slot = lax.rem(step, 3)
        for f in range(FIELDS):
            early = early_ref[f, pl.ds(2 * step, 2), :]
            late = late_ref[f, pl.ds(2 * step, 2), :]
            swirl[slot, f, ROWS - 2 : ROWS, :] = jnp.where(odd, early, late)
            swirl[slot, f, ROWS + sector : ROWS + sector + 2, :] = jnp.where(odd, late, early)

        def body(i, _):
            start = pl.multiple_of(i * chunk, chunk)
            rows = pl.ds(start, chunk)
            q = [q_ref[f, 0, rows, :] for f in range(FIELDS)]
            u, v, w, p = primitives(q)
            along = carried(q, p, u, 1)
            around = carried(q, p, w, 3)
            outward = carried(q, p, v, 2)
            for f in range(FIELDS):
                axial[step + 2, f, rows, :] = along[f]
                swirl[slot, f, pl.ds(start + ROWS, chunk), :] = around[f]
                g = outward[f] * radius
                value = q[f] - near_up * pltpu.roll(g, radial - 1, 1)
                value = value + near_down * pltpu.roll(g, 1, 1)
                value = value + far_up * pltpu.roll(g, radial - 2, 1)
                value = value - far_down * pltpu.roll(g, 2, 1)
                if f == 2:
                    value = value + source * (p + q[3] * w)
                if f == 3:
                    value = value - source * (q[2] * w)
                local[slot, f, rows, :] = value
            return 0

        lax.fori_loop(0, sector // chunk, body, 0)

    @pl.when(step >= 2)
    def _():
        plane = step - 2
        slot = lax.rem(plane, 3)
        turn = scale * inverse / dtheta
        smooth[...] = lax.dot_general(
            basis_ref[ROWS : ROWS + sector, :], spec[plane], (((1,), (1,)), ((), ())),
            precision=HIGHEST, preferred_element_type=jnp.float32,
        )

        def body(i, _):
            start = pl.multiple_of(i * chunk, chunk)
            rows = pl.ds(start, chunk)
            for f in range(FIELDS):
                at = lambda k: swirl[slot, f, pl.ds(start + (ROWS + k), chunk), :]
                of = lambda k: axial[plane + 2 + k, f, rows, :]
                around = 8.0 * (at(1) - at(-1)) - (at(2) - at(-2))
                along = 8.0 * (of(1) - of(-1)) - (of(2) - of(-2))
                value = local[slot, f, rows, :] - turn * around - scale * along
                moved = smooth[rows, :]
                if f > 0:
                    moved = pltpu.roll(moved, radial - CYCLES * f, 1)
                out_ref[f, 0, rows, :] = jnp.where(lane < CYCLES, moved, value)
            return 0

        lax.fori_loop(0, sector // chunk, body, 0)


def local_section(conserved, az, mine, theirs, early, late, basis, length):
    fields, planes, sector, radial = conserved.shape
    two_back = lambda i: jnp.maximum(i - 2, 0)
    ring = (fields, 2 * planes, radial)
    last = late.shape[1] // ring[1] - 1
    full = lambda a: pl.BlockSpec(a.shape, lambda i, *_: (0,) * a.ndim)
    plane = (fields, 1, sector, radial)
    return pl.pallas_call(
        functools.partial(section_kernel, 2.0 * math.pi / length),
        grid_spec=pltpu.PrefetchScalarGridSpec(
            num_scalar_prefetch=1,
            grid=(planes + 2,),
            in_specs=[
                pl.BlockSpec(plane, lambda i, *_: (0, jnp.minimum(i, planes - 1), 0, 0)),
                full(mine),
                full(theirs),
                full(early),
                pl.BlockSpec(ring, lambda i, *_: (0, last, 0)),
                full(basis),
            ],
            out_specs=pl.BlockSpec(plane, lambda i, *_: (0, two_back(i), 0, 0)),
            scratch_shapes=[
                pltpu.VMEM((planes + 4, fields, sector, radial), jnp.float32),
                pltpu.VMEM((3, fields, sector + 2 * ROWS, radial), jnp.float32),
                pltpu.VMEM((3, fields, sector, radial), jnp.float32),
                pltpu.VMEM((planes, radial, COEFS), jnp.float32),
                pltpu.VMEM((sector, radial), jnp.float32),
            ],
        ),
        out_shape=jax.ShapeDtypeStruct(conserved.shape, jnp.float32),
        compiler_params=params(),
        cost_estimate=cost(
            600 * planes * sector * radial, 10 * 4 * fields * planes * sector * radial
        ),
        name="local_section",
    )(az, conserved, mine, theirs, early, late, basis)


def add_kernel(part_ref, low_ref, high_ref, spec_low, spec_high, basis_ref, sums_ref, *outs):
    out_ref, signal_ref, padded, turned = outs
    step = pl.program_id(0)
    fields, _, sector, radial = part_ref.shape
    groups = radial // CYCLES - 1
    tail = sector // (groups + 1)
    main = groups * tail
    lane = lax.broadcasted_iota(jnp.int32, (1, radial), 1)
    wide = lane >= CYCLES

    @pl.when(step == 0)
    def _():
        padded[...] = jnp.zeros_like(padded)
        observers, _ = turned.shape
        bins = signal_ref.shape[0]
        total = jnp.sum(sums_ref[...], axis=0)
        for o in range(observers):
            row, at = o * bins // 128, o * bins % 128
            piece = total[row : row + 1]
            turned[o : o + 1, :] = pltpu.roll(piece, 128 - at, 1) if at else piece
        signal_ref[...] = jnp.transpose(turned[...])[:bins]

    weight = basis_ref[sector + 2 * ROWS :, :]

    def go(ref, spec_ref):
        for slot in range(2):
            for f in range(fields):
                rows = slice(slot * CYCLES, (slot + 1) * CYCLES)
                at = (slot * fields + f) * CYCLES
                padded[at : at + CYCLES, :] = spec_ref[f, rows, :] * weight
        smooth = lax.dot_general(
            basis_ref[ROWS : ROWS + sector, :], padded[...], (((1,), (1,)), ((), ())),
            precision=HIGHEST, preferred_element_type=jnp.float32,
        )
        for slot in range(2):
            for f in range(fields):
                k = slot * fields + f
                inner = smooth if k == 0 else pltpu.roll(smooth, radial - CYCLES * k, 1)
                out_ref[f, slot, :main, :] = part_ref[f, slot, :main, :] + jnp.where(
                    wide, ref[f, slot], inner[:main]
                )
                rest = inner[main:]
                for g in range(groups):
                    moved = pltpu.roll(ref[f, slot, g * tail : (g + 1) * tail, :], CYCLES * (g + 1), 1)
                    rest = jnp.where(lane // CYCLES == g + 1, moved, rest)
                out_ref[f, slot, main:, :] = part_ref[f, slot, main:, :] + rest

    pl.when(step == 0)(lambda: go(low_ref, spec_low))
    pl.when(step == 1)(lambda: go(high_ref, spec_high))


def add_edges(section, low, high, spec_low, spec_high, basis, sums, observers):
    fields, planes, sector, radial = section.shape
    bins = sums.shape[1] * sums.shape[2] // observers
    full = lambda a: pl.BlockSpec(a.shape, lambda i, *_: (0,) * a.ndim)
    plane = pl.BlockSpec(
        (fields, 2, sector, radial), lambda i, *_: (0, (planes // 2 - 1) * i, 0, 0)
    )
    return pl.pallas_call(
        add_kernel,
        grid_spec=pltpu.PrefetchScalarGridSpec(
            num_scalar_prefetch=0,
            grid=(2,),
            in_specs=[
                plane,
                full(low),
                full(high),
                full(spec_low),
                full(spec_high),
                full(basis),
                full(sums),
            ],
            out_specs=[plane, pl.BlockSpec((bins, observers), lambda i, *_: (0, 0))],
            scratch_shapes=[
                pltpu.VMEM((radial, COEFS), jnp.float32),
                pltpu.VMEM((observers, 128), jnp.float32),
            ],
        ),
        out_shape=[
            jax.ShapeDtypeStruct(section.shape, jnp.float32),
            jax.ShapeDtypeStruct((bins, observers), jnp.float32),
        ],
        input_output_aliases={0: 0},
        compiler_params=params(),
        cost_estimate=cost(8 * fields * sector * radial, 4 * 12 * fields * sector * radial),
        name="add_edges",
    )(section, low, high, spec_low, spec_high, basis, sums)


def exchanged_sums(partial, observers):
    n_ax, n_az = lax.axis_size("ax"), lax.axis_size("az")
    mine = BINS // (n_ax * n_az)
    if mine != LOW_BINS:
        partial = partial.reshape(-1, observers, LOW_BINS).transpose(0, 2, 1)
        partial = partial.reshape(n_ax, n_az, mine, observers).transpose(1, 0, 3, 2)
    blocks = partial.reshape(n_az, n_ax, observers * mine // 128, 128)
    blocks = lax.all_to_all(blocks, "az", split_axis=0, concat_axis=0, tiled=True).sum(axis=0)
    return lax.all_to_all(blocks, "ax", split_axis=0, concat_axis=0, tiled=True)


def on_device(conserved, panel_cells, panel_counts, time_bins, amplitudes):
    fields, planes, sector, radial = conserved.shape
    observers = time_bins.shape[1]
    n_ax, n_az = lax.axis_size("ax"), lax.axis_size("az")
    length = sector * n_az
    up = [(i, i + 1) for i in range(n_ax - 1)]
    down = [(j, i) for i, j in up]
    az = lax.axis_index("az").astype(jnp.int32).reshape(1)
    table = basis_table(length)
    table = jnp.asarray(np.concatenate([table[-ROWS:], table, table[:ROWS]], axis=0))
    basis = lax.dynamic_slice_in_dim(table, az[0] * sector, sector + 2 * ROWS, axis=0)
    basis = jnp.concatenate([basis, jnp.asarray(mode_weights(length))], axis=0)

    pair = [(i, i ^ 1) for i in range(n_az)]
    send_up, send_down, early = edge_terms(conserved, az)
    early = lax.ppermute(early, "az", pair)
    low = lax.ppermute(send_up, "ax", up)
    high = lax.ppermute(send_down, "ax", down)

    message, later = inner_terms(conserved, az, basis, length, early)
    edge = (planes + 4) * CYCLES
    partial = panel_sums(conserved, panel_cells, panel_counts, time_bins, amplitudes, message)
    sums = exchanged_sums(partial, observers)

    mine = jnp.concatenate([message + lax.ppermute(message, "az", pair), later], axis=1)
    pairs = [(i, (i + 1) % n_az) for i in range(1, n_az, 2)]
    theirs = lax.ppermute(mine, "az", pairs + [(j, i) for i, j in pairs])
    late = theirs
    shift = 4
    while shift < n_az:
        mine = mine + theirs
        theirs = lax.ppermute(mine, "az", [(i, (i + shift) % n_az) for i in range(n_az)])
        shift *= 2
    outside = mine[:, planes * CYCLES : edge] + theirs[:, planes * CYCLES : edge]
    spec_low = lax.ppermute(outside[:, : 2 * CYCLES], "ax", up)
    spec_high = lax.ppermute(outside[:, 2 * CYCLES :], "ax", down)

    section = local_section(pltpu.with_memory_space_constraint(conserved, pltpu.HBM), az, mine, theirs, early, late, basis, length)
    section, signal = add_edges(
        section, low, high, spec_low, spec_high, basis, sums, observers
    )
    return (section, signal.T)


def solution(mesh):
    placed = (
        P(None, "ax", "az", None),
        P(("ax", "az")),
        P(("ax", "az")),
        P(("ax", "az"), None),
        P(("ax", "az"), None),
    )
    return jax.shard_map(
        on_device,
        mesh=mesh,
        in_specs=placed,
        out_specs=(P(None, "ax", "az", None), P(None, ("ax", "az"))),
        check_vma=False,
    )
```

```python
import functools
import math

import jax
import jax.numpy as jnp
import numpy as np
from jax import lax
from jax.experimental import pallas as pl
from jax.experimental.pallas import tpu as pltpu
from jax.sharding import PartitionSpec as P

CYCLES = 8
BINS = 1024
LOW_BINS = 32
FIELDS = 5
MODES = 8 * CYCLES
COEFS = 2 * MODES
ROWS = 8

gas_factor = 0.4
time_step = 0.02
ref_pressure = 0.95
VMEM_BYTES = 48 * 1024 * 1024

HIGHEST = lax.Precision.HIGHEST


def params(**more):
    return pltpu.CompilerParams(vmem_limit_bytes=VMEM_BYTES, **more)


def cost(flops, touched):
    return pl.CostEstimate(flops=flops, bytes_accessed=touched, transcendentals=0)


def basis_table(length):
    phase = (np.arange(length)[:, None] * np.arange(MODES)[None, :] % length) * (
        2.0 * math.pi / length
    )
    return np.concatenate([np.cos(phase), np.sin(phase)], axis=1).astype(np.float32)


def mode_weights(length):
    modes = np.arange(MODES).astype(np.float64)
    cutoff = 4.0 * (np.arange(CYCLES) + 1.0)
    weight = np.exp(-((modes[None, :] / cutoff[:, None]) ** 8))
    weight = weight * np.where(modes == 0, 1.0, 2.0)[None, :] / length
    return np.concatenate([weight, weight], axis=1).astype(np.float32)


def primitives(q):
    inverse = 1.0 / q[0]
    u, v, w = q[1] * inverse, q[2] * inverse, q[3] * inverse
    p = gas_factor * (q[4] - 0.5 * (q[1] * u + q[2] * v + q[3] * w))
    return u, v, w, p


def carried(q, p, speed, heading):
    flux = [q[0] * speed, q[1] * speed, q[2] * speed, q[3] * speed, (q[4] + p) * speed]
    flux[heading] = flux[heading] + p
    return flux


def swirl_rows(ref, low):
    for k in range(ref.shape[1]):
        q = [ref[f, k] for f in range(FIELDS)]
        _, _, w, p = primitives(q)
        flux = carried(q, p, w, 3)
        yield k, [jnp.where(low, f[:2], f[ROWS - 2 :]) for f in flux]


def edge_kernel(az_ref, top_ref, bottom_ref, rim_ref, up_ref, down_ref, early_ref):
    sector, radial = top_ref.shape[2:]
    groups = radial // CYCLES - 1
    tail = sector * CYCLES // radial
    scale = time_step / 12.0
    lane = lax.broadcasted_iota(jnp.int32, (1, radial), 1)

    def go(up, q_ref, send):
        def terms(start):
            rows = pl.ds(start, tail)
            flux = []
            for plane in range(2):
                q = [q_ref[f, plane, rows, :] for f in range(FIELDS)]
                u, _, _, p = primitives(q)
                flux.append(carried(q, p, u, 1))
            near, far = (flux[1], flux[0]) if up else (flux[0], flux[1])
            whole, part = [], []
            for f in range(FIELDS):
                wide = scale * (8.0 * near[f] - far[f])
                narrow = scale * near[f]
                whole.append(wide if up else -wide)
                part.append(-narrow if up else narrow)
            return (whole, part) if up else (part, whole)

        last = terms(groups * tail)
        for g in range(groups):
            slots = terms(g * tail)
            shift = radial - CYCLES * (g + 1)
            for s in range(2):
                for f in range(FIELDS):
                    moved = pltpu.roll(last[s][f], shift, 1)
                    send[f, s, pl.ds(g * tail, tail), :] = jnp.where(
                        lane < CYCLES, moved, slots[s][f]
                    )

    go(True, top_ref, up_ref)
    go(False, bottom_ref, down_ref)
    for k, flux in swirl_rows(rim_ref, lax.rem(az_ref[0], 2) == 1):
        for f in range(FIELDS):
            early_ref[f, 2 * k : 2 * k + 2, :] = flux[f]


def edge_terms(conserved, az):
    fields, planes, sector, radial = conserved.shape
    out = jax.ShapeDtypeStruct((fields, 2, sector - sector * CYCLES // radial, radial), jnp.float32)
    early = jax.ShapeDtypeStruct((fields, 2 * planes, radial), jnp.float32)
    last = sector // ROWS - 1
    wide = pl.BlockSpec(out.shape, lambda i, *_: (0, 0, 0, 0))
    return pl.pallas_call(
        edge_kernel,
        grid_spec=pltpu.PrefetchScalarGridSpec(
            num_scalar_prefetch=1,
            grid=(1,),
            in_specs=[
                pl.BlockSpec((fields, 2, sector, radial), lambda i, az: (0, planes // 2 - 1, 0, 0)),
                pl.BlockSpec((fields, 2, sector, radial), lambda i, az: (0, 0, 0, 0)),
                pl.BlockSpec(
                    (fields, planes, ROWS, radial),
                    lambda i, az: (0, 0, last * (1 - lax.rem(az[0], 2)), 0),
                ),
            ],
            out_specs=[wide, wide, pl.BlockSpec(early.shape, lambda i, *_: (0, 0, 0))],
        ),
        out_shape=[out, out, early],
        compiler_params=params(),
        cost_estimate=cost(400 * sector * radial, 4 * 8 * fields * sector * radial),
        name="edge_terms",
    )(az, conserved, conserved, conserved)


def inner_kernel(dtheta, *refs):
    az_ref, q_ref, rim_ref, basis_ref, _ = refs[:5]
    message_ref, later_ref, local, swirl, outside = refs[5:]
    fields, planes, sector, radial = q_ref.shape
    group = 2 * CYCLES
    scale = time_step / 12.0
    chunk = min(sector, 32 * ROWS)
    lane = lax.broadcasted_iota(jnp.int32, (1, radial), 1)
    cycle = lane & (group - 1)
    plane = lane // group
    radius = cycle.astype(jnp.float32) + 0.5
    inverse = 1.0 / radius
    near = 8.0 * scale * inverse
    far = scale * inverse
    near_down = jnp.where(cycle >= 1, near, 0.0)
    far_down = jnp.where(cycle >= 2, far, 0.0)
    source = time_step * inverse
    turn = scale * inverse / dtheta

    def split(there, value):
        return jnp.where(there, value, 0.0), jnp.where(there, 0.0, value)

    behind, behind_out = split(plane >= 1, 8.0 * scale)
    behind2, behind2_out = split(plane >= 2, scale)
    ahead, ahead_out = split(plane < planes - 1, 8.0 * scale)
    ahead2, ahead2_out = split(plane < planes - 2, scale)

    zeros = jnp.zeros((FIELDS, 2 * ROWS, radial), jnp.float32)
    swirl[:, : 2 * ROWS, :] = zeros
    swirl[:, 2 * ROWS + sector :, :] = zeros
    local[:, :ROWS, :] = zeros[:, :ROWS]
    local[:, ROWS + sector :, :] = zeros[:, :ROWS]

    def body(i, _):
        start = pl.multiple_of(i * chunk, chunk)
        rows = pl.ds(start, chunk)
        q = []
        for f in range(FIELDS):
            packed = q_ref[f, 0, rows, :]
            for k in range(1, planes):
                moved = pltpu.roll(q_ref[f, k, rows, :], group * k, 1)
                packed = jnp.where(plane == k, moved, packed)
            q.append(packed)
        u, v, w, p = primitives(q)
        along = carried(q, p, u, 1)
        around = carried(q, p, w, 3)
        outward = carried(q, p, v, 2)
        for f in range(FIELDS):
            swirl[f, pl.ds(start + 2 * ROWS, chunk), :] = around[f]
            g = outward[f] * radius
            value = q[f] - near * pltpu.roll(g, radial - 1, 1)
            value = value + near_down * pltpu.roll(g, 1, 1)
            value = value + far * pltpu.roll(g, radial - 2, 1)
            value = value - far_down * pltpu.roll(g, 2, 1)
            if f == 2:
                value = value + source * (p + q[3] * w)
            if f == 3:
                value = value - source * (q[2] * w)
            up1 = pltpu.roll(along[f], group, 1)
            up2 = pltpu.roll(along[f], 2 * group, 1)
            down1 = pltpu.roll(along[f], radial - group, 1)
            down2 = pltpu.roll(along[f], radial - 2 * group, 1)
            value = value + behind * up1 - behind2 * up2 - ahead * down1 + ahead2 * down2
            local[f, pl.ds(start + ROWS, chunk), :] = value
            outside[f, rows, :] = (
                behind_out * up1 - behind2_out * up2 - ahead_out * down1 + ahead2_out * down2
            )
        return 0

    lax.fori_loop(0, sector // chunk, body, 0)

    def rest(start, size):
        for f in range(FIELDS):
            at = lambda k: swirl[f, pl.ds(start + (ROWS + k), size), :]
            around = 8.0 * (at(1) - at(-1)) - (at(2) - at(-2))
            rows = pl.ds(start, size)
            local[f, rows, :] = local[f, rows, :] - turn * around

    rest(0, ROWS)
    rest(ROWS + sector, ROWS)

    def body2(i, _):
        rest(pl.multiple_of(i * chunk, chunk) + ROWS, chunk)
        return 0

    lax.fori_loop(0, sector // chunk, body2, 0)

    def transform(rows, table):
        return lax.dot_general(
            rows, table, (((0,), (0,)), ((), ())),
            precision=HIGHEST, preferred_element_type=jnp.float32,
        )

    for f in range(FIELDS):
        own = transform(local[f], basis_ref[: sector + 2 * ROWS, :])
        for k in range(planes):
            message_ref[f, k * CYCLES : (k + 1) * CYCLES, :] = own[k * group : k * group + CYCLES]
        other = transform(outside[f], basis_ref[ROWS : ROWS + sector, :])
        for s, k in enumerate((0, 1, planes - 2, planes - 1)):
            at = (planes + s) * CYCLES
            message_ref[f, at : at + CYCLES, :] = other[k * group : k * group + CYCLES]

    for k, flux in swirl_rows(rim_ref, lax.rem(az_ref[0], 2) == 0):
        for f in range(FIELDS):
            later_ref[f, 2 * k : 2 * k + 2, :] = flux[f]


def inner_terms(conserved, az, basis, length, after):
    fields, planes, sector, radial = conserved.shape
    message = (fields, (planes + 4) * CYCLES, COEFS)
    later = (fields, 2 * planes, radial)
    full = lambda *shape: pl.BlockSpec(shape, lambda i, *_: (0,) * len(shape))
    tiles = sector // ROWS
    return pl.pallas_call(
        functools.partial(inner_kernel, 2.0 * math.pi / length),
        grid_spec=pltpu.PrefetchScalarGridSpec(
            num_scalar_prefetch=1,
            grid=(1,),
            in_specs=[
                full(*conserved.shape),
                pl.BlockSpec(
                    (fields, planes, ROWS, radial),
                    lambda i, az: (0, 0, (tiles - 1) * lax.rem(az[0], 2), 0),
                ),
                full(*basis.shape),
                pl.BlockSpec(memory_space=pl.ANY),
            ],
            out_specs=[full(*message), full(*later)],
            scratch_shapes=[
                pltpu.VMEM((fields, sector + 2 * ROWS, radial), jnp.float32),
                pltpu.VMEM((fields, sector + 4 * ROWS, radial), jnp.float32),
                pltpu.VMEM((fields, sector, radial), jnp.float32),
            ],
        ),
        out_shape=[
            jax.ShapeDtypeStruct(message, jnp.float32),
            jax.ShapeDtypeStruct(later, jnp.float32),
        ],
        compiler_params=params(),
        cost_estimate=cost(60 * sector * radial * COEFS, 4 * fields * planes * sector * radial),
        name="inner_terms",
    )(az, conserved, conserved, basis, after)


def panel_kernel(n_ax, n_az, cells_ref, count_ref, row_ref, q_ref, bins_ref, amp_ref, _, out_ref, held):
    slots = row_ref.shape[1]
    radial = q_ref.shape[2]
    observers = bins_ref.shape[0]
    count = count_ref[0]
    width = 8

    def fetch(i, _):
        for k in range(width):
            s = i * width + k
            at = cells_ref[s] // radial
            held[:, pl.ds(s, 1), :] = q_ref[:, pl.ds(at, 1), :]
        return 0

    lax.fori_loop(0, (count + width - 1) // width, fetch, 0)
    q = [held[f] for f in range(FIELDS)]
    p = gas_factor * (q[4] - 0.5 * (q[1] * q[1] + q[2] * q[2] + q[3] * q[3]) / q[0])
    turned = jnp.transpose(p)
    which = lax.broadcasted_iota(jnp.int32, (radial, slots), 0)
    here = which == (row_ref[...] & (radial - 1))
    sampled = jnp.sum(jnp.where(here, turned, 0.0), axis=0, keepdims=True) - ref_pressure
    slot = lax.broadcasted_iota(jnp.int32, (1, slots), 1)
    sampled = jnp.where(slot < count, sampled, 0.0)

    contrib = sampled * amp_ref[...]
    first = contrib.astype(jnp.bfloat16).astype(jnp.float32)
    second = contrib - first
    bins = bins_ref[...]
    low = bins & (LOW_BINS - 1)
    high = bins // LOW_BINS
    if n_ax * n_az * LOW_BINS == BINS:
        high = (high % n_az) * n_ax + high // n_az
    each = 128 // LOW_BINS
    high_count = BINS // LOW_BINS
    low_iota = lax.broadcasted_iota(jnp.int32, (LOW_BINS, slots), 0)
    high_iota = lax.broadcasted_iota(jnp.int32, (high_count, slots), 0)
    lane = lax.broadcasted_iota(jnp.int32, (high_count, 128), 1)
    for g in range(observers // each):
        left, right = [], []
        for k in range(each):
            o = g * each + k
            hit = high_iota == high[o : o + 1]
            left.append(jnp.where(hit, first[o : o + 1], 0.0).astype(jnp.bfloat16))
            left.append(jnp.where(hit, second[o : o + 1], 0.0).astype(jnp.bfloat16))
            same = low_iota == low[o : o + 1]
            right.append(jnp.where(same, 1.0, 0.0).astype(jnp.bfloat16))
        sums = lax.dot_general(
            jnp.concatenate(left, axis=0),
            jnp.concatenate(right, axis=0),
            (((1,), (1,)), ((), ())),
            preferred_element_type=jnp.float32,
        )
        total = jnp.zeros((high_count, 128), jnp.float32)
        for k in range(each):
            at = 2 * k * high_count
            both = sums[at : at + high_count] + sums[at + high_count : at + 2 * high_count]
            total = jnp.where(lane // LOW_BINS == k, both, total)
        out_ref[:, g, :] = total


def panel_sums(conserved, cells, counts, bins, amplitudes, after):
    fields, planes, sector, radial = conserved.shape
    slots, observers = bins.shape
    flat = conserved.reshape(fields, planes * sector, radial)
    high_count = BINS // LOW_BINS
    full = lambda *shape: pl.BlockSpec(shape, lambda i, *_: (0,) * len(shape))
    return pl.pallas_call(
        functools.partial(panel_kernel, lax.axis_size("ax"), lax.axis_size("az")),
        grid_spec=pltpu.PrefetchScalarGridSpec(
            num_scalar_prefetch=2,
            grid=(1,),
            in_specs=[
                full(1, slots),
                full(fields, planes * sector, radial),
                full(observers, slots),
                full(observers, slots),
                pl.BlockSpec(memory_space=pl.ANY),
            ],
            out_specs=full(high_count, observers * LOW_BINS // 128, 128),
            scratch_shapes=[pltpu.VMEM((fields, slots, radial), jnp.float32)],
        ),
        out_shape=jax.ShapeDtypeStruct(
            (high_count, observers * LOW_BINS // 128, 128), jnp.float32
        ),
        compiler_params=params(),
        cost_estimate=cost(8 * observers * slots * BINS, 4 * fields * planes * sector * radial),
        name="panel_sums",
    )(cells, counts, cells.reshape(1, slots), flat, bins.T, amplitudes.T, after)


def section_kernel(dtheta, *refs):
    az_ref, q_ref, mine_ref, theirs_ref, early_ref, late_ref, basis_ref = refs[:7]
    out_ref, axial, swirl, local, spec, smooth = refs[7:]
    fields, _, sector, radial = q_ref.shape
    step = pl.program_id(0)
    planes = pl.num_programs(0) - 2
    scale = time_step / 12.0
    chunk = min(sector, 32 * ROWS)
    lane = lax.broadcasted_iota(jnp.int32, (1, radial), 1)
    radius = lane.astype(jnp.float32) + 0.5
    inverse = 1.0 / radius
    near = 8.0 * scale * inverse
    far = scale * inverse
    near_up = jnp.where(lane < radial - 1, near, 0.0)
    near_down = jnp.where(lane >= 1, near, 0.0)
    far_up = jnp.where(lane < radial - 2, far, 0.0)
    far_down = jnp.where(lane >= 2, far, 0.0)
    source = time_step * inverse
    odd = lax.rem(az_ref[0], 2) == 1
    static_planes = axial.shape[0] - 4

    @pl.when(step == 0)
    def _():
        axial[0:2] = jnp.zeros((2,) + axial.shape[1:], jnp.float32)
        axial[planes + 2 : planes + 4] = jnp.zeros((2,) + axial.shape[1:], jnp.float32)
        spec[...] = jnp.zeros_like(spec)
        for k in range(static_planes):
            for f in range(FIELDS):
                rows = slice(k * CYCLES, (k + 1) * CYCLES)
                value = mine_ref[f, rows, :] + theirs_ref[f, rows, :]
                spec[k, f * CYCLES : (f + 1) * CYCLES, :] = value * basis_ref[sector + 2 * ROWS :, :]

    @pl.when(step < planes)
    def _():
        slot = lax.rem(step, 3)
        for f in range(FIELDS):
            early = early_ref[f, pl.ds(2 * step, 2), :]
            late = late_ref[f, pl.ds(2 * step, 2), :]
            swirl[slot, f, ROWS - 2 : ROWS, :] = jnp.where(odd, early, late)
            swirl[slot, f, ROWS + sector : ROWS + sector + 2, :] = jnp.where(odd, late, early)

        def body(i, _):
            start = pl.multiple_of(i * chunk, chunk)
            rows = pl.ds(start, chunk)
            q = [q_ref[f, 0, rows, :] for f in range(FIELDS)]
            u, v, w, p = primitives(q)
            along = carried(q, p, u, 1)
            around = carried(q, p, w, 3)
            outward = carried(q, p, v, 2)
            for f in range(FIELDS):
                axial[step + 2, f, rows, :] = along[f]
                swirl[slot, f, pl.ds(start + ROWS, chunk), :] = around[f]
                g = outward[f] * radius
                value = q[f] - near_up * pltpu.roll(g, radial - 1, 1)
                value = value + near_down * pltpu.roll(g, 1, 1)
                value = value + far_up * pltpu.roll(g, radial - 2, 1)
                value = value - far_down * pltpu.roll(g, 2, 1)
                if f == 2:
                    value = value + source * (p + q[3] * w)
                if f == 3:
                    value = value - source * (q[2] * w)
                local[slot, f, rows, :] = value
            return 0

        lax.fori_loop(0, sector // chunk, body, 0)

    @pl.when(step >= 2)
    def _():
        plane = step - 2
        slot = lax.rem(plane, 3)
        turn = scale * inverse / dtheta
        smooth[...] = lax.dot_general(
            basis_ref[ROWS : ROWS + sector, :], spec[plane], (((1,), (1,)), ((), ())),
            precision=HIGHEST, preferred_element_type=jnp.float32,
        )

        def body(i, _):
            start = pl.multiple_of(i * chunk, chunk)
            rows = pl.ds(start, chunk)
            for f in range(FIELDS):
                at = lambda k: swirl[slot, f, pl.ds(start + (ROWS + k), chunk), :]
                of = lambda k: axial[plane + 2 + k, f, rows, :]
                around = 8.0 * (at(1) - at(-1)) - (at(2) - at(-2))
                along = 8.0 * (of(1) - of(-1)) - (of(2) - of(-2))
                value = local[slot, f, rows, :] - turn * around - scale * along
                moved = smooth[rows, :]
                if f > 0:
                    moved = pltpu.roll(moved, radial - CYCLES * f, 1)
                out_ref[f, 0, rows, :] = jnp.where(lane < CYCLES, moved, value)
            return 0

        lax.fori_loop(0, sector // chunk, body, 0)


def local_section(conserved, az, mine, theirs, early, late, basis, length):
    fields, planes, sector, radial = conserved.shape
    two_back = lambda i: jnp.maximum(i - 2, 0)
    ring = (fields, 2 * planes, radial)
    last = late.shape[1] // ring[1] - 1
    full = lambda a: pl.BlockSpec(a.shape, lambda i, *_: (0,) * a.ndim)
    plane = (fields, 1, sector, radial)
    return pl.pallas_call(
        functools.partial(section_kernel, 2.0 * math.pi / length),
        grid_spec=pltpu.PrefetchScalarGridSpec(
            num_scalar_prefetch=1,
            grid=(planes + 2,),
            in_specs=[
                pl.BlockSpec(plane, lambda i, *_: (0, jnp.minimum(i, planes - 1), 0, 0)),
                full(mine),
                full(theirs),
                full(early),
                pl.BlockSpec(ring, lambda i, *_: (0, last, 0)),
                full(basis),
            ],
            out_specs=pl.BlockSpec(plane, lambda i, *_: (0, two_back(i), 0, 0)),
            scratch_shapes=[
                pltpu.VMEM((planes + 4, fields, sector, radial), jnp.float32),
                pltpu.VMEM((3, fields, sector + 2 * ROWS, radial), jnp.float32),
                pltpu.VMEM((3, fields, sector, radial), jnp.float32),
                pltpu.VMEM((planes, radial, COEFS), jnp.float32),
                pltpu.VMEM((sector, radial), jnp.float32),
            ],
        ),
        out_shape=jax.ShapeDtypeStruct(conserved.shape, jnp.float32),
        compiler_params=params(),
        cost_estimate=cost(
            600 * planes * sector * radial, 10 * 4 * fields * planes * sector * radial
        ),
        name="local_section",
    )(az, conserved, mine, theirs, early, late, basis)


def add_kernel(part_ref, low_ref, high_ref, spec_low, spec_high, basis_ref, sums_ref, *outs):
    out_ref, signal_ref, padded, turned = outs
    step = pl.program_id(0)
    fields, _, sector, radial = part_ref.shape
    groups = radial // CYCLES - 1
    tail = sector // (groups + 1)
    main = groups * tail
    lane = lax.broadcasted_iota(jnp.int32, (1, radial), 1)
    wide = lane >= CYCLES

    @pl.when(step == 0)
    def _():
        padded[...] = jnp.zeros_like(padded)
        observers, _ = turned.shape
        bins = signal_ref.shape[0]
        total = jnp.sum(sums_ref[...], axis=0)
        for o in range(observers):
            row, at = o * bins // 128, o * bins % 128
            piece = total[row : row + 1]
            turned[o : o + 1, :] = pltpu.roll(piece, 128 - at, 1) if at else piece
        signal_ref[...] = jnp.transpose(turned[...])[:bins]

    weight = basis_ref[sector + 2 * ROWS :, :]

    def go(ref, spec_ref):
        for slot in range(2):
            for f in range(fields):
                rows = slice(slot * CYCLES, (slot + 1) * CYCLES)
                at = (slot * fields + f) * CYCLES
                padded[at : at + CYCLES, :] = spec_ref[f, rows, :] * weight
        smooth = lax.dot_general(
            basis_ref[ROWS : ROWS + sector, :], padded[...], (((1,), (1,)), ((), ())),
            precision=HIGHEST, preferred_element_type=jnp.float32,
        )
        for slot in range(2):
            for f in range(fields):
                k = slot * fields + f
                inner = smooth if k == 0 else pltpu.roll(smooth, radial - CYCLES * k, 1)
                out_ref[f, slot, :main, :] = part_ref[f, slot, :main, :] + jnp.where(
                    wide, ref[f, slot], inner[:main]
                )
                rest = inner[main:]
                for g in range(groups):
                    moved = pltpu.roll(ref[f, slot, g * tail : (g + 1) * tail, :], CYCLES * (g + 1), 1)
                    rest = jnp.where(lane // CYCLES == g + 1, moved, rest)
                out_ref[f, slot, main:, :] = part_ref[f, slot, main:, :] + rest

    pl.when(step == 0)(lambda: go(low_ref, spec_low))
    pl.when(step == 1)(lambda: go(high_ref, spec_high))


def add_edges(section, low, high, spec_low, spec_high, basis, sums, observers):
    fields, planes, sector, radial = section.shape
    bins = sums.shape[1] * sums.shape[2] // observers
    full = lambda a: pl.BlockSpec(a.shape, lambda i, *_: (0,) * a.ndim)
    plane = pl.BlockSpec(
        (fields, 2, sector, radial), lambda i, *_: (0, (planes // 2 - 1) * i, 0, 0)
    )
    return pl.pallas_call(
        add_kernel,
        grid_spec=pltpu.PrefetchScalarGridSpec(
            num_scalar_prefetch=0,
            grid=(2,),
            in_specs=[
                plane,
                pl.BlockSpec(memory_space=pltpu.VMEM),
                pl.BlockSpec(memory_space=pltpu.VMEM),
                full(spec_low),
                full(spec_high),
                full(basis),
                full(sums),
            ],
            out_specs=[plane, pl.BlockSpec((bins, observers), lambda i, *_: (0, 0))],
            scratch_shapes=[
                pltpu.VMEM((radial, COEFS), jnp.float32),
                pltpu.VMEM((observers, 128), jnp.float32),
            ],
        ),
        out_shape=[
            jax.ShapeDtypeStruct(section.shape, jnp.float32),
            jax.ShapeDtypeStruct((bins, observers), jnp.float32),
        ],
        input_output_aliases={0: 0},
        compiler_params=params(),
        cost_estimate=cost(8 * fields * sector * radial, 4 * 12 * fields * sector * radial),
        name="add_edges",
    )(section, low, high, spec_low, spec_high, basis, sums)


def exchanged_sums(partial, observers):
    n_ax, n_az = lax.axis_size("ax"), lax.axis_size("az")
    mine = BINS // (n_ax * n_az)
    if mine != LOW_BINS:
        partial = partial.reshape(-1, observers, LOW_BINS).transpose(0, 2, 1)
        partial = partial.reshape(n_ax, n_az, mine, observers).transpose(1, 0, 3, 2)
    blocks = partial.reshape(n_az, n_ax, observers * mine // 128, 128)
    blocks = lax.all_to_all(blocks, "az", split_axis=0, concat_axis=0, tiled=True).sum(axis=0)
    return lax.all_to_all(blocks, "ax", split_axis=0, concat_axis=0, tiled=True)


def on_device(conserved, panel_cells, panel_counts, time_bins, amplitudes):
    fields, planes, sector, radial = conserved.shape
    observers = time_bins.shape[1]
    n_ax, n_az = lax.axis_size("ax"), lax.axis_size("az")
    length = sector * n_az
    up = [(i, i + 1) for i in range(n_ax - 1)]
    down = [(j, i) for i, j in up]
    az = lax.axis_index("az").astype(jnp.int32).reshape(1)
    table = basis_table(length)
    table = jnp.asarray(np.concatenate([table[-ROWS:], table, table[:ROWS]], axis=0))
    basis = lax.dynamic_slice_in_dim(table, az[0] * sector, sector + 2 * ROWS, axis=0)
    basis = jnp.concatenate([basis, jnp.asarray(mode_weights(length))], axis=0)

    pair = [(i, i ^ 1) for i in range(n_az)]
    send_up, send_down, early = edge_terms(conserved, az)
    early = lax.ppermute(early, "az", pair)
    low = lax.ppermute(send_up, "ax", up)
    high = lax.ppermute(send_down, "ax", down)

    message, later = inner_terms(conserved, az, basis, length, early)
    edge = (planes + 4) * CYCLES
    partial = panel_sums(conserved, panel_cells, panel_counts, time_bins, amplitudes, message)
    sums = exchanged_sums(partial, observers)

    mine = jnp.concatenate([message + lax.ppermute(message, "az", pair), later], axis=1)
    pairs = [(i, (i + 1) % n_az) for i in range(1, n_az, 2)]
    theirs = lax.ppermute(mine, "az", pairs + [(j, i) for i, j in pairs])
    late = theirs
    shift = 4
    while shift < n_az:
        mine = mine + theirs
        theirs = lax.ppermute(mine, "az", [(i, (i + shift) % n_az) for i in range(n_az)])
        shift *= 2
    outside = mine[:, planes * CYCLES : edge] + theirs[:, planes * CYCLES : edge]
    spec_low = lax.ppermute(outside[:, : 2 * CYCLES], "ax", up)
    spec_high = lax.ppermute(outside[:, 2 * CYCLES :], "ax", down)

    section = local_section(pltpu.with_memory_space_constraint(conserved, pltpu.HBM), az, mine, theirs, early, late, basis, length)
    section, signal = add_edges(
        section, low, high, spec_low, spec_high, basis, sums, observers
    )
    return (section, signal.T)


def solution(mesh):
    placed = (
        P(None, "ax", "az", None),
        P(("ax", "az")),
        P(("ax", "az")),
        P(("ax", "az"), None),
        P(("ax", "az"), None),
    )
    return jax.shard_map(
        on_device,
        mesh=mesh,
        in_specs=placed,
        out_specs=(P(None, "ax", "az", None), P(None, ("ax", "az"))),
        check_vma=False,
    )
```
